128 devices in a mesh: replica: 16 (over x_hi, z, core), group: 8 (over y, x_lo).
Axes of the slice: x: 4 (x_hi: 2, x_lo: 2; x = x_hi * 2 + x_lo), y: 4, z: 4, core: 2. Of those that a mesh axis runs over, the one named last changes fastest.
Arguments:
- tokens: bfloat16 [16384, 960], P(('replica', 'group')), may hold values from -6 to 6
- cotangent: bfloat16 [16384, 960], P(('replica', 'group')), may hold values from -6 to 6
- lengths: int32 [128, 3], P(('replica', 'group')), may hold values from 1 to 64, 128 in all within a row
- gain_attn: bfloat16 [2, 960], P(None, 'group'), may hold values from 0.5 to 1.5
- w_query: bfloat16 [2, 960, 960], P(None, 'group'), may hold values from -0.1875 to 0.1875
- w_key: bfloat16 [2, 960, 320], P(None, 'group'), may hold values from -0.1875 to 0.1875
- w_value: bfloat16 [2, 960, 320], P(None, 'group'), may hold values from -0.1875 to 0.1875
- w_out: bfloat16 [2, 960, 960], P(None, 'group'), may hold values from -1.5 to 1.5
- gain_mlp: bfloat16 [2, 960], P(None, 'group'), may hold values from 0.5 to 1.5
- w_gate: bfloat16 [2, 960, 2560], P(None, None, 'group'), may hold values from -0.1875 to 0.1875
- w_up: bfloat16 [2, 960, 2560], P(None, None, 'group'), may hold values from -0.1875 to 0.1875
- w_down: bfloat16 [2, 2560, 960], P(None, 'group'), may hold values from -0.125 to 0.125
Outputs:
- activations: bfloat16 [16384, 960], P(('replica', 'group'))
- grad_tokens: float32 [16384, 960], P(('replica', 'group'))
- grad_gain_attn: float32 [2, 960], P(None, 'group')
- grad_w_query: float32 [2, 960, 960], P(None, 'group')
- grad_w_key: float32 [2, 960, 320], P(None, 'group')
- grad_w_value: float32 [2, 960, 320], P(None, 'group')
- grad_w_out: float32 [2, 960, 960], P(None, 'group')
- grad_gain_mlp: float32 [2, 960], P(None, 'group')
- grad_w_gate: float32 [2, 960, 2560], P(None, None, 'group')
- grad_w_up: float32 [2, 960, 2560], P(None, None, 'group')
- grad_w_down: float32 [2, 2560, 960], P(None, 'group')
The draws below stay inside these ranges and needn't reach their ends.
Inputs may be any that keep to these rules, and one draw needn't show every extreme that they name: Each row holds the lengths of 3 sequences that fill one device's 128 tokens in order; one of them is exactly 64 long.
All inputs are finite; a program needn't handle non-finite values.
Results may differ from the reference program's by a relative error of at most 0.03.
Values may be sent and summed in bfloat16 or wider, within the bound.
A program may use at most 192 MiB of HBM per device.

```python
import math
import jax
import jax.numpy as jnp
import numpy as np
from jax import lax

D = 960
FF = 2560
Q_HEADS = 15
KV_HEADS = 5
HEAD = 64
LAYERS = 2
SEQS = 3
ROWS = 128
LONGEST = 64
TOKENS = 16384
N_REPLICA = 16
N_GROUP = 8
DEVICES = 128


def shard_levels(stream_key, extent, pieces, low, high):
    def one(axis_at, shards_of):
        heights = jax.random.uniform(jax.random.fold_in(jax.random.fold_in(stream_key, 6), axis_at), (shards_of,), jnp.float32, low / len(pieces), high / len(pieces))
        return jnp.repeat(jnp.exp(heights), extent[axis_at] // shards_of).reshape((-1,) + (1,) * (len(extent) - axis_at - 1))

    factor_of = one(*pieces[0])
    for cut in pieces[1:]:
        factor_of = factor_of * one(*cut)
    return factor_of


def profile(count, total, reach, slope):
    portions = [(1 << 20) // math.isqrt(grade ** slope) + 1 for grade in range(2, count + 1)]
    surplus, counts = total - reach - (count - 1), [1] * (count - 1)
    while surplus > 0:
        movable = [i for i in range(count - 1) if counts[i] < reach]
        whole, remaining = sum([portions[i] for i in movable]), surplus
        for i in movable:
            extra = min(reach - counts[i], max(1, remaining * portions[i] // whole), surplus)
            counts[i] = counts[i] + extra
            surplus = surplus - extra
    return np.array([reach] + counts)


def ragged(own_key, number_of, total, reach, slope):
    if number_of == 2:
        one = jax.random.randint(own_key, (), max(1, total - reach), min(reach, total - 1) + 1)
        return jnp.stack([one, total - one])
    tallies = jnp.asarray(profile(number_of, total, reach, slope), jnp.int32)
    couples = (number_of - 1) // 2
    source_of, taker = tallies[1:1 + 2 * couples:2], tallies[2:2 + 2 * couples:2]
    slack = jnp.minimum(source_of - 1, reach - taker)
    passed = jax.random.randint(jax.random.fold_in(own_key, 1), (couples,), 0, 1 << 20) % (slack + 1)
    tallies = tallies.at[1:1 + 2 * couples:2].set(source_of - passed).at[2:2 + 2 * couples:2].set(taker + passed)
    return tallies[jax.random.permutation(jax.random.fold_in(own_key, 2), number_of)]


def noise(key, extent, deviation, bound, shards=(), held_as=jnp.bfloat16):
    drawn = jax.random.normal(key, extent, jnp.float32) * deviation
    if len(shards) > 0:
        drawn = shard_levels(key, extent, shards, -0.22, 0.18) * drawn
    return jnp.clip(drawn, min=-bound, max=bound).astype(held_as)


def setup_inputs(seed: int = 0) -> dict:
    streams_of = jax.random.split(jax.random.key(seed), 13)
    return {
        "tokens": noise(streams_of[0], (TOKENS, D), 1.0, 6.0, ((0, 128),)),
        "cotangent": noise(streams_of[1], (TOKENS, D), 1.0, 6.0, ((0, 128),)),
        "lengths": jax.vmap(lambda own: ragged(own, SEQS, ROWS, LONGEST, 1))(jax.random.split(streams_of[2], DEVICES)).reshape((DEVICES, SEQS)).astype(jnp.int32),
        "gain_attn": jnp.clip(1.0 + 0.1 * jax.random.normal(streams_of[3], (LAYERS, D), jnp.float32), 0.5, 1.5).astype(jnp.bfloat16),
        "w_query": noise(streams_of[4], (LAYERS, D, Q_HEADS * HEAD), D ** -0.5, 0.1875, ((1, 8),)),
        "w_key": noise(streams_of[5], (LAYERS, D, KV_HEADS * HEAD), D ** -0.5, 0.1875, ((1, 8),)),
        "w_value": noise(streams_of[6], (LAYERS, D, KV_HEADS * HEAD), D ** -0.5, 0.1875, ((1, 8),)),
        "w_out": noise(streams_of[7], (LAYERS, Q_HEADS * HEAD, D), (max(Q_HEADS * HEAD // 64, 1)) ** -0.5, 1.5, ((1, 8),)),
        "gain_mlp": jnp.clip(1.0 + 0.1 * jax.random.normal(streams_of[8], (LAYERS, D), jnp.float32), 0.5, 1.5).astype(jnp.bfloat16),
        "w_gate": noise(streams_of[9], (LAYERS, D, FF), D ** -0.5, 0.1875, ((2, 8),)),
        "w_up": noise(streams_of[10], (LAYERS, D, FF), D ** -0.5, 0.1875, ((2, 8),)),
        "w_down": noise(streams_of[11], (LAYERS, FF, D), FF ** -0.5, 0.125, ((1, 8),)),
    }


@jax.custom_vjp
def low(v):
    return lax.optimization_barrier(v.astype(jnp.bfloat16)).astype(jnp.float32)

@jax.custom_vjp
def low_back(v):
    return v

def low_keep(v):
    return (low(v), None)

def low_pass(kept, grad):
    return (grad,)

def back_keep(v):
    return (v, None)

def back_low(kept, grad):
    return (low(grad),)
low.defvjp(low_keep, low_pass)
low_back.defvjp(back_keep, back_low)
norm_eps = 1e-05
rope_base = 100000.0
score_scale = 0.125
masked_value = -1e+30
highest = lax.Precision.HIGHEST

def product(left_side, right_side):
    return jnp.dot(left_side, right_side, precision=highest)

def rms_scale(stream, gain_vec):
    return stream * lax.rsqrt(lax.optimization_barrier(jnp.mean(stream * stream, axis=-1, keepdims=True)) + norm_eps) * gain_vec

def rope_tables(positions):
    steps_half = jnp.arange(HEAD // 2, dtype=jnp.float32)
    inverse = rope_base ** (-2.0 * steps_half / HEAD)
    angles = positions[:, None] * inverse[None, :]
    cosine = jnp.cos(angles)
    sine_table = jnp.sin(angles)
    return (jnp.concatenate([cosine, cosine], axis=1), jnp.concatenate([sine_table, sine_table], axis=1))

def rotate(values, cosine, sine_table):
    amount = values.shape[0]
    shaped = values.reshape(amount, -1, HEAD)
    first_half = shaped[..., :HEAD // 2]
    second_half = shaped[..., HEAD // 2:]
    turned = jnp.concatenate([-second_half, first_half], axis=-1)
    return (shaped * cosine[:, None, :] + turned * sine_table[:, None, :]).reshape(values.shape)

def layout(seq_lengths, first_index, amount):
    finish = jnp.cumsum(seq_lengths).astype(jnp.int32)
    indices = (first_index + jnp.arange(amount, dtype=jnp.int32)).astype(jnp.int32)
    documents = lax.optimization_barrier(jnp.sum((indices[:, None] >= finish[None, :]).astype(jnp.int32), axis=1)).astype(jnp.int32)
    starts = (finish - seq_lengths).astype(jnp.int32)
    member = documents[:, None] == jnp.arange(seq_lengths.shape[0], dtype=jnp.int32)[None, :]
    begins = lax.optimization_barrier(jnp.sum(jnp.where(member, starts[None, :], 0), axis=1)).astype(jnp.int32)
    return (documents, (indices - begins).astype(jnp.int32))

def attend(query_rot, key_rot, values, allowed):
    amount = query_rot.shape[0]
    group_share = Q_HEADS // KV_HEADS
    queries = query_rot.reshape(amount, KV_HEADS, group_share, HEAD).transpose(1, 2, 0, 3)
    keyed = key_rot.reshape(amount, KV_HEADS, HEAD).transpose(1, 0, 2)
    valued = values.reshape(amount, KV_HEADS, HEAD).transpose(1, 0, 2)

    def one_head(head_parts):
        query_head, key_head, value_head = head_parts
        raw_scores = jnp.einsum('gsd,td->gst', query_head, key_head, precision=highest)
        scores = jnp.where(allowed[None], low_back(raw_scores * score_scale), masked_value)
        row_max = lax.optimization_barrier(jnp.max(scores, axis=-1, keepdims=True))
        weights = jnp.exp(scores - row_max)
        weights_soft = weights / lax.optimization_barrier(jnp.sum(weights, axis=-1, keepdims=True))
        return jnp.einsum('gst,td->gsd', low(weights_soft), value_head, precision=highest)
    mixed_heads = lax.map(jax.checkpoint(one_head), (queries, keyed, valued))
    return mixed_heads.transpose(2, 0, 1, 3).reshape(amount, Q_HEADS * HEAD)

def layer(stream, weight_set, cosine, sine_table, allowed):
    gain_one, query_w, key_w, value_w, out_w, gain_two, gate_w, up_w, down_w = weight_set
    normed = low(rms_scale(stream, gain_one))
    query_proj = low_back(product(normed, query_w))
    key_proj = low_back(product(normed, key_w))
    values = low_back(low(product(normed, value_w)))
    query_rot = low(rotate(query_proj, cosine, sine_table))
    key_rot = low(rotate(key_proj, cosine, sine_table))
    mixed_low = low_back(low(attend(query_rot, key_rot, values, allowed)))
    hidden = stream + low_back(product(mixed_low, out_w))
    normed_two = low(rms_scale(hidden, gain_two))
    gate_pre = low_back(product(normed_two, gate_w))
    up_pre = low_back(product(normed_two, up_w))
    active = low(gate_pre * jax.nn.sigmoid(gate_pre) * up_pre)
    return hidden + low_back(product(active, down_w))

def reference(tokens, cotangent, lengths, gain_attn, w_query, w_key, w_value, w_out, gain_mlp, w_gate, w_up, w_down):
    params = (gain_attn.astype(jnp.float32), w_query.astype(jnp.float32), w_key.astype(jnp.float32), w_value.astype(jnp.float32), w_out.astype(jnp.float32), gain_mlp.astype(jnp.float32), w_gate.astype(jnp.float32), w_up.astype(jnp.float32), w_down.astype(jnp.float32))
    block_count = N_REPLICA * N_GROUP
    stream_blocks = tokens.astype(jnp.float32).reshape(block_count, ROWS, D)
    grad_blocks = cotangent.astype(jnp.float32).reshape(block_count, ROWS, D)

    def one_block(totals, block_parts):
        block_in, block_grad, seq_lengths = block_parts
        documents, positions = layout(seq_lengths, 0, ROWS)
        cosine, sine_table = rope_tables(positions.astype(jnp.float32))
        indices = jnp.arange(ROWS, dtype=jnp.int32)
        allowed = (documents[:, None] == documents[None, :]) & (indices[None, :] <= indices[:, None])

        def forward(stream, weights):
            for layer_index in range(LAYERS):
                weight_set = tuple((weight_arr[layer_index] for weight_arr in weights))
                stream = layer(stream, weight_set, cosine, sine_table, allowed)
            return stream
        result, pullback = jax.vjp(forward, block_in, params)
        grad_in, grad_params = pullback(block_grad)
        totals = jax.tree.map(jnp.add, totals, grad_params)
        return (totals, (result, grad_in))
    zero_grads = tuple((jnp.zeros(weight_arr.shape, jnp.float32) for weight_arr in params))
    grads_all, (results, grad_ins) = lax.scan(one_block, zero_grads, (stream_blocks, grad_blocks, lengths))
    return (results.reshape(TOKENS, D).astype(jnp.bfloat16), grad_ins.reshape(TOKENS, D), grads_all[0], grads_all[1], grads_all[2], grads_all[3], grads_all[4], grads_all[5], grads_all[6], grads_all[7], grads_all[8])
```

```python
import functools

import jax
import jax.numpy as jnp
from jax import lax
from jax.experimental import pallas as pl
from jax.experimental.pallas import tpu as pltpu
from jax.sharding import PartitionSpec as P

Q_HEADS = 15
KV_HEADS = 5
HEAD = 64
LAYERS = 2
D = 960
SHARD = 120
PAD = 128
QKV = 1600
FFS = 320

norm_eps = 1e-05
rope_base = 100000.0
score_scale = 0.125
masked_value = -1e30
MESH = pl.DeviceIdType.MESH
BF = jnp.bfloat16
F32 = jnp.float32


def coords():
    r = lax.axis_index("replica")
    g = lax.axis_index("group")
    return r // 8, (r // 2) % 4, r % 2, g // 2, g % 2


def device(x_hi, z, core, y, x_lo):
    return ((x_hi * 4 + z) * 2 + core, y * 2 + x_lo)


def remote(src, dst, sems, index, target):
    return pltpu.make_async_remote_copy(
        src_ref=src,
        dst_ref=dst,
        send_sem=sems[0].at[index],
        recv_sem=sems[1].at[index],
        device_id=target,
        device_id_type=MESH,
    )


def greet(targets):
    barrier = pltpu.get_barrier_semaphore()
    for target in targets:
        pl.semaphore_signal(barrier, inc=1, device_id=target, device_id_type=MESH)
    pl.semaphore_wait(barrier, len(targets))


ANY = pl.BlockSpec(memory_space=pl.ANY)
VMEM = pl.BlockSpec(memory_space=pltpu.VMEM)


def gather_kernel(aq, ao, mg, md, fq, fo, fg, fd, send, recv, local):
    x_hi, z, core, y, x_lo = coords()
    sems = (send, recv)
    sibling = device(x_hi, z, 1 - core, y, x_lo)
    near = [device(x_hi, z, core, y, 1 - x_lo), device(1 - x_hi, z, core, y, 1 - x_lo)]
    ring = [None] + [device(x_hi, z, core, (y + k) % 4, x_lo) for k in (1, 2, 3)]
    greet(ring[1:] + near + [sibling])
    home = core == x_lo
    slot = [0]

    def index():
        slot[0] += 1
        return slot[0] - 1

    own_pairs = [(aq, fq), (ao, fo)]
    started = []

    first = []
    for l in range(LAYERS):
        for src, dst in own_pairs:
            first.append(remote(src.at[l], dst.at[l, y, core], sems, index(), near[l]))
    half_g, half_d = D // 2, FFS // 2
    rows_g = pl.ds(pl.multiple_of(core * half_g, 16), half_g)
    rows_d = pl.ds(pl.multiple_of(core * half_d, 16), half_d)
    other_g = pl.ds(pl.multiple_of((1 - core) * half_g, 16), half_g)
    other_d = pl.ds(pl.multiple_of((1 - core) * half_d, 16), half_d)
    swaps = []
    for l in range(LAYERS):
        swaps.append(
            [
                remote(mg.at[l, rows_g], fg.at[l, x_lo, rows_g], sems, index(), near[l]),
                remote(md.at[l, rows_d], fd.at[l, x_lo, rows_d], sems, index(), near[l]),
            ]
        )
    keeps = []
    for l in range(LAYERS):
        for k, (src, dst) in enumerate(own_pairs):
            keeps.append(pltpu.make_async_copy(src.at[l], dst.at[l, y, core], local.at[l * 4 + k]))
    keeps_m = []
    for l in range(LAYERS):
        for k, (src, dst) in enumerate([(mg, fg), (md, fd)]):
            keeps_m.append(pltpu.make_async_copy(src.at[l], dst.at[l, x_lo], local.at[l * 4 + 2 + k]))

    @pl.when(home)
    def _():
        for copy in first:
            copy.start()
        for copy in keeps:
            copy.start()

    for swap in swaps:
        for copy in swap:
            copy.start()
    for copy in keeps_m:
        copy.start()

    ring_copies = {}
    for l in range(LAYERS):

        @pl.when(home)
        def _():
            for copy in keeps[2 * l : 2 * l + 2]:
                copy.wait()

        @pl.when(jnp.logical_not(home))
        def _():
            for copy in first[2 * l : 2 * l + 2]:
                copy.wait_recv()

        for k in (1, 3, 2):
            for f in (fq, fo):
                copy = remote(f.at[l, y, core], f.at[l, y, core], sems, index(), ring[k])
                copy.start()
                ring_copies[l, k, f is fq] = copy
        for f in (fq, fo):
            copy = remote(f.at[l, y, core], f.at[l, y, core], sems, index(), sibling)
            copy.start()
            started.append(copy)
    for l in range(LAYERS):
        for k in (1, 3, 2):
            for f in (fq, fo):
                came = (y - k) % 4
                ring_copies[l, k, f is fq].wait_recv()
                copy = remote(f.at[l, came, core], f.at[l, came, core], sems, index(), sibling)
                copy.start()
                started.append(copy)
    for l in range(LAYERS):
        for copy, f, rows in zip(swaps[l], (fg, fd), (rows_g, rows_d)):
            copy.wait_recv()
            passed = remote(
                f.at[l, 1 - x_lo, rows], f.at[l, 1 - x_lo, rows], sems, index(), sibling
            )
            passed.start()
            started.append(passed)

    @pl.when(home)
    def _():
        for copy in first:
            copy.wait_send()

    for swap in swaps:
        for copy in swap:
            copy.wait_send()
    for copy in keeps_m:
        copy.wait()
    for copy in ring_copies.values():
        copy.wait_send()
    for copy in started:
        copy.wait()


def gather(aq, ao, mg, md):
    count = 40
    return pl.pallas_call(
        gather_kernel,
        out_shape=(
            jax.ShapeDtypeStruct((LAYERS, 4, 2, PAD, QKV), BF),
            jax.ShapeDtypeStruct((LAYERS, 4, 2, PAD, D), BF),
            jax.ShapeDtypeStruct((LAYERS, 2, D, 2 * FFS), BF),
            jax.ShapeDtypeStruct((LAYERS, 2, FFS, D), BF),
        ),
        in_specs=[ANY] * 4,
        out_specs=[ANY] * 4,
        scratch_shapes=[
            pltpu.SemaphoreType.DMA((count,)),
            pltpu.SemaphoreType.DMA((count,)),
            pltpu.SemaphoreType.DMA((8,)),
        ],
        compiler_params=pltpu.CompilerParams(collective_id=1, has_side_effects=True),
    )(aq, ao, mg, md)


def spread_kernel(x, out, send, recv):
    x_hi, z, core, y, x_lo = coords()
    targets = [device(x_hi, z, core, (y + k) % 4, x_lo) for k in (1, 3, 2)]
    greet(targets)
    copies = [
        remote(x, out.at[y], (send, recv), k, target) for k, target in enumerate(targets)
    ]
    for copy in copies:
        copy.start()
    out[y] = x[...]
    for copy in copies:
        copy.wait()


def spread(x):
    return pl.pallas_call(
        spread_kernel,
        out_shape=jax.ShapeDtypeStruct((4,) + x.shape, x.dtype),
        in_specs=[VMEM],
        out_specs=VMEM,
        scratch_shapes=[pltpu.SemaphoreType.DMA((3,)), pltpu.SemaphoreType.DMA((3,))],
        compiler_params=pltpu.CompilerParams(collective_id=2, has_side_effects=True),
    )(x)


def collect_kernel(x, base, out, came, send, recv):
    x_hi, z, core, y, x_lo = coords()
    targets = [device(x_hi, z, core, (y + k) % 4, x_lo) for k in (1, 3, 2)]
    greet(targets)
    copies = [
        remote(x.at[(y + k) % 4], came.at[i], (send, recv), i, targets[i])
        for i, k in enumerate((1, 3, 2))
    ]
    for copy in copies:
        copy.start()
    total = base[...] + x[y].astype(F32)
    for i, copy in enumerate(copies):
        copy.wait()
        total = total + came[i].astype(F32)
    out[...] = total


def collect(x, base):
    return pl.pallas_call(
        collect_kernel,
        out_shape=jax.ShapeDtypeStruct(base.shape, F32),
        in_specs=[VMEM, VMEM],
        out_specs=VMEM,
        scratch_shapes=[
            pltpu.VMEM((3,) + base.shape, BF),
            pltpu.SemaphoreType.DMA((3,)),
            pltpu.SemaphoreType.DMA((3,)),
        ],
        compiler_params=pltpu.CompilerParams(collective_id=3, has_side_effects=True),
    )(x, base)


def add_into(dst, others, step=16):
    rows = dst.shape[0]

    def body(i, carry):
        at = pl.ds(pl.multiple_of(i * step, step), step)
        total = dst[at, :].astype(F32)
        for other in others:
            total = total + other[at, :].astype(F32)
        dst[at, :] = total.astype(dst.dtype)
        return carry

    lax.fori_loop(0, rows // step, body, 0)


def add_to(dst, terms, step=16):
    rows = dst.shape[0]

    def body(i, carry):
        at = pl.ds(pl.multiple_of(i * step, step), step)
        total = terms[0][at, :].astype(F32)
        for other in terms[1:]:
            total = total + other[at, :].astype(F32)
        dst[at, :] = total.astype(dst.dtype)
        return carry

    lax.fori_loop(0, rows // step, body, 0)


def reduce_kernel(
    gq, go, gg, gd,
    fq, fo, fg, fd,
    sq, so, sg, sd,
    xq, xo, xg, xd,
    yq, yo,
    lq, lo,
    zq, zo, zg, zd,
    pq, po, pg, pd,
    hq, ho, hg, hd,
    send, recv,
):
    x_hi, z, core, y, x_lo = coords()
    sems = (send, recv)
    sibling = device(x_hi, z, 1 - core, y, x_lo)
    near = [device(x_hi, z, core, y, 1 - x_lo), device(1 - x_hi, z, core, y, 1 - x_lo)]
    far = device(1 - x_hi, z, core, y, x_lo)
    ring_y = {k: device(x_hi, z, core, (y + k) % 4, x_lo) for k in (1, 2, 3)}
    ring_z = {k: device(x_hi, (z + k) % 4, core, y, x_lo) for k in (1, 2, 3)}
    greet(list(ring_y.values()) + list(ring_z.values()) + near + [far, sibling])
    home = core == x_lo
    slot = [0]

    def index():
        slot[0] += 1
        return slot[0] - 1

    layers = (1, 0)
    pair = {}
    for l in layers:
        pair[l] = [
            remote(gg.at[l, 1 - core], sg.at[l], sems, index(), sibling),
            remote(gd.at[l, 1 - core], sd.at[l], sems, index(), sibling),
            remote(gq.at[l, :, 1 - core], sq.at[l], sems, index(), sibling),
            remote(go.at[l, :, 1 - core], so.at[l], sems, index(), sibling),
        ]
        for copy in pair[l]:
            copy.start()
    over_x = {}
    for l in layers:
        over_x[l] = [
            remote(src.at[l], dst.at[l], sems, index(), near[l])
            for src, dst in ((sg, xg), (sd, xd), (sq, xq), (so, xo))
        ]
    for l in layers:
        for k, (own, total) in enumerate(((gg, sg), (gd, sd), (gq, sq), (go, so))):
            pair[l][k].wait_recv()
            if k < 2:
                add_into(total.at[l], [own.at[l, core]])
            else:
                for q in range(4):
                    add_into(total.at[l, q], [own.at[l, q, core]])

            @pl.when(jnp.logical_not(home))
            def _():
                over_x[l][k].start()

    over_y = {}
    over_z = {}
    out_z = {}
    over_h = {}
    for l in layers:
        for k in (1, 3, 2):
            over_y[l, k] = [
                remote(sq.at[l, (y + k) % 4], yq.at[l, k - 1], sems, index(), ring_y[k]),
                remote(so.at[l, (y + k) % 4], yo.at[l, k - 1], sems, index(), ring_y[k]),
            ]

    def part(rows, where):
        return pl.ds(pl.multiple_of(where * (rows // 4), 16), rows // 4)

    pieces = ((sg, zg, pg, hg, fg, D), (sd, zd, pd, hd, fd, FFS), (lq, zq, pq, hq, fq, PAD), (lo, zo, po, ho, fo, PAD))
    for l in layers:
        for m, (src, zb, pb, hb, fb, rows) in enumerate(pieces):
            for k in (1, 3, 2):
                over_z[l, m, k] = remote(
                    src.at[l, part(rows, (z + k) % 4)], zb.at[l, k - 1], sems, index(), ring_z[k]
                )
            over_h[l, m] = remote(pb.at[l], hb.at[l], sems, index(), far)
            for k in (1, 3, 2):
                out_z[l, m, k] = remote(
                    fb.at[l, part(rows, z)], fb.at[l, part(rows, z)], sems, index(), ring_z[k]
                )
    last = {
        (l, m): remote(piece[4].at[l], piece[4].at[l], sems, index(), sibling)
        for l in layers
        for m, piece in enumerate(pieces)
    }

    @pl.when(home)
    def _():
        for l in layers:
            over_x[l][0].wait_recv()
            add_into(sg.at[l], [xg.at[l]])
            over_x[l][1].wait_recv()
            add_into(sd.at[l], [xd.at[l]])
            for m in (0, 1):
                for k in (1, 3, 2):
                    over_z[l, m, k].start()
            over_x[l][2].wait_recv()
            over_x[l][3].wait_recv()
            for k in (1, 3, 2, 0):
                for total, came in ((sq, xq), (so, xo)):
                    add_into(total.at[l, (y + k) % 4], [came.at[l, (y + k) % 4]])
                if k:
                    for copy in over_y[l, k]:
                        copy.start()
        for l in layers:
            for k in (1, 3, 2):
                for copy in over_y[l, k]:
                    copy.wait_recv()
            add_to(lq.at[l], [sq.at[l, y]] + [yq.at[l, j] for j in range(3)])
            add_to(lo.at[l], [so.at[l, y]] + [yo.at[l, j] for j in range(3)])
            for m in (2, 3):
                for k in (1, 3, 2):
                    over_z[l, m, k].start()
        for l in layers:
            for m, (src, zb, pb, hb, fb, rows) in enumerate(pieces):
                for k in (1, 3, 2):
                    over_z[l, m, k].wait_recv()
                add_to(pb.at[l], [src.at[l, part(rows, z)]] + [zb.at[l, j] for j in range(3)])
                over_h[l, m].start()
        for l in layers:
            for m, (src, zb, pb, hb, fb, rows) in enumerate(pieces):
                over_h[l, m].wait_recv()
                add_to(fb.at[l, part(rows, z)], [pb.at[l], hb.at[l]])
                for k in (1, 3, 2):
                    out_z[l, m, k].start()
        for l in layers:
            for m in range(4):
                for k in (1, 3, 2):
                    out_z[l, m, k].wait_recv()
                last[l, m].start()
        for l in layers:
            for m in range(4):
                last[l, m].wait_send()
                over_h[l, m].wait_send()
                for k in (1, 3, 2):
                    over_z[l, m, k].wait_send()
                    out_z[l, m, k].wait_send()
            for k in (1, 3, 2):
                for copy in over_y[l, k]:
                    copy.wait_send()

    @pl.when(jnp.logical_not(home))
    def _():
        for l in layers:
            for copy in over_x[l]:
                copy.wait_send()
        for copy in last.values():
            copy.wait_recv()

    for l in layers:
        for copy in pair[l]:
            copy.wait_send()


def reduce(gq, go, gg, gd):
    count = 144
    L = LAYERS

    def buf(*shape):
        return pltpu.VMEM(shape, BF)

    return pl.pallas_call(
        reduce_kernel,
        out_shape=(
            jax.ShapeDtypeStruct((L, PAD, QKV), BF),
            jax.ShapeDtypeStruct((L, PAD, D), BF),
            jax.ShapeDtypeStruct((L, D, 2 * FFS), BF),
            jax.ShapeDtypeStruct((L, FFS, D), BF),
        ),
        in_specs=[VMEM] * 4,
        out_specs=[VMEM] * 4,
        scratch_shapes=[
            buf(L, 4, PAD, QKV), buf(L, 4, PAD, D), buf(L, D, 2 * FFS), buf(L, FFS, D),
            buf(L, 4, PAD, QKV), buf(L, 4, PAD, D), buf(L, D, 2 * FFS), buf(L, FFS, D),
            buf(L, 3, PAD, QKV), buf(L, 3, PAD, D),
            buf(L, PAD, QKV), buf(L, PAD, D),
            buf(L, 3, PAD // 4, QKV), buf(L, 3, PAD // 4, D), buf(L, 3, D // 4, 2 * FFS), buf(L, 3, FFS // 4, D),
            buf(L, PAD // 4, QKV), buf(L, PAD // 4, D), buf(L, D // 4, 2 * FFS), buf(L, FFS // 4, D),
            buf(L, PAD // 4, QKV), buf(L, PAD // 4, D), buf(L, D // 4, 2 * FFS), buf(L, FFS // 4, D),
            pltpu.SemaphoreType.DMA((count,)),
            pltpu.SemaphoreType.DMA((count,)),
        ],
        compiler_params=pltpu.CompilerParams(
            collective_id=4, has_side_effects=True, vmem_limit_bytes=62 * 2**20
        ),
    )(gq, go, gg, gd)


def rms_scale(stream, gain_vec):
    return (
        stream * lax.rsqrt(jnp.mean(stream * stream, axis=-1, keepdims=True) + norm_eps) * gain_vec
    )


def rope_tables(positions):
    steps_half = jnp.arange(HEAD // 2, dtype=jnp.float32)
    inverse = rope_base ** (-2.0 * steps_half / HEAD)
    angles = positions[:, None] * inverse[None, :]
    cosine = jnp.cos(angles)
    sine_table = jnp.sin(angles)
    return (
        jnp.concatenate([cosine, cosine], axis=1),
        jnp.concatenate([sine_table, sine_table], axis=1),
    )


def rotate(values, cosine, sine_table):
    amount = values.shape[0]
    shaped = values.reshape(amount, -1, HEAD)
    first_half = shaped[..., : HEAD // 2]
    second_half = shaped[..., HEAD // 2 :]
    turned = jnp.concatenate([-second_half, first_half], axis=-1)
    return (shaped * cosine[:, None, :] + turned * sine_table[:, None, :]).reshape(values.shape)


def rotate_back(grad_values, cosine, sine_table):
    amount = grad_values.shape[0]
    shaped = grad_values.reshape(amount, -1, HEAD)
    scaled = shaped * sine_table[:, None, :]
    turned = jnp.concatenate([scaled[..., HEAD // 2 :], -scaled[..., : HEAD // 2]], axis=-1)
    return (shaped * cosine[:, None, :] + turned).reshape(grad_values.shape)


def layout(seq_lengths, amount):
    finish = jnp.cumsum(seq_lengths)
    indices = jnp.arange(amount, dtype=jnp.int32)
    documents = jnp.sum((indices[:, None] >= finish[None, :]).astype(jnp.int32), axis=1)
    starts = finish - seq_lengths
    member = documents[:, None] == jnp.arange(seq_lengths.shape[0], dtype=jnp.int32)[None, :]
    begins = jnp.sum(jnp.where(member, starts[None, :], 0), axis=1)
    return (documents, indices - begins)


def times_transposed(left_side, right_side):
    return lax.dot_general(
        left_side, right_side, (((1,), (1,)), ((), ())), preferred_element_type=jnp.float32
    )


def transposed_times(left_side, right_side):
    return lax.dot_general(
        left_side, right_side, (((0,), (0,)), ((), ())), preferred_element_type=jnp.float32
    )


def split_queries(query_rows):
    own_rows = query_rows.shape[0]
    share = Q_HEADS // KV_HEADS
    return (
        query_rows.reshape(own_rows, KV_HEADS, share, HEAD)
        .transpose(1, 2, 0, 3)
        .reshape(KV_HEADS, share * own_rows, HEAD)
    )


def join_queries(rows):
    share = Q_HEADS // KV_HEADS
    own_rows = rows.shape[1] // share
    return (
        rows.reshape(KV_HEADS, share, own_rows, HEAD)
        .transpose(2, 0, 1, 3)
        .reshape(own_rows, Q_HEADS * HEAD)
    )


def split_keys(key_rows):
    return key_rows.reshape(key_rows.shape[0], KV_HEADS, HEAD).transpose(1, 0, 2)


def join_keys(rows):
    return rows.transpose(1, 0, 2).reshape(rows.shape[1], KV_HEADS * HEAD)


def bdot(a, b, ca, cb):
    return lax.dot_general(a, b, (((ca,), (cb,)), ((0,), (0,))), preferred_element_type=F32)


def attention_weights(query_heads, key_heads, allowed):
    scores = bdot(query_heads, key_heads, 2, 2) * score_scale
    scores = jnp.where(allowed[None], scores, masked_value)
    weights = jnp.exp(scores - jnp.max(scores, axis=-1, keepdims=True))
    return weights / jnp.sum(weights, axis=-1, keepdims=True)


def attention_forward(query_rot, key_rot, values, allowed):
    soft = attention_weights(split_queries(query_rot), split_keys(key_rot), allowed)
    mixed = bdot(soft.astype(BF), split_keys(values), 2, 1)
    return join_queries(mixed.astype(BF))


def attention_backward(query_rot, key_rot, values, grad_mixed, allowed):
    q, k, v = split_queries(query_rot), split_keys(key_rot), split_keys(values)
    g = split_queries(grad_mixed)
    soft = attention_weights(q, k, allowed)
    grad_probs = bdot(g, v, 2, 2)
    inner = jnp.sum(soft * grad_probs, axis=-1, keepdims=True)
    grad_scores = (soft * (grad_probs - inner)).astype(BF)
    grad_query = bdot(grad_scores, k, 2, 1) * score_scale
    grad_key = bdot(grad_scores, q, 1, 1) * score_scale
    grad_value = bdot(soft.astype(BF), g, 1, 1)
    return join_queries(grad_query), join_keys(grad_key), join_keys(grad_value)


def pad_cols(a):
    rows = a.shape[0]
    a = a.reshape(rows, 8, SHARD)
    return jnp.pad(a, ((0, 0), (0, 0), (0, PAD - SHARD))).reshape(rows, 8 * PAD)


def unpad_cols(a):
    rows = a.shape[0]
    return a.reshape(rows, 8, PAD)[:, :, :SHARD].reshape(rows, D)


def dot(a, b):
    return jnp.dot(a, b, preferred_element_type=F32)


def shards(
    tokens, cotangent, lengths, gain_attn, w_query, w_key, w_value, w_out, gain_mlp, w_gate, w_up, w_down
):
    own_rows = tokens.shape[0]
    doc_own, pos_own = layout(lengths[0], own_rows)
    cosine, sine_table = rope_tables(pos_own.astype(F32))
    row_index = jnp.arange(own_rows, dtype=jnp.int32)
    allowed = (doc_own[:, None] == doc_own[None, :]) & (row_index[None, :] <= row_index[:, None])
    allowed3 = jnp.concatenate([allowed] * (Q_HEADS // KV_HEADS), axis=0)

    gains = jnp.stack([gain_attn, gain_mlp], axis=1)
    gains = jnp.pad(gains, ((0, 0), (0, PAD - SHARD - 2), (0, QKV - SHARD)))
    packed_qkv = jnp.concatenate(
        [jnp.concatenate([w_query, w_key, w_value], axis=2), gains], axis=1
    )
    packed_out = jnp.pad(w_out, ((0, 0), (0, PAD - SHARD), (0, 0)))
    packed_gu = jnp.concatenate([w_gate, w_up], axis=2)
    fq, fo, fg, fd = gather(packed_qkv, packed_out, packed_gu, w_down)
    all_gains = fq[:, :, :, SHARD : SHARD + 2, :SHARD].reshape(LAYERS, 8, 2, SHARD)
    gain_one = all_gains[:, :, 0].reshape(LAYERS, D).astype(F32)
    gain_two = all_gains[:, :, 1].reshape(LAYERS, D).astype(F32)
    full_qkv = fq.reshape(LAYERS, 8 * PAD, QKV)
    full_out = fo.reshape(LAYERS, 8 * PAD, D)

    stream = tokens.astype(F32)
    saved = []
    for l in range(LAYERS):
        normed = rms_scale(stream, gain_one[l]).astype(BF)
        normed_pad = pad_cols(normed)
        proj = dot(normed_pad, full_qkv[l])
        query_rot = rotate(proj[:, :D], cosine, sine_table).astype(BF)
        key_rot = rotate(proj[:, D : D + FFS], cosine, sine_table).astype(BF)
        values = proj[:, D + FFS :].astype(BF)
        mixed_low = attention_forward(query_rot, key_rot, values, allowed3)
        mixed_pad = pad_cols(mixed_low)
        hidden = stream + dot(mixed_pad, full_out[l])
        normed_two = rms_scale(hidden, gain_two[l]).astype(BF)
        mlp_in = spread(normed_two).reshape(4 * own_rows, D)
        pre = [dot(mlp_in, fg[l, p]) for p in range(2)]
        active = []
        for p in range(2):
            gate, up = pre[p][:, :FFS], pre[p][:, FFS:]
            active.append((gate * jax.nn.sigmoid(gate) * up).astype(BF))
        partial = sum(dot(active[p], fd[l, p]) for p in range(2))
        result = collect(partial.astype(BF).reshape(4, own_rows, D), hidden)
        saved.append((stream, hidden, normed_pad, query_rot, key_rot, values, mixed_pad, mlp_in, pre, active))
        stream = result

    grad_stream = cotangent.astype(F32)
    zero = jnp.zeros((own_rows, D), F32)
    collected = [None] * LAYERS
    for l in reversed(range(LAYERS)):
        layer_in, hidden, normed_pad, query_rot, key_rot, values, mixed_pad, mlp_in, pre, active = saved[l]
        grad_low = spread(grad_stream.astype(BF)).reshape(4 * own_rows, D)
        grad_in = 0.0
        grads_gu, grads_d = [], []
        for p in range(2):
            gate, up = pre[p][:, :FFS], pre[p][:, FFS:]
            sig = jax.nn.sigmoid(gate)
            grad_active = times_transposed(grad_low, fd[l, p])
            grad_gate = grad_active * up * sig * (1.0 + gate * (1.0 - sig))
            grad_up = grad_active * gate * sig
            both = jnp.concatenate([grad_gate, grad_up], axis=1).astype(BF)
            grad_in = grad_in + times_transposed(both, fg[l, p])
            grads_gu.append(transposed_times(mlp_in, both).astype(BF))
            grads_d.append(transposed_times(active[p], grad_low).astype(BF))
        grad_input = collect(grad_in.astype(BF).reshape(4, own_rows, D), zero)
        norm_value, norm_back = jax.vjp(rms_scale, hidden, gain_two[l])
        grad_hidden_norm, grad_gain_two = norm_back(grad_input)
        grad_hidden = grad_stream + grad_hidden_norm
        grad_hidden_low = grad_hidden.astype(BF)
        grad_mixed = unpad_cols(times_transposed(grad_hidden_low, full_out[l]).astype(BF))
        grad_out = transposed_times(mixed_pad, grad_hidden_low).astype(BF)
        grad_query_rot, grad_key_rot, grad_values = attention_backward(
            query_rot, key_rot, values, grad_mixed, allowed3
        )
        grad_proj = jnp.concatenate(
            [
                rotate_back(grad_query_rot, cosine, sine_table),
                rotate_back(grad_key_rot, cosine, sine_table),
                grad_values,
            ],
            axis=1,
        ).astype(BF)
        grad_normed = unpad_cols(times_transposed(grad_proj, full_qkv[l]))
        norm_first, back_first = jax.vjp(rms_scale, layer_in, gain_one[l])
        grad_stream_norm, grad_gain_one = back_first(grad_normed)
        grad_stream = grad_hidden + grad_stream_norm
        grad_qkv = transposed_times(normed_pad, grad_proj).astype(BF).reshape(8, PAD, QKV)
        both_gains = jnp.stack([grad_gain_one.reshape(8, SHARD), grad_gain_two.reshape(8, SHARD)], axis=1)
        both_gains = jnp.pad(both_gains, ((0, 0), (0, PAD - SHARD - 2), (0, QKV - SHARD))).astype(BF)
        grad_qkv = jnp.concatenate([grad_qkv[:, :SHARD], both_gains], axis=1)
        collected[l] = (
            grad_qkv.reshape(4, 2, PAD, QKV),
            grad_out.reshape(4, 2, PAD, D),
            jnp.stack(grads_gu),
            jnp.stack(grads_d),
        )
    rq, ro, rg, rd = reduce(*[jnp.stack([collected[0][k], collected[1][k]]) for k in range(4)])
    rq, ro, rg, rd = (a.astype(F32) for a in (rq, ro, rg, rd))
    return (
        stream.astype(BF),
        grad_stream,
        rq[:, SHARD, :SHARD],
        rq[:, :SHARD, :D],
        rq[:, :SHARD, D : D + FFS],
        rq[:, :SHARD, D + FFS :],
        ro[:, :SHARD],
        rq[:, SHARD + 1, :SHARD],
        rg[:, :, :FFS],
        rg[:, :, FFS:],
        rd,
    )


def solution(mesh):
    in_specs = (
        P(("replica", "group"), None),
        P(("replica", "group"), None),
        P(("replica", "group"), None),
        P(None, "group"),
        P(None, "group", None),
        P(None, "group", None),
        P(None, "group", None),
        P(None, "group", None),
        P(None, "group"),
        P(None, None, "group"),
        P(None, None, "group"),
        P(None, "group", None),
    )
    out_specs = (
        P(("replica", "group"), None),
        P(("replica", "group"), None),
        P(None, "group"),
        P(None, "group", None),
        P(None, "group", None),
        P(None, "group", None),
        P(None, "group", None),
        P(None, "group"),
        P(None, None, "group"),
        P(None, None, "group"),
        P(None, "group", None),
    )
    return jax.shard_map(shards, mesh=mesh, in_specs=in_specs, out_specs=out_specs, check_vma=False)
```

```python
import functools

import jax
import jax.numpy as jnp
from jax import lax
from jax.experimental import pallas as pl
from jax.experimental.pallas import tpu as pltpu
from jax.sharding import PartitionSpec as P

Q_HEADS = 15
KV_HEADS = 5
HEAD = 64
LAYERS = 2
D = 960
SHARD = 120
PAD = 128
QKV = 1600
FFS = 320

norm_eps = 1e-05
rope_base = 100000.0
score_scale = 0.125
masked_value = -1e30
MESH = pl.DeviceIdType.MESH
BF = jnp.bfloat16
F32 = jnp.float32


def coords():
    r = lax.axis_index("replica")
    g = lax.axis_index("group")
    return r // 8, (r // 2) % 4, r % 2, g // 2, g % 2


def device(x_hi, z, core, y, x_lo):
    return ((x_hi * 4 + z) * 2 + core, y * 2 + x_lo)


def remote(src, dst, sems, index, target):
    return pltpu.make_async_remote_copy(
        src_ref=src,
        dst_ref=dst,
        send_sem=sems[0].at[index],
        recv_sem=sems[1].at[index],
        device_id=target,
        device_id_type=MESH,
    )


def greet(targets):
    barrier = pltpu.get_barrier_semaphore()
    for target in targets:
        pl.semaphore_signal(barrier, inc=1, device_id=target, device_id_type=MESH)
    pl.semaphore_wait(barrier, len(targets))


ANY = pl.BlockSpec(memory_space=pl.ANY)
VMEM = pl.BlockSpec(memory_space=pltpu.VMEM)
ROWS = 128
KV = KV_HEADS * HEAD
SHARE = Q_HEADS // KV_HEADS


def dot(a, b):
    return lax.dot_general(a, b, (((1,), (0,)), ((), ())), preferred_element_type=F32)


def dot_t(a, b):
    return lax.dot_general(a, b, (((1,), (1,)), ((), ())), preferred_element_type=F32)


def t_dot(a, b):
    return lax.dot_general(a, b, (((0,), (0,)), ((), ())), preferred_element_type=F32)


def lanes(g, width):
    return pl.ds(pl.multiple_of(g * PAD, PAD), width)


def halves(a):
    high = a.astype(BF)
    return high, (a - high.astype(F32)).astype(BF)


class Slots:
    def __init__(self):
        self.used = 0

    def take(self, count=1):
        self.used += count
        return self.used - count


def order(k):
    return k + (k // 2) * (5 - 2 * k)


def step_kernel(
    tokens, cotangent, cosine, sine, bias, gains,
    wq, wk, wv, wo, wg, wu, wd,
    out_act, out_grad, gq, gk, gv, go, gg, gu, gd,
    fq, fk, fv, fo, fg, fu, fd, fgain,
    place, gain_full, gain_pad, stream, hidden, grad, wide, narrow, wide_pad,
    npad, mpad, qrot, krot, vals, mixed, gproj_q, gproj_k, gproj_v, gmix,
    acts_in, grads_in, parts, came,
    s_gate, s_up, s_act, s_gg, s_gu, tg, tu, td, own_part, glow, gain_grad,
    send, recv, local,
):
    x_hi, z, core, y, x_lo = coords()
    sems = (send, recv)
    slots = Slots()
    sibling = device(x_hi, z, 1 - core, y, x_lo)
    near = [device(x_hi, z, core, y, 1 - x_lo), device(1 - x_hi, z, core, y, 1 - x_lo)]

    def along_y(k):
        return device(x_hi, z, core, (y + k) % 4, x_lo)

    greet(
        [device(x_hi, z, core, (y + k) % 4, (x_lo + e) % 2) for k in range(4) for e in range(2) if k + e]
        + [near[1], sibling]
    )
    home = core == x_lo
    guest = jnp.logical_not(home)

    slabs = [(wq, fq, 0), (wk, fk, 1), (wv, fv, 1), (wo, fo, 1)]
    keep, ring, cross, swap_cores = {}, {}, {}, {}
    for l in range(LAYERS):
        for a, (src, dst, side) in enumerate(slabs):
            keep[l, a] = pltpu.make_async_copy(src.at[l], dst.at[l, y, core], local.at[l * 8 + a])
            for k in (1, 2, 3):
                ring[l, a, k] = remote(src.at[l], dst.at[l, y, core], sems, slots.take(), along_y(k))
            for k in range(4):
                at = dst.at[l, (y - k) % 4, core]
                cross[l, a, k] = remote(
                    src.at[l] if k == 0 else at, at, sems, slots.take(), near[side]
                )
                swap_cores[l, a, k] = remote(at, at, sems, slots.take(), sibling)
    own_gain = fgain.at[y, x_lo]
    gain_keep = pltpu.make_async_copy(gains, own_gain, local.at[16])
    members = [(k, e) for k in range(4) for e in range(2) if k + e > 0]

    def member(k, e):
        return device(x_hi, z, core, (y + k) % 4, (x_lo + e) % 2)

    gain_send = {
        (k, e): remote(gains, own_gain, sems, slots.take(), member(k, e)) for k, e in members
    }
    half_g, half_d = D // 2, FFS // 2
    rows_g = pl.ds(pl.multiple_of(core * half_g, 16), half_g)
    rows_d = pl.ds(pl.multiple_of(core * half_d, 16), half_d)
    pairs = [(wg, fg, rows_g), (wu, fu, rows_g), (wd, fd, rows_d)]
    keep_m, cross_m, pass_m = {}, {}, {}
    for l in range(LAYERS):
        for a, (src, dst, rows) in enumerate(pairs):
            keep_m[l, a] = pltpu.make_async_copy(src.at[l], dst.at[l, x_lo], local.at[l * 8 + 4 + a])
            cross_m[l, a] = remote(src.at[l, rows], dst.at[l, x_lo, rows], sems, slots.take(), near[l])
            there = dst.at[l, 1 - x_lo, rows]
            pass_m[l, a] = remote(there, there, sems, slots.take(), sibling)

    def gather_begin(l, arrays):
        @pl.when(home)
        def _():
            for a in arrays:
                for k in (1, 3, 2):
                    ring[l, a, k].start()
                cross[l, a, 0].start()
                keep[l, a].start()

    def gather_pass(l, arrays):
        for a in arrays:

            @pl.when(home)
            def _():
                keep[l, a].wait()
                swap_cores[l, a, 0].start()
                for k in (1, 3, 2):
                    ring[l, a, k].wait_recv()
                    cross[l, a, k].start()
                    swap_cores[l, a, k].start()

            @pl.when(guest)
            def _():
                for k in (0, 1, 3, 2):
                    cross[l, a, k].wait_recv()
                    swap_cores[l, a, k].start()

    def gather_end(l, arrays):
        for a in arrays:
            for k in range(4):
                swap_cores[l, a, k].wait_recv()

    def gather_sent(l, arrays):
        for a in arrays:

            @pl.when(home)
            def _():
                for k in (1, 2, 3):
                    ring[l, a, k].wait_send()
                for k in range(4):
                    cross[l, a, k].wait_send()

            for k in range(4):
                swap_cores[l, a, k].wait_send()

    def pairs_begin(l):
        for a in range(3):
            cross_m[l, a].start()
            keep_m[l, a].start()

    def pairs_pass(l):
        for a in range(3):
            cross_m[l, a].wait_recv()
            pass_m[l, a].start()

    def pairs_end(l):
        for a in range(3):
            pass_m[l, a].wait_recv()
            keep_m[l, a].wait()

    spread_at = [slots.take(4) for _ in range(4)]
    back_at = [slots.take(4) for _ in range(4)]

    def spread_copy(n, buffer, k):
        return remote(
            buffer.at[y], buffer.at[y], sems, spread_at[n] + k, along_y(k)
        )

    def spread(n, buffer):
        for k in (1, 3, 2):
            spread_copy(n, buffer, k).start()

    def arrived(n, buffer, k):
        there = buffer.at[(y - k + 4) % 4]
        remote(there, there, sems, spread_at[n] + k, along_y(k)).wait_recv()

    def back_copy(n, k):
        return remote(
            parts.at[n % 2, k - 1], came.at[n % 2, k - 1], sems, back_at[n] + k, along_y(4 - k)
        )

    def collect(n, total):
        for k in (1, 3, 2):
            back_copy(n, k).wait_recv()
            total = total + came[n % 2, k - 1].astype(F32)
        return total

    def sent(n, buffer):
        for k in (1, 2, 3):
            spread_copy(n, buffer, k).wait_send()
            back_copy(n, k).wait_send()

    column = lax.broadcasted_iota(jnp.int32, (ROWS, PAD), 1)
    first_half = column % HEAD < HEAD // 2

    def turn(block, sign):
        ahead = pltpu.roll(block, PAD - HEAD // 2, 1)
        behind = pltpu.roll(block, HEAD // 2, 1)
        return jnp.where(first_half, -sign * ahead, sign * behind)

    def rotated(block):
        return block * cosine[...] + turn(block, 1.0) * sine[...]

    def rotated_back(block):
        return block * cosine[...] + turn(block * sine[...], -1.0)

    def inverse_rms(x):
        return lax.rsqrt(jnp.mean(x * x, axis=-1, keepdims=True) + norm_eps)

    def head_lanes(h):
        return slice(h * HEAD, (h + 1) * HEAD)

    def soft_weights(l, kv):
        rows = jnp.concatenate([qrot[l, :, head_lanes(kv * SHARE + i)] for i in range(SHARE)], axis=0)
        keys = krot[l, :, head_lanes(kv)]
        scores = dot_t(rows, keys) * score_scale
        scores = scores + jnp.concatenate([bias[...]] * SHARE, axis=0)
        weights = jnp.exp(scores - jnp.max(scores, axis=-1, keepdims=True))
        return rows, keys, weights / jnp.sum(weights, axis=-1, keepdims=True)

    def attention_forward(l):
        x = stream[l]
        normed = (x * inverse_rms(x) * gain_full[l : l + 1, :]).astype(BF)
        npad[l] = dot(normed, place[...]).astype(BF)

        def project(weights, width):
            total = jnp.zeros((ROWS, width), F32)
            for g in range(8):
                total = total + dot(npad[l, :, g * PAD : g * PAD + SHARD], weights[l, g // 2, g % 2])
            return total

        gather_end(l, (0, 1, 2))
        wide[:, :D] = project(fq, D)
        narrow[:, :KV] = project(fk, KV)
        vals[l, :, :KV] = project(fv, KV).astype(BF)
        for j in range(8):
            at = slice(j * PAD, (j + 1) * PAD)
            qrot[l, :, at] = rotated(wide[:, at]).astype(BF)
        for j in range(3):
            at = slice(j * PAD, (j + 1) * PAD)
            krot[l, :, at] = rotated(narrow[:, at]).astype(BF)
        for kv in range(KV_HEADS):
            rows, keys, soft = soft_weights(l, kv)
            out = dot(soft.astype(BF), vals[l, :, head_lanes(kv)]).astype(BF)
            for i in range(SHARE):
                mixed[:, head_lanes(kv * SHARE + i)] = out[i * ROWS : (i + 1) * ROWS]
        mpad[l] = dot(mixed[:, :D], place[...]).astype(BF)
        gather_end(l, (3,))
        total = x
        for g in range(8):
            total = total + dot(mpad[l, :, g * PAD : g * PAD + SHARD], fo[l, g // 2, g % 2])
        hidden[l] = total
        acts_in[l, y] = (total * inverse_rms(total) * gain_full[2 + l : 3 + l, :]).astype(BF)

    def mlp_forward(l, n):
        buffer = acts_in.at[l]

        def block(i, carry):
            k = order(i)
            b = (y - k + 4) % 4

            @pl.when(i > 0)
            def _():
                arrived(n, buffer, k)

            rows = acts_in[l, b]
            total = jnp.zeros((ROWS, D), F32)
            for p in range(2):
                gate = dot(rows, fg[l, p])
                up = dot(rows, fu[l, p])
                act = (gate * jax.nn.sigmoid(gate) * up).astype(BF)
                s_gate[l, p, b] = gate.astype(BF)
                s_up[l, p, b] = up.astype(BF)
                s_act[l, p, b] = act
                total = total + dot(act, fd[l, p])

            @pl.when(i == 0)
            def _():
                own_part[...] = total

            @pl.when(i > 0)
            def _():
                parts[n % 2, k - 1] = total.astype(BF)
                back_copy(n, k).start()

            return carry

        lax.fori_loop(0, 4, block, 0)

    def mlp_backward(l, n):
        buffer = grads_in.at[1 - l]

        def block(i, carry):
            k = order(i)
            b = (y - k + 4) % 4

            @pl.when(i > 0)
            def _():
                arrived(n, buffer, k)

            rows = grads_in[1 - l, b]
            total = jnp.zeros((ROWS, D), F32)
            for p in range(2):
                grad_active = dot_t(rows, fd[l, p])
                gate = s_gate[l, p, b].astype(F32)
                up = s_up[l, p, b].astype(F32)
                sig = jax.nn.sigmoid(gate)
                grad_gate = (grad_active * up * sig * (1.0 + gate * (1.0 - sig))).astype(BF)
                grad_up = (grad_active * gate * sig).astype(BF)
                s_gg[p, b] = grad_gate
                s_gu[p, b] = grad_up
                total = total + dot_t(grad_gate, fg[l, p]) + dot_t(grad_up, fu[l, p])

            @pl.when(i == 0)
            def _():
                own_part[...] = total

            @pl.when(i > 0)
            def _():
                parts[n % 2, k - 1] = total.astype(BF)
                back_copy(n, k).start()

            return carry

        lax.fori_loop(0, 4, block, 0)

        if l == 0:
            for copy in out_pairs(1):
                copy.wait()

        def grads(p, carry):
            ins = acts_in[l].reshape(4 * ROWS, D)
            tg[p] = t_dot(ins, s_gg[p].reshape(4 * ROWS, FFS)).astype(BF)
            tu[p] = t_dot(ins, s_gu[p].reshape(4 * ROWS, FFS)).astype(BF)
            td[p] = t_dot(
                s_act[l, p].reshape(4 * ROWS, FFS), grads_in[1 - l].reshape(4 * ROWS, D)
            ).astype(BF)
            return carry

        lax.fori_loop(0, 2, grads, 0)
        for copy in out_pairs(l):
            copy.start()

    def out_pairs(l):
        return [
            pltpu.make_async_copy(src, dst.at[l], local.at[17 + l * 3 + a])
            for a, (src, dst) in enumerate(((tg, gg), (tu, gu), (td, gd)))
        ]

    def slab_loop(body):
        def run(g, carry):
            body(g, g // 2, g % 2)
            return carry

        lax.fori_loop(0, 8, run, 0)

    def norm_back(x, grad_normed, gain_row):
        r = inverse_rms(x)
        u = grad_normed * gain_row
        back = r * u - x * (r * r * r) * jnp.mean(u * x, axis=-1, keepdims=True)
        return back, jnp.sum(grad_normed * x * r, axis=0, keepdims=True)

    def attention_backward(l, n):
        grad_input = collect(n, own_part[...])
        back, grad_gain_two = norm_back(hidden[l], grad_input, gain_full[2 + l : 3 + l, :])
        grad_hidden = grad[...] + back
        grad[...] = grad_hidden
        grad_low = grad_hidden.astype(BF)
        glow[...] = grad_low

        def back_out(g, h, i):
            wide_pad[:, lanes(g, SHARD)] = dot_t(glow[...], fo[l, h, i])

        slab_loop(back_out)
        gmix[...] = dot_t(wide_pad[...].astype(BF), place[...]).astype(BF)

        def grads_out(g, h, i):
            go[l, h, i] = t_dot(mpad[l, :, lanes(g, PAD)], glow[...]).astype(BF)

        slab_loop(grads_out)
        for kv in range(KV_HEADS):
            rows, keys, soft = soft_weights(l, kv)
            heads = [kv * SHARE + i for i in range(SHARE)]
            gm = jnp.concatenate([gmix[:, head_lanes(h)] for h in heads], axis=0)
            grad_probs = dot_t(gm, vals[l, :, head_lanes(kv)])
            inner = jnp.sum(soft * grad_probs, axis=-1, keepdims=True)
            grad_scores = (soft * (grad_probs - inner)).astype(BF)
            grad_rows = dot(grad_scores, keys) * score_scale
            for i, h in enumerate(heads):
                wide[:, head_lanes(h)] = grad_rows[i * ROWS : (i + 1) * ROWS]
            narrow[:, head_lanes(kv)] = t_dot(grad_scores, rows) * score_scale
            gproj_v[:, head_lanes(kv)] = t_dot(soft.astype(BF), gm).astype(BF)
        for j in range(8):
            at = slice(j * PAD, (j + 1) * PAD)
            gproj_q[:, at] = rotated_back(wide[:, at]).astype(BF)
        for j in range(3):
            at = slice(j * PAD, (j + 1) * PAD)
            gproj_k[:, at] = rotated_back(narrow[:, at]).astype(BF)

        def back_in(g, h, i):
            wide_pad[:, lanes(g, SHARD)] = (
                dot_t(gproj_q[:, :D], fq[l, h, i])
                + dot_t(gproj_k[:, :KV], fk[l, h, i])
                + dot_t(gproj_v[:, :KV], fv[l, h, i])
            )

        slab_loop(back_in)
        high, low = halves(wide_pad[...])
        grad_normed = dot_t(high, place[...]) + dot_t(low, place[...])
        back, grad_gain_one = norm_back(stream[l], grad_normed, gain_full[l : l + 1, :])
        grad_stream = grad[...] + back
        grad[...] = grad_stream
        if l > 0:
            grads_in[1, y] = grad_stream.astype(BF)
            spread(3, grads_in.at[1])
        else:
            out_grad[...] = grad_stream
        row = lax.broadcasted_iota(jnp.int32, (16, D), 0)
        both = jnp.where(row == 0, grad_gain_one, 0.0) + jnp.where(row == 1, grad_gain_two, 0.0)
        high, low = halves(both)
        gain_grad[...] = dot(high, place[...]) + dot(low, place[...])

        def grads_in_proj(g, h, i):
            left = npad[l, :, lanes(g, PAD)]
            total = t_dot(left, gproj_q[:, :D])
            rows = lax.broadcasted_iota(jnp.int32, (PAD, PAD), 0)
            one = gain_grad[0:1, lanes(g, PAD)]
            two = gain_grad[1:2, lanes(g, PAD)]
            corner = (
                total[:, :PAD]
                + jnp.where(rows == SHARD, one, 0.0)
                + jnp.where(rows == SHARD + 1, two, 0.0)
            )
            gq[l, h, i] = total.astype(BF)
            gq[l, h, i, :, :PAD] = corner.astype(BF)
            gk[l, h, i] = t_dot(left, gproj_k[:, :KV]).astype(BF)
            gv[l, h, i] = t_dot(left, gproj_v[:, :KV]).astype(BF)

        slab_loop(grads_in_proj)

    gather_begin(0, range(4))
    gain_keep.start()
    for copy in gain_send.values():
        copy.start()
    wide_column = lax.broadcasted_iota(jnp.int32, (D, 8 * PAD), 1)
    row = lax.broadcasted_iota(jnp.int32, (D, 8 * PAD), 0)
    lane = wide_column % PAD
    place[...] = jnp.where(
        jnp.logical_and(lane < SHARD, (wide_column // PAD) * SHARD + lane == row), 1.0, 0.0
    ).astype(BF)
    wide[...] = jnp.zeros_like(wide)
    wide_pad[...] = jnp.zeros_like(wide_pad)
    narrow[...] = jnp.zeros_like(narrow)
    stream[0] = tokens[...].astype(F32)
    gather_pass(0, (0, 1, 2))
    pairs_begin(0)
    gather_pass(0, (3,))
    gather_begin(1, range(4))
    pairs_begin(1)
    gain_keep.wait()
    for copy in gain_send.values():
        copy.wait()
    for g in range(8):
        gain_pad[:, g * PAD : (g + 1) * PAD] = fgain[g // 2, g % 2]
    gain_full[...] = dot_t(gain_pad[...], place[...])
    attention_forward(0)
    spread(0, acts_in.at[0])
    gather_pass(1, range(4))
    pairs_pass(0)
    pairs_pass(1)
    pairs_end(0)
    mlp_forward(0, 0)
    grads_in[0, y] = cotangent[...]
    grad[...] = cotangent[...].astype(F32)
    stream[1] = collect(0, own_part[...] + hidden[0])
    spread(2, grads_in.at[0])
    attention_forward(1)
    spread(1, acts_in.at[1])
    pairs_end(1)
    sent(0, acts_in.at[0])
    mlp_forward(1, 1)
    result = own_part[...] + hidden[1]
    wide[:, :D] = result
    mlp_backward(1, 2)
    out_act[...] = collect(1, wide[:, :D]).astype(BF)
    attention_backward(1, 2)
    sent(1, acts_in.at[1])
    mlp_backward(0, 3)
    attention_backward(0, 3)
    for copy in out_pairs(0):
        copy.wait()
    sent(2, grads_in.at[0])
    sent(3, grads_in.at[1])
    for l in range(LAYERS):
        gather_sent(l, range(4))
        for a in range(3):
            cross_m[l, a].wait_send()
            pass_m[l, a].wait_send()


def step(tokens, cotangent, cosine, sine, bias, gains, *weights):
    L = LAYERS

    def buf(*shape, dtype=BF):
        return pltpu.VMEM(shape, dtype)

    def out(*shape, dtype=BF):
        return jax.ShapeDtypeStruct(shape, dtype)

    count = 160
    return pl.pallas_call(
        step_kernel,
        out_shape=(
            out(ROWS, D),
            out(ROWS, D, dtype=F32),
            out(L, 4, 2, PAD, D),
            out(L, 4, 2, PAD, KV),
            out(L, 4, 2, PAD, KV),
            out(L, 4, 2, PAD, D),
            out(L, 2, D, FFS),
            out(L, 2, D, FFS),
            out(L, 2, FFS, D),
        ),
        in_specs=[VMEM] * 6 + [ANY] * 7,
        out_specs=[VMEM] * 6 + [ANY] * 3,
        scratch_shapes=[
            buf(L, 4, 2, SHARD, D),
            buf(L, 4, 2, SHARD, KV),
            buf(L, 4, 2, SHARD, KV),
            buf(L, 4, 2, SHARD, D),
            buf(L, 2, D, FFS),
            buf(L, 2, D, FFS),
            buf(L, 2, FFS, D),
            buf(4, 2, 16, PAD),
            buf(D, 8 * PAD),
            buf(16, D, dtype=F32),
            buf(16, 8 * PAD),
            buf(L, ROWS, D, dtype=F32),
            buf(L, ROWS, D, dtype=F32),
            buf(ROWS, D, dtype=F32),
            buf(ROWS, 8 * PAD, dtype=F32),
            buf(ROWS, 3 * PAD, dtype=F32),
            buf(ROWS, 8 * PAD, dtype=F32),
            buf(L, ROWS, 8 * PAD),
            buf(L, ROWS, 8 * PAD),
            buf(L, ROWS, 8 * PAD),
            buf(L, ROWS, 3 * PAD),
            buf(L, ROWS, 3 * PAD),
            buf(ROWS, 8 * PAD),
            buf(ROWS, 8 * PAD),
            buf(ROWS, 3 * PAD),
            buf(ROWS, 3 * PAD),
            buf(ROWS, D),
            buf(L, 4, ROWS, D),
            buf(2, 4, ROWS, D),
            buf(2, 3, ROWS, D),
            buf(2, 3, ROWS, D),
            buf(L, 2, 4, ROWS, FFS),
            buf(L, 2, 4, ROWS, FFS),
            buf(L, 2, 4, ROWS, FFS),
            buf(2, 4, ROWS, FFS),
            buf(2, 4, ROWS, FFS),
            buf(2, D, FFS),
            buf(2, D, FFS),
            buf(2, FFS, D),
            buf(ROWS, D, dtype=F32),
            buf(ROWS, D),
            buf(16, 8 * PAD, dtype=F32),
            pltpu.SemaphoreType.DMA((count,)),
            pltpu.SemaphoreType.DMA((count,)),
            pltpu.SemaphoreType.DMA((24,)),
        ],
        compiler_params=pltpu.CompilerParams(
            collective_id=1, has_side_effects=True, vmem_limit_bytes=63 * 2**20
        ),
    )(tokens, cotangent, cosine, sine, bias, gains, *weights)


def add_into(dst, others, step=16):
    rows = dst.shape[0]

    def body(i, carry):
        at = pl.ds(pl.multiple_of(i * step, step), step)
        total = dst[at, :].astype(F32)
        for other in others:
            total = total + other[at, :].astype(F32)
        dst[at, :] = total.astype(dst.dtype)
        return carry

    lax.fori_loop(0, rows // step, body, 0)


def add_to(dst, terms, step=16):
    rows = dst.shape[0]

    def body(i, carry):
        at = pl.ds(pl.multiple_of(i * step, step), step)
        total = terms[0][at, :].astype(F32)
        for other in terms[1:]:
            total = total + other[at, :].astype(F32)
        dst[at, :] = total.astype(dst.dtype)
        return carry

    lax.fori_loop(0, rows // step, body, 0)


SLABS = (D, KV, KV, D)
PAIRS = ((D, FFS), (D, FFS), (FFS, D))


def reduce_kernel(*refs):
    def take(count):
        nonlocal refs
        got, refs = refs[:count], refs[count:]
        return got

    gs, gp = take(4), take(3)
    fs, fp = take(4), take(3)
    ss, sp = take(4), take(3)
    xs, xp = take(4), take(3)
    ys, ls = take(4), take(4)
    zs, zp = take(4), take(3)
    ps, pp = take(4), take(3)
    hs, hp = take(4), take(3)
    send, recv = refs
    x_hi, z, core, y, x_lo = coords()
    sems = (send, recv)
    sibling = device(x_hi, z, 1 - core, y, x_lo)
    near = [device(x_hi, z, core, y, 1 - x_lo), device(1 - x_hi, z, core, y, 1 - x_lo)]
    far = device(1 - x_hi, z, core, y, x_lo)
    ring_y = {k: device(x_hi, z, core, (y + k) % 4, x_lo) for k in (1, 2, 3)}
    ring_z = {k: device(x_hi, (z + k) % 4, core, y, x_lo) for k in (1, 2, 3)}
    greet(list(ring_y.values()) + list(ring_z.values()) + near + [far, sibling])
    home = core == x_lo
    slots = Slots()
    layers = (1, 0)

    def part(rows, where):
        return pl.ds(pl.multiple_of(where * (rows // 4), 16), rows // 4)

    pieces = [(sp[a], zp[a], pp[a], hp[a], fp[a], PAIRS[a][0]) for a in range(3)] + [
        (ls[a], zs[a], ps[a], hs[a], fs[a], PAD) for a in range(4)
    ]
    pair, over_x, over_y, over_z, over_h, out_z, last = {}, {}, {}, {}, {}, {}, {}
    for l in layers:
        for a in range(7):
            if a < 3:
                own, got = gp[a].at[l, 1 - core], sp[a].at[l]
                src, dst = sp[a].at[l], xp[a].at[l]
            else:
                own, got = gs[a - 3].at[l, :, 1 - core], ss[a - 3].at[l]
                src, dst = ss[a - 3].at[l], xs[a - 3].at[l]
                for k in (1, 2, 3):
                    over_y[l, a, k] = remote(
                        src.at[(y + k) % 4], ys[a - 3].at[l, k - 1], sems, slots.take(), ring_y[k]
                    )
            pair[l, a] = remote(own, got, sems, slots.take(), sibling)
            over_x[l, a] = remote(src, dst, sems, slots.take(), near[l])
            src, zb, pb, hb, fb, rows = pieces[a]
            for k in (1, 2, 3):
                over_z[l, a, k] = remote(
                    src.at[l, part(rows, (z + k) % 4)], zb.at[l, k - 1], sems, slots.take(), ring_z[k]
                )
                mine = fb.at[l, part(rows, z)]
                out_z[l, a, k] = remote(mine, mine, sems, slots.take(), ring_z[k])
            over_h[l, a] = remote(pb.at[l], hb.at[l], sems, slots.take(), far)
            last[l, a] = remote(fb.at[l], fb.at[l], sems, slots.take(), sibling)
    for l in layers:
        for a in range(7):
            pair[l, a].start()
    for l in layers:
        for a in range(7):
            pair[l, a].wait_recv()
            if a < 3:
                add_into(sp[a].at[l], [gp[a].at[l, core]])
            else:
                for q in range(4):
                    add_into(ss[a - 3].at[l, q], [gs[a - 3].at[l, q, core]])

            @pl.when(jnp.logical_not(home))
            def _():
                over_x[l, a].start()

    @pl.when(home)
    def _():
        for l in layers:
            for a in range(7):
                over_x[l, a].wait_recv()
                if a < 3:
                    add_into(sp[a].at[l], [xp[a].at[l]])
                    for k in (1, 3, 2):
                        over_z[l, a, k].start()
                else:
                    for k in (1, 3, 2, 0):
                        q = (y + k) % 4
                        add_into(ss[a - 3].at[l, q], [xs[a - 3].at[l, q]])
                        if k:
                            over_y[l, a, k].start()
        for l in layers:
            for a in range(3, 7):
                for k in (1, 3, 2):
                    over_y[l, a, k].wait_recv()
                add_to(ls[a - 3].at[l], [ss[a - 3].at[l, y]] + [ys[a - 3].at[l, j] for j in range(3)])
                for k in (1, 3, 2):
                    over_z[l, a, k].start()
        for l in layers:
            for a in range(7):
                src, zb, pb, hb, fb, rows = pieces[a]
                for k in (1, 3, 2):
                    over_z[l, a, k].wait_recv()
                add_to(pb.at[l], [src.at[l, part(rows, z)]] + [zb.at[l, j] for j in range(3)])
                over_h[l, a].start()
        for l in layers:
            for a in range(7):
                src, zb, pb, hb, fb, rows = pieces[a]
                over_h[l, a].wait_recv()
                add_to(fb.at[l, part(rows, z)], [pb.at[l], hb.at[l]])
                for k in (1, 3, 2):
                    out_z[l, a, k].start()
        for l in layers:
            for a in range(7):
                for k in (1, 3, 2):
                    out_z[l, a, k].wait_recv()
                last[l, a].start()
        for l in layers:
            for a in range(7):
                last[l, a].wait_send()
                over_h[l, a].wait_send()
                for k in (1, 3, 2):
                    over_z[l, a, k].wait_send()
                    out_z[l, a, k].wait_send()
                    if a >= 3:
                        over_y[l, a, k].wait_send()

    @pl.when(jnp.logical_not(home))
    def _():
        for copy in over_x.values():
            copy.wait_send()
        for copy in last.values():
            copy.wait_recv()

    for copy in pair.values():
        copy.wait_send()


def reduce(*grads):
    count = 180
    L = LAYERS

    def bufs(slab, pair_of):
        return [pltpu.VMEM(slab + (n,), BF) for n in SLABS] + [
            pltpu.VMEM(pair_of(r) + (n,), BF) for r, n in PAIRS
        ]

    full = bufs((L, 4, PAD), lambda r: (L, r))
    quarter = bufs((L, PAD // 4), lambda r: (L, r // 4))
    return pl.pallas_call(
        reduce_kernel,
        out_shape=[jax.ShapeDtypeStruct((L, PAD, n), BF) for n in SLABS]
        + [jax.ShapeDtypeStruct((L, r, n), BF) for r, n in PAIRS],
        in_specs=[VMEM] * 7,
        out_specs=[VMEM] * 7,
        scratch_shapes=full
        + full
        + bufs((L, 3, PAD), lambda r: (L, 3, r))[:4]
        + bufs((L, PAD), lambda r: (L, r))[:4]
        + bufs((L, 3, PAD // 4), lambda r: (L, 3, r // 4))
        + quarter
        + quarter
        + [pltpu.SemaphoreType.DMA((count,)), pltpu.SemaphoreType.DMA((count,))],
        compiler_params=pltpu.CompilerParams(
            collective_id=2, has_side_effects=True, vmem_limit_bytes=63 * 2**20
        ),
    )(*grads)


def rope_tables(positions):
    steps_half = jnp.arange(HEAD // 2, dtype=jnp.float32)
    inverse = rope_base ** (-2.0 * steps_half / HEAD)
    angles = positions[:, None] * inverse[None, :]
    cosine = jnp.cos(angles)
    sine_table = jnp.sin(angles)
    return (
        jnp.concatenate([cosine, cosine], axis=1),
        jnp.concatenate([sine_table, sine_table], axis=1),
    )


def layout(seq_lengths, amount):
    finish = jnp.cumsum(seq_lengths)
    indices = jnp.arange(amount, dtype=jnp.int32)
    documents = jnp.sum((indices[:, None] >= finish[None, :]).astype(jnp.int32), axis=1)
    starts = finish - seq_lengths
    member = documents[:, None] == jnp.arange(seq_lengths.shape[0], dtype=jnp.int32)[None, :]
    begins = jnp.sum(jnp.where(member, starts[None, :], 0), axis=1)
    return (documents, indices - begins)


def shards(
    tokens, cotangent, lengths, gain_attn, w_query, w_key, w_value, w_out, gain_mlp, w_gate, w_up, w_down
):
    doc_own, pos_own = layout(lengths[0], ROWS)
    cosine, sine_table = rope_tables(pos_own.astype(F32))
    row_index = jnp.arange(ROWS, dtype=jnp.int32)
    allowed = (doc_own[:, None] == doc_own[None, :]) & (row_index[None, :] <= row_index[:, None])
    bias = jnp.where(allowed, 0.0, masked_value).astype(F32)
    twice = functools.partial(jnp.tile, reps=(1, 2))
    gains = jnp.pad(jnp.concatenate([gain_attn, gain_mlp], axis=0), ((0, 12), (0, PAD - SHARD)))
    act, grad, *grads = step(
        tokens, cotangent, twice(cosine), twice(sine_table), bias, gains,
        w_query, w_key, w_value, w_out, w_gate, w_up, w_down,
    )
    rq, rk, rv, ro, rg, ru, rd = (a.astype(F32) for a in reduce(*grads))
    return (
        act,
        grad,
        rq[:, SHARD, :SHARD],
        rq[:, :SHARD],
        rk[:, :SHARD],
        rv[:, :SHARD],
        ro[:, :SHARD],
        rq[:, SHARD + 1, :SHARD],
        rg,
        ru,
        rd,
    )


def solution(mesh):
    in_specs = (
        P(("replica", "group"), None),
        P(("replica", "group"), None),
        P(("replica", "group"), None),
        P(None, "group"),
        P(None, "group", None),
        P(None, "group", None),
        P(None, "group", None),
        P(None, "group", None),
        P(None, "group"),
        P(None, None, "group"),
        P(None, None, "group"),
        P(None, "group", None),
    )
    out_specs = (
        P(("replica", "group"), None),
        P(("replica", "group"), None),
        P(None, "group"),
        P(None, "group", None),
        P(None, "group", None),
        P(None, "group", None),
        P(None, "group", None),
        P(None, "group"),
        P(None, None, "group"),
        P(None, None, "group"),
        P(None, "group", None),
    )
    return jax.shard_map(shards, mesh=mesh, in_specs=in_specs, out_specs=out_specs, check_vma=False)
```

```python
import jax
import jax.numpy as jnp
from jax import lax
from jax.experimental import pallas as pl
from jax.experimental.pallas import tpu as pltpu
from jax.sharding import PartitionSpec as P

Q_HEADS = 15
KV_HEADS = 5
HEAD = 64
LAYERS = 2
D = 960
SHARD = 120
PAD = 128
FFS = 320
ROWS = 128
KV = KV_HEADS * HEAD
SHARE = Q_HEADS // KV_HEADS

norm_eps = 1e-05
rope_base = 100000.0
log_base = 11.512925464970229
score_scale = 0.125
masked_value = -1e30
MESH = pl.DeviceIdType.MESH
BF = jnp.bfloat16
F32 = jnp.float32
ANY = pl.BlockSpec(memory_space=pl.ANY)
VMEM = pl.BlockSpec(memory_space=pltpu.VMEM)
SMEM = pl.BlockSpec(memory_space=pltpu.SMEM)


def coords():
    r = lax.axis_index("replica")
    g = lax.axis_index("group")
    return r // 8, (r // 2) % 4, r % 2, g // 2, g % 2


def device(x_hi, z, core, y, x_lo):
    return ((x_hi * 4 + z) * 2 + core, y * 2 + x_lo)


def remote(src, dst, sems, index, target):
    return pltpu.make_async_remote_copy(
        src_ref=src,
        dst_ref=dst,
        send_sem=sems[0].at[index],
        recv_sem=sems[1].at[index],
        device_id=target,
        device_id_type=MESH,
    )


def dot(a, b):
    return lax.dot_general(a, b, (((1,), (0,)), ((), ())), preferred_element_type=F32)


def dot_t(a, b):
    return lax.dot_general(a, b, (((1,), (1,)), ((), ())), preferred_element_type=F32)


def t_dot(a, b):
    return lax.dot_general(a, b, (((0,), (0,)), ((), ())), preferred_element_type=F32)


def lanes(g, width):
    return pl.ds(pl.multiple_of(g * PAD, PAD), width)


def halves(a):
    high = a.astype(BF)
    return high, (a - high.astype(F32)).astype(BF)


def accumulate(dst, others, chunk):
    def body(i, carry):
        at = pl.ds(pl.multiple_of(i * chunk, chunk), chunk)
        total = dst[at, :].astype(F32)
        for other in others:
            total = total + other[at, :].astype(F32)
        dst[at, :] = total.astype(dst.dtype)
        return carry

    lax.fori_loop(0, dst.shape[0] // chunk, body, 0)


class Slots:
    def __init__(self):
        self.used = 0

    def take(self, count=1):
        self.used += count
        return self.used - count


def order(k):
    return k + (k // 2) * (5 - 2 * k)


KINDS = {
    "m": ((3, FFS, D), False),
    "o": ((1, ROWS, D), True),
    "q": ((1, ROWS, D), True),
    "kv": ((2, KV, PAD), True),
}
TWICE = ("q", "kv")
ORDER_Y = (1, 3, 2)


def quarter(shape):
    return (shape[0], shape[1] // 4, shape[2])


def scratch_shapes():
    L = LAYERS
    named = {}

    def buf(name, *shape, dtype=BF):
        named[name] = pltpu.VMEM(shape, dtype)

    buf("aq", 4, 2, SHARD, D)
    buf("ao", 4, 2, SHARD, D)
    buf("ak", 4, 2, KV, SHARD)
    buf("av", 4, 2, KV, SHARD)
    buf("mw", 2, 3, FFS, D)
    buf("all_gains", 4, 2, 16, PAD)
    buf("own_gains", 16, PAD)
    buf("place", D, 8 * PAD)
    buf("cosine", ROWS, PAD, dtype=F32)
    buf("sine", ROWS, PAD, dtype=F32)
    buf("bias", ROWS, ROWS, dtype=F32)
    buf("gain_full", 16, D, dtype=F32)
    buf("gain_pad", 16, 8 * PAD)
    buf("gain_grad", 16, 8 * PAD, dtype=F32)
    buf("stream", L, ROWS, D, dtype=F32)
    buf("hidden", L, ROWS, D, dtype=F32)
    buf("grad", ROWS, D, dtype=F32)
    buf("wide", ROWS, 8 * PAD, dtype=F32)
    buf("narrow", ROWS, 3 * PAD, dtype=F32)
    buf("own_part", ROWS, D, dtype=F32)
    buf("npad", L, ROWS, 8 * PAD)
    buf("mpad", L, ROWS, 8 * PAD)
    buf("qrot", L, ROWS, 8 * PAD)
    buf("krot", L, ROWS, 3 * PAD)
    buf("vals", L, ROWS, 3 * PAD)
    buf("gproj_q", ROWS, 8 * PAD)
    buf("gproj_k", ROWS, 3 * PAD)
    buf("gproj_v", ROWS, 3 * PAD)
    buf("gmix", ROWS, D)
    buf("glow", ROWS, D)
    buf("acts_in", L, 4, ROWS, D)
    buf("grads_in", 2, 4, ROWS, D)
    buf("parts", 2, 3, ROWS, D)
    buf("came", 2, 3, ROWS, D)
    buf("s_gate", L, 2, 4, ROWS, FFS)
    buf("s_up", L, 2, 4, ROWS, FFS)
    buf("s_act", L, 2, 4, ROWS, FFS)
    for kind, (shape, spread) in KINDS.items():
        four = (4,) if spread else ()
        copies = L if kind in TWICE else 1
        buf("g_" + kind, *four, 2, *shape)
        buf("s_" + kind, copies, *four, *shape)
        buf("x_" + kind, copies, *four, *shape)
        if spread:
            buf("y_" + kind, copies, 3, *shape)
        buf("z_" + kind, copies, 3, *quarter(shape))
        buf("p_" + kind, copies, *quarter(shape))
        buf("h_" + kind, copies, *quarter(shape))
    named["send"] = pltpu.SemaphoreType.DMA((SEMS,))
    named["recv"] = pltpu.SemaphoreType.DMA((SEMS,))
    named["local"] = pltpu.SemaphoreType.DMA((48,))
    named["credit"] = pltpu.SemaphoreType.REGULAR((2,))
    return named


SEMS = 320
INPUTS = ("tokens", "cotangent", "lengths", "gain_one", "gain_two", "wq", "wk", "wv", "wo", "wg", "wu", "wd")
OUTPUTS = ("out_act", "out_grad", "f_m", "f_o", "f_q", "f_kv", "hq", "hk", "hv", "ho", "hm")


class Refs:
    pass


def step_kernel(*refs):
    R = Refs()
    names = INPUTS + OUTPUTS + tuple(scratch_shapes())
    for name, ref in zip(names, refs, strict=True):
        setattr(R, name, ref)
    x_hi, z, core, y, x_lo = coords()
    sems = (R.send, R.recv)
    slots = Slots()
    local_slots = Slots()
    sibling = device(x_hi, z, 1 - core, y, x_lo)
    near = [device(x_hi, z, core, y, 1 - x_lo), device(1 - x_hi, z, core, y, 1 - x_lo)]
    far = device(1 - x_hi, z, core, y, x_lo)

    def along_y(k):
        return device(x_hi, z, core, (y + k) % 4, x_lo)

    def along_z(k):
        return device(x_hi, (z + k) % 4, core, y, x_lo)

    def member(k, e):
        return device(x_hi, z, core, (y + k) % 4, (x_lo + e) % 2)

    barrier = pltpu.get_barrier_semaphore()
    everyone = [member(k, e) for k in range(4) for e in range(2) if k + e]
    everyone += [along_z(k) for k in (1, 2, 3)] + [near[1], far, sibling]
    for target in everyone:
        pl.semaphore_signal(barrier, inc=1, device_id=target, device_id_type=MESH)
    pl.semaphore_wait(barrier, len(everyone))
    home = core == x_lo
    guest = jnp.logical_not(home)

    def keep(src, dst):
        return pltpu.make_async_copy(src, dst, R.local.at[local_slots.take()])

    slab_weights = [
        (R.wq, (R.aq, R.hq), 0),
        (R.wk, (R.ak, R.hk), 1),
        (R.wv, (R.av, R.hv), 1),
        (R.wo, (R.ao, R.ho), None),
    ]
    own_copy, ring, cross, swap = {}, {}, {}, {}
    for l in range(LAYERS):
        for a, (src, (here, there), side) in enumerate(slab_weights):
            dst = here if l == 0 else there.at[1]
            own_copy[l, a] = keep(src.at[l], dst.at[y, core])
            for k in (1, 2, 3):
                ring[l, a, k] = remote(src.at[l], dst.at[y, core], sems, slots.take(), along_y(k))
            for k in range(4):
                at = dst.at[(y - k + 4) % 4, core]
                to = near[(k % 2) if side is None else side]
                cross[l, a, k] = remote(src.at[l] if k == 0 else at, at, sems, slots.take(), to)
                swap[l, a, k] = remote(at, at, sems, slots.take(), sibling)
    QKV, OUT, ALL = (0, 1, 2), (3,), (0, 1, 2, 3)

    def gather_begin(l, arrays):
        @pl.when(home)
        def _():
            for a in arrays:
                for k in ORDER_Y:
                    ring[l, a, k].start()
                cross[l, a, 0].start()
                own_copy[l, a].start()

    def gather_home(l, arrays):
        @pl.when(home)
        def _():
            for a in arrays:
                own_copy[l, a].wait()
                swap[l, a, 0].start()
            for k in ORDER_Y:
                for a in arrays:
                    ring[l, a, k].wait_recv()
                    cross[l, a, k].start()
                    swap[l, a, k].start()

    def gather_guest(l, arrays):
        @pl.when(guest)
        def _():
            for k in (0,) + ORDER_Y:
                for a in arrays:
                    cross[l, a, k].wait_recv()
                    swap[l, a, k].start()

    def gather_end(l, arrays):
        for a in arrays:
            for k in range(4):
                swap[l, a, k].wait_recv()

    def gather_sent(l, arrays):
        for a in arrays:

            @pl.when(home)
            def _():
                for k in (1, 2, 3):
                    ring[l, a, k].wait_send()
                for k in range(4):
                    cross[l, a, k].wait_send()

            for k in range(4):
                swap[l, a, k].wait_send()

    saves = [keep(here, there.at[0]) for _, (here, there), _ in slab_weights]
    loads = {
        (l, a): keep(there.at[l], here)
        for l in range(LAYERS)
        for a, (_, (here, there), _) in enumerate(slab_weights)
    }
    save_m = keep(R.mw, R.hm.at[0])
    load_m = [keep(R.hm.at[l], R.mw) for l in range(LAYERS)]

    own_gain = R.all_gains.at[y, x_lo]
    gain_keep = keep(R.own_gains, own_gain)
    gain_send = [
        remote(R.own_gains, own_gain, sems, slots.take(), member(k, e))
        for k in range(4)
        for e in range(2)
        if k + e
    ]

    SIZES = ((0, 48), (48, 32))
    mlp_in = [R.wg, R.wu, R.wd]
    cross_m, ring_m, pass_m, keep_m = {}, {}, {}, {}
    slot_cross = {(l, a): slots.take() for l in range(LAYERS) for a in range(3)}
    slot_ring = {(l, k): slots.take() for l in range(LAYERS) for k in (1, 2, 3)}
    slot_pass = {(l, k): slots.take() for l in range(LAYERS) for k in range(4)}
    for l in range(LAYERS):
        dst = R.mw if l == 0 else R.hm.at[1]
        for a in range(3):
            keep_m[l, a] = keep(mlp_in[a].at[l], dst.at[x_lo, a])
        for c, (first, size) in enumerate(SIZES):

            def rows(where):
                return pl.ds(pl.multiple_of(where * (FFS // 4) + first, 16), size)

            for a in range(3):
                cross_m[l, c, a] = remote(
                    mlp_in[a].at[l, rows(z)], dst.at[x_lo, a, rows(z)], sems, slot_cross[l, a], near[c]
                )
            for k in range(4):
                at = dst.at[1 - x_lo, :, rows((z - k + 4) % 4)]
                pass_m[l, c, k] = remote(at, at, sems, slot_pass[l, k], sibling)
            for k in (1, 2, 3):
                at = dst.at[1 - x_lo, :, rows(z)]
                ring_m[l, c, k] = remote(at, at, sems, slot_ring[l, k], along_z(k))

    def by_core(body):
        for c in range(2):

            @pl.when(core == c)
            def _():
                body(c)

    def pairs_begin(l):
        def body(c):
            for a in range(3):
                cross_m[l, c, a].start()

        by_core(body)
        for a in range(3):
            keep_m[l, a].start()

    def pairs_z(l):
        def body(c):
            for a in range(3):
                cross_m[l, c, a].wait_recv()
            for k in ORDER_Y:
                ring_m[l, c, k].start()
            pass_m[l, c, 0].start()

        by_core(body)

    def pairs_pass(l):
        def body(c):
            for k in ORDER_Y:
                ring_m[l, c, k].wait_recv()
                pass_m[l, c, k].start()

        by_core(body)

    def pairs_end(l):
        def body(c):
            for k in range(4):
                pass_m[l, 1 - c, k].wait_recv()

        by_core(body)
        for a in range(3):
            keep_m[l, a].wait()

    def pairs_sent(l):
        def body(c):
            for a in range(3):
                cross_m[l, c, a].wait_send()
            for k in (1, 2, 3):
                ring_m[l, c, k].wait_send()
            for k in range(4):
                pass_m[l, c, k].wait_send()

        by_core(body)

    spread_at = [slots.take(4) for _ in range(4)]
    back_at = [slots.take(4) for _ in range(4)]

    def spread_copy(n, buffer, k):
        return remote(buffer.at[y], buffer.at[y], sems, spread_at[n] + k, along_y(k))

    def spread(n, buffer):
        for k in ORDER_Y:
            spread_copy(n, buffer, k).start()

    def arrived(n, buffer, k):
        there = buffer.at[(y - k + 4) % 4]
        remote(there, there, sems, spread_at[n] + k, along_y(k)).wait_recv()

    def back_copy(n, k):
        return remote(
            R.parts.at[n % 2, k - 1], R.came.at[n % 2, k - 1], sems, back_at[n] + k, along_y(4 - k)
        )

    def collect(n, total):
        for k in ORDER_Y:
            back_copy(n, k).wait_recv()
            total = total + R.came[n % 2, k - 1].astype(F32)
        return total

    def sent(n, buffer):
        for k in (1, 2, 3):
            spread_copy(n, buffer, k).wait_send()
            back_copy(n, k).wait_send()

    reds = {}

    class Reduction:
        def __init__(self, kind, l):
            self.kind, self.l = kind, l
            shape, self.spread = KINDS[kind]
            self.planes, self.rows = shape[0], shape[1]
            self.b = b = l if kind in TWICE else 0
            self.g = getattr(R, "g_" + kind)
            self.s = getattr(R, "s_" + kind).at[b]
            self.x = getattr(R, "x_" + kind).at[b]
            self.zb = getattr(R, "z_" + kind).at[b]
            self.p = getattr(R, "p_" + kind).at[b]
            self.h = getattr(R, "h_" + kind).at[b]
            self.f = getattr(R, "f_" + kind).at[l]
            self.chunk = {128: 64, 320: 80}[self.rows]
            n = 4 if self.spread else 1
            self.at_pair = slots.take(n)
            self.at_x = slots.take(4 if self.spread else 2)
            self.at_y = slots.take(4)
            self.at_z = slots.take(4)
            self.at_out = slots.take(4)
            self.at_far = slots.take()
            self.at_last = slots.take()
            self.own = pltpu.make_async_copy(self.p, self.piece(self.f, z), R.local.at[local_slots.take()])
            if self.spread:
                self.yb = getattr(R, "y_" + kind).at[b]

        def piece(self, ref, where):
            size = self.rows // 4
            return ref.at[:, pl.ds(pl.multiple_of(where * size, 16), size)]

        def add(self, dst, others, chunk=None):
            for i in range(self.planes):
                accumulate(dst.at[i], [o.at[i] for o in others], chunk or self.chunk)

        def pair(self, q):
            if self.spread:
                return remote(self.g.at[q, 1 - core], self.s.at[q], sems, self.at_pair + q, sibling)
            return remote(self.g.at[1 - core], self.s, sems, self.at_pair, sibling)

        def over_x(self, q):
            if self.spread:
                return remote(self.s.at[q], self.x.at[q], sems, self.at_x + q, near[q // 2])
            half = slice(q * (self.rows // 2), (q + 1) * (self.rows // 2))
            return remote(self.s.at[:, half], self.x.at[:, half], sems, self.at_x + q, near[q])

        def came_x(self, q):
            return remote(self.s.at[q], self.x.at[q], sems, self.at_x + q, near[0])

        def over_y(self, k):
            return remote(self.s.at[(y + k) % 4], self.yb.at[k - 1], sems, self.at_y + k, along_y(k))

        def mine(self):
            return self.s.at[y] if self.spread else self.s

        def over_z(self, k):
            return remote(
                self.piece(self.mine(), (z + k) % 4), self.zb.at[k - 1], sems, self.at_z + k, along_z(k)
            )

        def over_far(self):
            return remote(self.p, self.h, sems, self.at_far, far)

        def out_z(self, k):
            return remote(self.p, self.piece(self.f, z), sems, self.at_out + k, along_z(k))

        def last(self):
            return remote(self.f, self.f, sems, self.at_last, sibling)

        def begin(self):
            for q in (0, 2, 1, 3) if self.spread else (0,):
                self.pair(q).start()

        def step_x(self):
            for q in (0, 2, 1, 3) if self.spread else (0,):
                self.pair(q).wait()
                if self.spread:
                    self.add(self.s.at[q], [self.g.at[q, core]])
                    self.when_guest(lambda: self.over_x(q).start())
                else:
                    self.add(self.s, [self.g.at[core]])
                    self.when_guest(lambda: [self.over_x(i).start() for i in range(2)])

        def step_y(self):
            @pl.when(home)
            def _():
                if self.spread:
                    for k in ORDER_Y + (0,):
                        q = (y + k) % 4
                        self.came_x(q).wait_recv()
                        self.add(self.s.at[q], [self.x.at[q]])
                        if k:
                            self.over_y(k).start()
                else:
                    for q in range(2):
                        self.over_x(q).wait_recv()
                    self.add(self.s, [self.x])
                    for k in ORDER_Y:
                        self.over_z(k).start()

        def step_z(self):
            if self.spread:

                @pl.when(home)
                def _():
                    for k in ORDER_Y:
                        self.over_y(k).wait_recv()
                    self.add(self.mine(), [self.yb.at[j] for j in range(3)])
                    for k in ORDER_Y:
                        self.over_z(k).start()

        def step_far(self):
            @pl.when(home)
            def _():
                for k in ORDER_Y:
                    self.over_z(k).wait_recv()
                for i in range(self.planes):
                    total = self.piece(self.mine(), z)[i].astype(F32)
                    for j in range(3):
                        total = total + self.zb[j, i].astype(F32)
                    self.p[i] = total.astype(BF)
                self.over_far().start()

        def step_out(self):
            @pl.when(home)
            def _():
                self.over_far().wait()
                self.add(self.p, [self.h], self.rows // 4)
                self.own.start()
                for k in ORDER_Y:
                    self.out_z(k).start()

        def step_last(self):
            @pl.when(home)
            def _():
                self.own.wait()
                for k in ORDER_Y:
                    self.out_z(k).wait_recv()
                self.last().start()

        def end(self):
            @pl.when(home)
            def _():
                for k in (1, 2, 3):
                    if self.spread:
                        self.over_y(k).wait_send()
                    self.over_z(k).wait_send()
                    self.out_z(k).wait_send()

            @pl.when(guest)
            def _():
                for q in range(4 if self.spread else 2):
                    self.over_x(q).wait_send()

        def finish(self):
            @pl.when(home)
            def _():
                self.last().wait_send()

            @pl.when(guest)
            def _():
                self.last().wait_recv()

        def when_guest(self, body):
            @pl.when(guest)
            def _():
                body()

    for l in (1, 0):
        for kind in KINDS:
            reds[kind, l] = Reduction(kind, l)

    partners = {
        "m": [sibling, near[0], near[1], far] + [along_z(k) for k in (1, 2, 3)],
        "o": [sibling, near[0], near[1], far]
        + [along_z(k) for k in (1, 2, 3)]
        + [along_y(k) for k in (1, 2, 3)],
    }

    def give_credit(kind):
        for target in partners[kind]:
            pl.semaphore_signal(
                R.credit.at[int(kind == "o")], inc=1, device_id=target, device_id_type=MESH
            )

    def take_credit(kind):
        pl.semaphore_wait(R.credit.at[int(kind == "o")], len(partners[kind]))

    column = lax.broadcasted_iota(jnp.int32, (ROWS, PAD), 1)
    first_half = column % HEAD < HEAD // 2

    def turn(block, sign):
        ahead = pltpu.roll(block, PAD - HEAD // 2, 1)
        behind = pltpu.roll(block, HEAD // 2, 1)
        return jnp.where(first_half, -sign * ahead, sign * behind)

    def rotated(block):
        return block * R.cosine[...] + turn(block, 1.0) * R.sine[...]

    def rotated_back(block):
        return block * R.cosine[...] + turn(block * R.sine[...], -1.0)

    def inverse_rms(x):
        return lax.rsqrt(jnp.mean(x * x, axis=-1, keepdims=True) + norm_eps)

    def head_lanes(h):
        return slice(h * HEAD, (h + 1) * HEAD)

    def tables():
        one, two = R.lengths[0, 0], R.lengths[0, 1]
        row = lax.broadcasted_iota(jnp.int32, (ROWS, PAD), 0)

        def doc(t):
            return (t >= one).astype(jnp.int32) + (t >= one + two).astype(jnp.int32)

        own = doc(row)
        begins = jnp.where(own == 0, 0, jnp.where(own == 1, one, one + two))
        allowed = jnp.logical_and(own == doc(column), column <= row)
        R.bias[...] = jnp.where(allowed, 0.0, masked_value)
        slow = jnp.exp((column % (HEAD // 2)).astype(F32) * (-2.0 * log_base / HEAD))
        angles = (row - begins).astype(F32) * slow
        R.cosine[...] = jnp.cos(angles)
        R.sine[...] = jnp.sin(angles)
        wide_column = lax.broadcasted_iota(jnp.int32, (D, 8 * PAD), 1)
        wide_row = lax.broadcasted_iota(jnp.int32, (D, 8 * PAD), 0)
        lane = wide_column % PAD
        R.place[...] = jnp.where(
            jnp.logical_and(lane < SHARD, (wide_column // PAD) * SHARD + lane == wide_row), 1.0, 0.0
        ).astype(BF)
        R.wide[...] = jnp.zeros_like(R.wide)
        R.narrow[...] = jnp.zeros_like(R.narrow)
        R.stream[0] = R.tokens[...].astype(F32).T

    def soft_weights(l, kv):
        rows = jnp.concatenate([R.qrot[l, :, head_lanes(kv * SHARE + i)] for i in range(SHARE)], axis=0)
        keys = R.krot[l, :, head_lanes(kv)]
        scores = dot_t(rows, keys) * score_scale
        scores = scores + jnp.concatenate([R.bias[...]] * SHARE, axis=0)
        weights = jnp.exp(scores - jnp.max(scores, axis=-1, keepdims=True))
        return rows, keys, weights / jnp.sum(weights, axis=-1, keepdims=True)

    def attention_forward(l, ready_qkv, ready_out):
        x = R.stream[l]
        normed = (x * inverse_rms(x) * R.gain_full[l : l + 1, :]).astype(BF)
        R.npad[l] = dot(normed, R.place[...]).astype(BF)

        def project(weights, width, product):
            total = jnp.zeros((ROWS, width), F32)
            for g in range(8):
                total = total + product(
                    R.npad[l, :, g * PAD : g * PAD + SHARD], weights[g // 2, g % 2]
                )
            return total

        ready_qkv()
        R.wide[:, :D] = project(R.aq, D, dot)
        R.narrow[:, :KV] = project(R.ak, KV, dot_t)
        R.vals[l, :, :KV] = project(R.av, KV, dot_t).astype(BF)
        for j in range(8):
            at = slice(j * PAD, (j + 1) * PAD)
            R.qrot[l, :, at] = rotated(R.wide[:, at]).astype(BF)
        for j in range(3):
            at = slice(j * PAD, (j + 1) * PAD)
            R.krot[l, :, at] = rotated(R.narrow[:, at]).astype(BF)
        for kv in range(KV_HEADS):
            rows, keys, soft = soft_weights(l, kv)
            out = dot(soft.astype(BF), R.vals[l, :, head_lanes(kv)]).astype(BF)
            for i in range(SHARE):
                R.gproj_q[:, head_lanes(kv * SHARE + i)] = out[i * ROWS : (i + 1) * ROWS]
        R.mpad[l] = dot(R.gproj_q[:, :D], R.place[...]).astype(BF)
        ready_out()
        total = x
        for g in range(8):
            total = total + dot(R.mpad[l, :, g * PAD : g * PAD + SHARD], R.ao[g // 2, g % 2])
        R.hidden[l] = total
        R.acts_in[l, y] = (total * inverse_rms(total) * R.gain_full[2 + l : 3 + l, :]).astype(BF)

    def blocks(n, buffer, body):
        def block(i, carry):
            k = order(i)
            b = (y - k + 4) % 4

            @pl.when(i > 0)
            def _():
                arrived(n, buffer, k)

            total = body(b)

            @pl.when(i == 0)
            def _():
                R.own_part[...] = total

            @pl.when(i > 0)
            def _():
                R.parts[n % 2, k - 1] = total.astype(BF)
                back_copy(n, k).start()

            return carry

        lax.fori_loop(0, 4, block, 0)

    def mlp_forward(l, n):
        def body(b):
            rows = R.acts_in[l, b]
            total = jnp.zeros((ROWS, D), F32)
            for p in range(2):
                gate = dot_t(rows, R.mw[p, 0])
                up = dot_t(rows, R.mw[p, 1])
                act = (gate * jax.nn.sigmoid(gate) * up).astype(BF)
                R.s_gate[l, p, b] = gate.astype(BF)
                R.s_up[l, p, b] = up.astype(BF)
                R.s_act[l, p, b] = act
                total = total + dot(act, R.mw[p, 2])
            return total

        blocks(n, R.acts_in.at[l], body)

    def mlp_backward(l, n):
        def body(b):
            rows = R.grads_in[1 - l, b]
            total = jnp.zeros((ROWS, D), F32)
            for p in range(2):
                grad_active = dot_t(rows, R.mw[p, 2])
                gate = R.s_gate[l, p, b].astype(F32)
                up = R.s_up[l, p, b].astype(F32)
                sig = jax.nn.sigmoid(gate)
                grad_gate = (grad_active * up * sig * (1.0 + gate * (1.0 - sig))).astype(BF)
                grad_up = (grad_active * gate * sig).astype(BF)
                R.s_gate[l, p, b] = grad_gate
                R.s_up[l, p, b] = grad_up
                total = total + dot(grad_gate, R.mw[p, 0]) + dot(grad_up, R.mw[p, 1])
            return total

        blocks(n, R.grads_in.at[1 - l], body)

    def mlp_grads(l):
        def grads(p, carry):
            ins = R.acts_in[l].reshape(4 * ROWS, D)
            R.g_m[p, 0] = t_dot(R.s_gate[l, p].reshape(4 * ROWS, FFS), ins).astype(BF)
            R.g_m[p, 1] = t_dot(R.s_up[l, p].reshape(4 * ROWS, FFS), ins).astype(BF)
            R.g_m[p, 2] = t_dot(
                R.s_act[l, p].reshape(4 * ROWS, FFS), R.grads_in[1 - l].reshape(4 * ROWS, D)
            ).astype(BF)
            return carry

        lax.fori_loop(0, 2, grads, 0)

    def slab_loop(body):
        def run(g, carry):
            body(g, g // 2, g % 2)
            return carry

        lax.fori_loop(0, 8, run, 0)

    def norm_back(x, grad_normed, gain_row):
        r = inverse_rms(x)
        u = grad_normed * gain_row
        back = r * u - x * (r * r * r) * jnp.mean(u * x, axis=-1, keepdims=True)
        return back, jnp.sum(grad_normed * x * r, axis=0, keepdims=True)

    def set_gain_grad(row_of, grad_gain):
        row = lax.broadcasted_iota(jnp.int32, (16, D), 0)
        high, low = halves(jnp.where(row == row_of, grad_gain, 0.0))
        return dot(high, R.place[...]) + dot(low, R.place[...])

    def back_hidden(l, n):
        grad_input = collect(n, R.own_part[...])
        back, grad_gain = norm_back(R.hidden[l], grad_input, R.gain_full[2 + l : 3 + l, :])
        grad_hidden = R.grad[...] + back
        R.grad[...] = grad_hidden
        R.glow[...] = grad_hidden.astype(BF)
        R.gain_grad[...] = set_gain_grad(1, grad_gain)

        def back_out(g, h, i):
            R.wide[:, lanes(g, SHARD)] = dot_t(R.glow[...], R.ao[h, i])

        slab_loop(back_out)
        R.gmix[...] = dot_t(R.wide[...].astype(BF), R.place[...]).astype(BF)

    def grads_out(l):
        def body(g, h, i):
            R.g_o[h, i, 0] = t_dot(R.mpad[l, :, lanes(g, PAD)], R.glow[...]).astype(BF)

        slab_loop(body)

    def back_heads(l):
        for kv in range(KV_HEADS):
            rows, keys, soft = soft_weights(l, kv)
            heads = [kv * SHARE + i for i in range(SHARE)]
            gm = jnp.concatenate([R.gmix[:, head_lanes(h)] for h in heads], axis=0)
            grad_probs = dot_t(gm, R.vals[l, :, head_lanes(kv)])
            inner = jnp.sum(soft * grad_probs, axis=-1, keepdims=True)
            grad_scores = (soft * (grad_probs - inner)).astype(BF)
            grad_rows = dot(grad_scores, keys) * score_scale
            for i, h in enumerate(heads):
                R.wide[:, head_lanes(h)] = grad_rows[i * ROWS : (i + 1) * ROWS]
            R.narrow[:, head_lanes(kv)] = t_dot(grad_scores, rows) * score_scale
            R.gproj_v[:, head_lanes(kv)] = t_dot(soft.astype(BF), gm).astype(BF)
        for j in range(8):
            at = slice(j * PAD, (j + 1) * PAD)
            R.gproj_q[:, at] = rotated_back(R.wide[:, at]).astype(BF)
        for j in range(3):
            at = slice(j * PAD, (j + 1) * PAD)
            R.gproj_k[:, at] = rotated_back(R.narrow[:, at]).astype(BF)

    def back_stream(l):
        def back_in(g, h, i):
            R.wide[:, lanes(g, SHARD)] = (
                dot_t(R.gproj_q[:, :D], R.aq[h, i])
                + dot(R.gproj_k[:, :KV], R.ak[h, i])
                + dot(R.gproj_v[:, :KV], R.av[h, i])
            )

        slab_loop(back_in)
        high, low = halves(R.wide[...])
        grad_normed = dot_t(high, R.place[...]) + dot_t(low, R.place[...])
        back, grad_gain = norm_back(R.stream[l], grad_normed, R.gain_full[l : l + 1, :])
        R.grad[...] = R.grad[...] + back
        R.gain_grad[...] = R.gain_grad[...] + set_gain_grad(0, grad_gain)

    def grads_kv(l):
        def body(g, h, i):
            right = R.npad[l, :, lanes(g, PAD)]
            R.g_kv[h, i, 0] = t_dot(R.gproj_k[:, :KV], right).astype(BF)
            R.g_kv[h, i, 1] = t_dot(R.gproj_v[:, :KV], right).astype(BF)

        slab_loop(body)

    def grads_q(l):
        def body(g, h, i):
            total = t_dot(R.npad[l, :, lanes(g, PAD)], R.gproj_q[:, :D])
            rows = lax.broadcasted_iota(jnp.int32, (PAD, PAD), 0)
            corner = (
                total[:, :PAD]
                + jnp.where(rows == SHARD, R.gain_grad[0:1, lanes(g, PAD)], 0.0)
                + jnp.where(rows == SHARD + 1, R.gain_grad[1:2, lanes(g, PAD)], 0.0)
            )
            R.g_q[h, i, 0] = total.astype(BF)
            R.g_q[h, i, 0, :, :PAD] = corner.astype(BF)

        slab_loop(body)

    def start_all(copies):
        for copy in copies:
            copy.start()

    def wait_all(copies):
        for copy in copies:
            copy.wait()

    gather_begin(0, QKV)
    R.own_gains[...] = jnp.zeros_like(R.own_gains)
    R.own_gains[0:2, :SHARD] = R.gain_one[...]
    R.own_gains[2:4, :SHARD] = R.gain_two[...]
    gain_keep.start()
    start_all(gain_send)
    gather_home(0, QKV)
    gather_begin(0, OUT)
    pairs_begin(0)
    tables()
    gather_guest(0, QKV)
    gather_home(0, OUT)
    pairs_z(0)
    gain_keep.wait()
    wait_all(gain_send)
    for g in range(8):
        R.gain_pad[:, g * PAD : (g + 1) * PAD] = R.all_gains[g // 2, g % 2]
    R.gain_full[...] = dot_t(R.gain_pad[...], R.place[...])
    gather_guest(0, OUT)
    gather_begin(1, ALL)
    pairs_begin(1)

    def ready_out():
        gather_end(0, OUT)
        start_all(saves)

    attention_forward(0, lambda: gather_end(0, QKV), ready_out)
    spread(0, R.acts_in.at[0])
    pairs_pass(0)
    gather_home(1, ALL)
    pairs_z(1)
    pairs_end(0)
    save_m.start()
    mlp_forward(0, 0)
    gather_guest(1, ALL)
    gather_sent(0, ALL)
    wait_all(saves)
    pairs_pass(1)
    cot = R.cotangent[...].astype(F32).T
    R.grads_in[0, y] = cot.astype(BF)
    R.grad[...] = cot
    gather_end(1, ALL)
    start_all([loads[1, a] for a in ALL])
    R.stream[1] = collect(0, R.own_part[...] + R.hidden[0])
    spread(2, R.grads_in.at[0])
    pairs_sent(0)
    save_m.wait()
    pairs_end(1)
    load_m[1].start()
    attention_forward(
        1,
        lambda: wait_all([loads[1, a] for a in QKV]),
        lambda: wait_all([loads[1, a] for a in OUT]),
    )
    spread(1, R.acts_in.at[1])
    sent(0, R.acts_in.at[0])
    load_m[1].wait()
    mlp_forward(1, 1)
    R.wide[:, :D] = R.own_part[...] + R.hidden[1]

    m1, o1, q1, kv1 = (reds[kind, 1] for kind in ("m", "o", "q", "kv"))
    m0, o0, q0, kv0 = (reds[kind, 0] for kind in ("m", "o", "q", "kv"))
    mlp_backward(1, 2)
    load_m[0].start()
    mlp_grads(1)
    m1.begin()
    R.out_act[...] = collect(1, R.wide[:, :D]).T.astype(BF)
    back_hidden(1, 2)
    m1.step_x()
    grads_out(1)
    o1.begin()
    back_heads(1)
    m1.step_y()
    o1.step_x()
    back_stream(1)
    R.grads_in[1, y] = R.grad[...].astype(BF)
    spread(3, R.grads_in.at[1])
    start_all([loads[0, a] for a in ALL])
    grads_kv(1)
    kv1.begin()
    grads_q(1)
    q1.begin()
    m1.step_far()
    o1.step_y()
    sent(1, R.acts_in.at[1])
    load_m[0].wait()
    mlp_backward(0, 3)
    kv1.step_x()
    q1.step_x()
    m1.step_out()
    o1.step_z()
    mlp_grads(0)
    kv1.step_y()
    q1.step_y()
    o1.step_far()
    m1.step_last()
    m1.end()
    give_credit("m")
    take_credit("m")
    m0.begin()
    wait_all([loads[0, a] for a in ALL])
    back_hidden(0, 3)
    m0.step_x()
    kv1.step_z()
    q1.step_z()
    o1.step_out()
    grads_out(0)
    back_heads(0)
    o1.step_last()
    o1.end()
    give_credit("o")
    m0.step_y()
    kv1.step_far()
    q1.step_far()
    grads_kv(0)
    kv0.begin()
    take_credit("o")
    o0.begin()
    back_stream(0)
    grads_q(0)
    q0.begin()
    R.out_grad[...] = R.grad[...].T
    kv0.step_x()
    o0.step_x()
    q0.step_x()
    kv1.step_out()
    q1.step_out()
    m0.step_far()
    kv0.step_y()
    o0.step_y()
    q0.step_y()
    kv1.step_last()
    q1.step_last()
    m0.step_out()
    kv0.step_z()
    o0.step_z()
    q0.step_z()
    kv0.step_far()
    o0.step_far()
    q0.step_far()
    m0.step_last()
    kv0.step_out()
    o0.step_out()
    q0.step_out()
    kv0.step_last()
    o0.step_last()
    q0.step_last()
    for red in (kv1, q1, m0, kv0, o0, q0):
        red.end()
    for red in (m1, o1, kv1, q1, m0, kv0, o0, q0):
        red.finish()
    sent(2, R.grads_in.at[0])
    sent(3, R.grads_in.at[1])
    gather_sent(1, ALL)
    pairs_sent(1)


def step(*args):
    L = LAYERS

    def out(*shape, dtype=BF):
        return jax.ShapeDtypeStruct(shape, dtype)

    return pl.pallas_call(
        step_kernel,
        out_shape=(
            out(D, ROWS),
            out(D, ROWS, dtype=F32),
            out(L, 3, FFS, D),
            out(L, 1, ROWS, D),
            out(L, 1, ROWS, D),
            out(L, 2, KV, PAD),
            out(L, 4, 2, SHARD, D),
            out(L, 4, 2, KV, SHARD),
            out(L, 4, 2, KV, SHARD),
            out(L, 4, 2, SHARD, D),
            out(L, 2, 3, FFS, D),
        ),
        in_specs=[VMEM] * 2 + [SMEM] + [VMEM] * 2 + [ANY] * 7,
        out_specs=[VMEM] * 2 + [ANY] * 9,
        scratch_shapes=list(scratch_shapes().values()),
        compiler_params=pltpu.CompilerParams(
            collective_id=1, has_side_effects=True, vmem_limit_bytes=63 * 2**20
        ),
    )(*args)


def shards(
    tokens, cotangent, lengths, gain_attn, w_query, w_key, w_value, w_out, gain_mlp, w_gate, w_up, w_down
):
    def turned(a):
        return jnp.swapaxes(a, -1, -2)

    act, grad, fm, fo, fq, fkv, *_ = step(
        turned(tokens), turned(cotangent), lengths, gain_attn, gain_mlp,
        w_query, turned(w_key), turned(w_value), w_out, turned(w_gate), turned(w_up), w_down,
    )
    return (
        turned(act),
        turned(grad),
        fq[:, 0, SHARD, :SHARD].astype(F32),
        fq[:, 0, :SHARD].astype(F32),
        turned(fkv[:, 0, :, :SHARD].astype(F32)),
        turned(fkv[:, 1, :, :SHARD].astype(F32)),
        fo[:, 0, :SHARD].astype(F32),
        fq[:, 0, SHARD + 1, :SHARD].astype(F32),
        turned(fm[:, 0].astype(F32)),
        turned(fm[:, 1].astype(F32)),
        fm[:, 2].astype(F32),
    )


def solution(mesh):
    in_specs = (
        P(("replica", "group"), None),
        P(("replica", "group"), None),
        P(("replica", "group"), None),
        P(None, "group"),
        P(None, "group", None),
        P(None, "group", None),
        P(None, "group", None),
        P(None, "group", None),
        P(None, "group"),
        P(None, None, "group"),
        P(None, None, "group"),
        P(None, "group", None),
    )
    out_specs = (
        P(("replica", "group"), None),
        P(("replica", "group"), None),
        P(None, "group"),
        P(None, "group", None),
        P(None, "group", None),
        P(None, "group", None),
        P(None, "group", None),
        P(None, "group"),
        P(None, None, "group"),
        P(None, None, "group"),
        P(None, "group", None),
    )
    return jax.shard_map(shards, mesh=mesh, in_specs=in_specs, out_specs=out_specs, check_vma=False)
```

```python
import jax
import jax.numpy as jnp
from jax import lax
from jax.experimental import pallas as pl
from jax.experimental.pallas import tpu as pltpu
from jax.sharding import PartitionSpec as P

Q_HEADS = 15
KV_HEADS = 5
HEAD = 64
LAYERS = 2
D = 960
SHARD = 120
PAD = 128
FFS = 320
ROWS = 128
KV = KV_HEADS * HEAD
SHARE = Q_HEADS // KV_HEADS

norm_eps = 1e-05
rope_base = 100000.0
log_base = 11.512925464970229
score_scale = 0.125
masked_value = -1e30
MESH = pl.DeviceIdType.MESH
BF = jnp.bfloat16
F32 = jnp.float32
ANY = pl.BlockSpec(memory_space=pl.ANY)
VMEM = pl.BlockSpec(memory_space=pltpu.VMEM)
SMEM = pl.BlockSpec(memory_space=pltpu.SMEM)


def coords():
    r = lax.axis_index("replica")
    g = lax.axis_index("group")
    return r // 8, (r // 2) % 4, r % 2, g // 2, g % 2


def device(x_hi, z, core, y, x_lo):
    return ((x_hi * 4 + z) * 2 + core, y * 2 + x_lo)


def remote(src, dst, sems, index, target):
    return pltpu.make_async_remote_copy(
        src_ref=src,
        dst_ref=dst,
        send_sem=sems[0].at[index],
        recv_sem=sems[1].at[index],
        device_id=target,
        device_id_type=MESH,
    )


def dot(a, b):
    return lax.dot_general(a, b, (((1,), (0,)), ((), ())), preferred_element_type=F32)


def dot_t(a, b):
    return lax.dot_general(a, b, (((1,), (1,)), ((), ())), preferred_element_type=F32)


def t_dot(a, b):
    return lax.dot_general(a, b, (((0,), (0,)), ((), ())), preferred_element_type=F32)


def lanes(g, width):
    return pl.ds(pl.multiple_of(g * PAD, PAD), width)


def halves(a):
    high = a.astype(BF)
    return high, (a - high.astype(F32)).astype(BF)


def accumulate(dst, others, chunk):
    def body(i, carry):
        at = pl.ds(pl.multiple_of(i * chunk, chunk), chunk)
        total = dst[at, :].astype(F32)
        for other in others:
            total = total + other[at, :].astype(F32)
        dst[at, :] = total.astype(dst.dtype)
        return carry

    lax.fori_loop(0, dst.shape[0] // chunk, body, 0)


class Slots:
    def __init__(self):
        self.used = 0

    def take(self, count=1):
        self.used += count
        return self.used - count


def order(k):
    return k + (k // 2) * (5 - 2 * k)


KINDS = {
    "m": ((3, FFS, D), False),
    "o": ((1, ROWS, D), True),
    "q": ((1, ROWS, D), True),
    "kv": ((2, KV, PAD), True),
}
TWICE = ("q", "kv")
SUMS_TWICE = ("o", "q", "kv")
ORDER_Y = (1, 3, 2)


def quarter(shape):
    return (shape[0], shape[1] // 4, shape[2])


def scratch_shapes():
    L = LAYERS
    named = {}

    def buf(name, *shape, dtype=BF):
        named[name] = pltpu.VMEM(shape, dtype)

    buf("aq", 4, 2, SHARD, D)
    buf("ao", 4, 2, SHARD, D)
    buf("ak", 4, 2, KV, SHARD)
    buf("av", 4, 2, KV, SHARD)
    buf("mw", 2, 3, FFS, D)
    buf("all_gains", 4, 2, 16, PAD)
    buf("own_gains", 16, PAD)
    buf("place", D, 8 * PAD)
    buf("cosine", ROWS, PAD, dtype=F32)
    buf("sine", ROWS, PAD, dtype=F32)
    buf("bias", ROWS, ROWS, dtype=F32)
    buf("gain_full", 16, D, dtype=F32)
    buf("gain_pad", 16, 8 * PAD)
    buf("gain_grad", 16, 8 * PAD, dtype=F32)
    buf("gain_rows", 16, D, dtype=F32)
    buf("stream", L, ROWS, D, dtype=F32)
    buf("hidden", L, ROWS, D, dtype=F32)
    buf("grad", ROWS, D, dtype=F32)
    buf("wide", ROWS, 8 * PAD, dtype=F32)
    buf("narrow", ROWS, 3 * PAD, dtype=F32)
    buf("own_part", ROWS, D, dtype=F32)
    buf("npad", L, ROWS, 8 * PAD)
    buf("mpad", L, ROWS, 8 * PAD)
    buf("qrot", L, ROWS, 8 * PAD)
    buf("krot", L, ROWS, 3 * PAD)
    buf("vals", L, ROWS, 3 * PAD)
    buf("gproj_q", ROWS, 8 * PAD)
    buf("gproj_k", ROWS, 3 * PAD)
    buf("gproj_v", ROWS, 3 * PAD)
    buf("gmix", ROWS, D)
    buf("glow", ROWS, D)
    buf("acts_in", L, 4, ROWS, D)
    buf("grads_in", 2, 4, ROWS, D)
    buf("parts", 2, 3, ROWS, D)
    buf("came", 2, 3, ROWS, D)
    buf("s_gate", L, 2, 4, ROWS, FFS)
    buf("s_up", L, 2, 4, ROWS, FFS)
    buf("s_act", L, 2, 4, ROWS, FFS)
    for kind, (shape, spread) in KINDS.items():
        four = (4,) if spread else ()
        copies = L if kind in TWICE else 1
        if kind != "o":
            buf("g_" + kind, *four, 2, *shape)
        buf("s_" + kind, L if kind in SUMS_TWICE else 1, *four, *shape)
        buf("x_" + kind, copies, *four, *shape)
        if spread:
            buf("y_" + kind, copies, 3, *shape)
        buf("z_" + kind, copies, 3, *quarter(shape))
        buf("p_" + kind, copies, *quarter(shape))
        buf("h_" + kind, copies, *quarter(shape))
    named["send"] = pltpu.SemaphoreType.DMA((SEMS,))
    named["recv"] = pltpu.SemaphoreType.DMA((SEMS,))
    named["local"] = pltpu.SemaphoreType.DMA((LOCAL_SEMS,))
    named["credit"] = pltpu.SemaphoreType.REGULAR((8,))
    return named


SEMS = 266
LOCAL_SEMS = 53
INPUTS = ("tokens", "cotangent", "lengths", "gain_one", "gain_two", "wq", "wk", "wv", "wo", "wg", "wu", "wd")
OUTPUTS = ("out_act", "out_grad", "f_m", "f_o", "f_q", "f_kv", "hq", "hk", "hv", "ho", "hm")


class Refs:
    pass


def step_kernel(*refs):
    R = Refs()
    names = INPUTS + OUTPUTS + tuple(scratch_shapes())
    for name, ref in zip(names, refs, strict=True):
        setattr(R, name, ref)
    x_hi, z, core, y, x_lo = coords()
    sems = (R.send, R.recv)
    slots = Slots()
    local_slots = Slots()
    spread_at = [slots.take(4) for _ in range(4)]
    back_at = [slots.take(4) for _ in range(4)]
    kept_slots = slots.used
    sibling = device(x_hi, z, 1 - core, y, x_lo)
    near = [device(x_hi, z, core, y, 1 - x_lo), device(1 - x_hi, z, core, y, 1 - x_lo)]
    far = device(1 - x_hi, z, core, y, x_lo)

    def along_y(k):
        return device(x_hi, z, core, (y + k) % 4, x_lo)

    def along_z(k):
        return device(x_hi, (z + k) % 4, core, y, x_lo)

    barrier = pltpu.get_barrier_semaphore()
    everyone = [along_y(k) for k in (1, 2, 3)] + [along_z(k) for k in (1, 2, 3)]
    everyone += near + [far, sibling]
    for target in everyone:
        pl.semaphore_signal(barrier, inc=1, device_id=target, device_id_type=MESH)
    pl.semaphore_wait(barrier, len(everyone))
    home = core == x_lo
    guest = jnp.logical_not(home)

    def keep(src, dst):
        return pltpu.make_async_copy(src, dst, R.local.at[local_slots.take()])

    def start_all(copies):
        for copy in copies:
            copy.start()

    def wait_all(copies):
        for copy in copies:
            copy.wait()

    slab_weights = [
        (R.wq, (R.aq, R.hq), 0),
        (R.wk, (R.ak, R.hk), 1),
        (R.wv, (R.av, R.hv), 1),
        (R.wo, (R.ao, R.ho), None),
    ]
    own_copy, ring, cross, swap, first_swap = {}, {}, {}, {}, {}
    for l in range(LAYERS):
        for a, (src, (here, there), side) in enumerate(slab_weights):
            dst = here if l == 0 else there.at[1]
            if l == 0:
                own_copy[a] = keep(src.at[l], dst.at[y, core])
            for k in (1, 2, 3):
                ring[l, a, k] = remote(src.at[l], dst.at[y, core], sems, slots.take(), along_y(k))
            for k in range(4):
                at = dst.at[(y - k + 4) % 4, core]
                to = near[(0, 0, 1, 1)[k] if side is None else 1 if side == 0 and k == 2 else side]
                cross[l, a, k] = remote(src.at[l] if k == 0 else at, at, sems, slots.take(), to)
                slot = slots.take()
                swap[l, a, k] = remote(at, at, sems, slot, sibling)
                if k == 0:
                    first_swap[l, a] = remote(src.at[l], at, sems, slot, sibling)
    QKV, OUT, ALL = (0, 1, 2), (3,), (0, 1, 2, 3)
    PLANES = (((0, 1), (3, 1)), ((0, 2), (3, 2)), ((0, 3), (3, 3)), tuple((a, k) for a in (1, 2) for k in (1, 2, 3)))
    ring_z = {}
    for units in PLANES:
        for a, k in units:
            at = slab_weights[a][1][1].at[1, (y - k + 4) % 4, core]
            for m in (1, 2, 3):
                ring_z[a, k, m] = remote(at, at, sems, slots.take(), along_z(m))

    def by_plane(body):
        for plane in range(4):

            @pl.when(jnp.logical_and(home, z == plane))
            def _():
                body(plane)

    def planes_begin():
        @pl.when(home)
        def _():
            for a in ALL:
                cross[1, a, 0].start()
                first_swap[1, a].start()

        def body(plane):
            for a, k in PLANES[plane]:
                ring[1, a, k].start()

        by_plane(body)

    def planes_z():
        def body(plane):
            for a, k in PLANES[plane]:
                ring[1, a, k].wait_recv()
                for m in (1, 3, 2):
                    ring_z[a, k, m].start()
                cross[1, a, k].start()
                swap[1, a, k].start()

        by_plane(body)

    def planes_pass():
        def body(plane):
            for other in (3, 0, 1, 2):
                if other != plane:
                    for a, k in PLANES[other]:
                        ring_z[a, k, (plane - other) % 4].wait_recv()
                        cross[1, a, k].start()
                        swap[1, a, k].start()

        by_plane(body)

    def planes_sent():
        def body(plane):
            for a, k in PLANES[plane]:
                ring[1, a, k].wait_send()
                for m in (1, 2, 3):
                    ring_z[a, k, m].wait_send()

        by_plane(body)

    def gather_begin(l, arrays):
        @pl.when(home)
        def _():
            for a in arrays:
                for k in ORDER_Y:
                    ring[l, a, k].start()
                cross[l, a, 0].start()
                first_swap[l, a].start()
                if l == 0:
                    own_copy[a].start()

    def gather_home(l, arrays):
        @pl.when(home)
        def _():
            for k in ORDER_Y:
                for a in arrays:
                    ring[l, a, k].wait_recv()
                    cross[l, a, k].start()
                    swap[l, a, k].start()

    def gather_guest(l, arrays):
        @pl.when(guest)
        def _():
            for k in (0,) + ORDER_Y:
                for a in arrays:
                    cross[l, a, k].wait_recv()
                    swap[l, a, k].start()

    def gather_end(l, arrays):
        for a in arrays:
            for k in range(4):
                swap[l, a, k].wait_recv()
        if l == 0:

            @pl.when(home)
            def _():
                for a in arrays:
                    own_copy[a].wait()

    def gather_sent(l, arrays):
        for a in arrays:

            @pl.when(home)
            def _():
                if l == 0:
                    for k in (1, 2, 3):
                        ring[l, a, k].wait_send()
                for k in range(4):
                    cross[l, a, k].wait_send()

            for k in range(4):
                swap[l, a, k].wait_send()

    saves = [keep(here, there.at[0]) for _, (here, there), _ in slab_weights]
    load_back = [keep(there.at[0], here) for _, (here, there), _ in slab_weights]
    load_own, load_core, load_rest = [], [], []
    for src, (here, there), _ in slab_weights:
        slot = local_slots.take()
        at = here.at[y, core]
        load_own.append(pltpu.make_async_copy(src.at[1], at, R.local.at[slot]))
        load_core.append(pltpu.make_async_copy(there.at[1, y, core], at, R.local.at[slot]))
        rest = [keep(there.at[1, y, 1 - core], here.at[y, 1 - core])]
        for k in (1, 2, 3):
            rest.append(keep(there.at[1, (y + k) % 4], here.at[(y + k) % 4]))
        load_rest.append(rest)

    def load_begin(arrays):
        for a in arrays:
            start_all(load_rest[a])

        @pl.when(home)
        def _():
            start_all([load_own[a] for a in arrays])

        @pl.when(guest)
        def _():
            start_all([load_core[a] for a in arrays])

    def load_end(arrays):
        for a in arrays:
            wait_all(load_rest[a])
            load_own[a].wait()

    mlp_in = [R.wg, R.wu, R.wd]
    save_m = keep(R.mw.at[1 - x_lo], R.hm.at[0])
    load_m = [
        [keep(R.hm.at[l], R.mw.at[1 - x_lo])]
        + [keep(mlp_in[a].at[l], R.mw.at[x_lo, a]) for a in range(3)]
        for l in range(LAYERS)
    ]

    own_gain, other_gain = R.all_gains.at[y, x_lo], R.all_gains.at[y, 1 - x_lo]
    gain_keep = keep(R.own_gains, own_gain)
    gain_x = remote(R.own_gains, own_gain, sems, slots.take(), near[0])
    gain_y = [remote(R.own_gains, own_gain, sems, slots.take(), along_y(k)) for k in (1, 2, 3)]
    gain_pass = [remote(other_gain, other_gain, sems, slots.take(), along_y(k)) for k in (1, 2, 3)]

    SIZES = ((0, 48), (48, 32))
    cross_m, ring_m, pass_m, keep_m = {}, {}, {}, {}
    slot_cross = {(l, a): slots.take() for l in range(LAYERS) for a in range(3)}
    slot_ring = {(l, k): slots.take() for l in range(LAYERS) for k in (1, 2, 3)}
    slot_pass = {(l, k): slots.take() for l in range(LAYERS) for k in range(4)}
    for l in range(LAYERS):
        there_m = R.mw.at[x_lo] if l == 0 else R.hm.at[1]
        here_m = R.mw.at[1 - x_lo] if l == 0 else R.hm.at[1]
        if l == 0:
            for a in range(3):
                keep_m[a] = keep(mlp_in[a].at[l], R.mw.at[x_lo, a])
        for c, (first, size) in enumerate(SIZES):

            def rows(where):
                return pl.ds(pl.multiple_of(where * (FFS // 4) + first, 16), size)

            for a in range(3):
                cross_m[l, c, a] = remote(
                    mlp_in[a].at[l, rows(z)], there_m.at[a, rows(z)], sems, slot_cross[l, a], near[c]
                )
            for k in range(4):
                at = here_m.at[:, rows((z - k + 4) % 4)]
                pass_m[l, c, k] = remote(at, at, sems, slot_pass[l, k], sibling)
            for k in (1, 2, 3):
                at = here_m.at[:, rows(z)]
                ring_m[l, c, k] = remote(at, at, sems, slot_ring[l, k], along_z(k))

    def by_core(body):
        for c in range(2):

            @pl.when(core == c)
            def _():
                body(c)

    def pairs_begin(l):
        def body(c):
            for a in range(3):
                cross_m[l, c, a].start()

        by_core(body)
        if l == 0:
            start_all(keep_m.values())

    def pairs_z(l):
        def body(c):
            for a in range(3):
                cross_m[l, c, a].wait_recv()
            for k in ORDER_Y:
                ring_m[l, c, k].start()
            pass_m[l, c, 0].start()

        by_core(body)

    def pairs_pass(l):
        def body(c):
            for k in ORDER_Y:
                ring_m[l, c, k].wait_recv()
                pass_m[l, c, k].start()

        by_core(body)

    def pairs_end(l):
        def body(c):
            for k in range(4):
                pass_m[l, 1 - c, k].wait_recv()

        by_core(body)
        if l == 0:
            wait_all(keep_m.values())

    def pairs_sent(l):
        def body(c):
            for a in range(3):
                cross_m[l, c, a].wait_send()
            for k in (1, 2, 3):
                ring_m[l, c, k].wait_send()
            for k in range(4):
                pass_m[l, c, k].wait_send()

        by_core(body)


    def spread_copy(n, buffer, k):
        return remote(buffer.at[y], buffer.at[y], sems, spread_at[n] + k, along_y(k))

    def spread(n, buffer, targets=ORDER_Y):
        for k in targets:
            spread_copy(n, buffer, k).start()

    def arrived(n, buffer, k):
        there = buffer.at[(y - k + 4) % 4]
        remote(there, there, sems, spread_at[n] + k, along_y(k)).wait_recv()

    def back_copy(n, k):
        return remote(
            R.parts.at[int(n == 1), k - 1], R.came.at[int(n == 1), k - 1], sems, back_at[n] + k, along_y(4 - k)
        )

    def collect(n, total):
        for k in ORDER_Y:
            back_copy(n, k).wait_recv()
            total = total + R.came[int(n == 1), k - 1].astype(F32)
        return total

    def back(n):
        for k in ORDER_Y:
            back_copy(n, k).start()

    def sent(n, buffer):
        for k in (1, 2, 3):
            spread_copy(n, buffer, k).wait_send()

    def sent_back(n):
        for k in (1, 2, 3):
            back_copy(n, k).wait_send()

    reds = {}
    credit_at = {"m": 0, "o": 4}

    def give(kind, which, targets):
        for target in targets:
            pl.semaphore_signal(
                R.credit.at[credit_at[kind] + which], inc=1, device_id=target, device_id_type=MESH
            )

    def take(kind, which, count):
        pl.semaphore_wait(R.credit.at[credit_at[kind] + which], count)

    class Reduction:
        def __init__(self, kind, l):
            self.kind, self.l = kind, l
            shape, self.spread = KINDS[kind]
            self.planes, self.rows = shape[0], shape[1]
            self.b = b = l if kind in TWICE else 0
            self.gives = kind in credit_at and l == 1
            self.takes = kind in credit_at and l == 0
            self.g = R.g_q if kind == "o" else getattr(R, "g_" + kind)
            self.s = getattr(R, "s_" + kind).at[l if kind in SUMS_TWICE else 0]
            self.x = getattr(R, "x_" + kind).at[b]
            self.zb = getattr(R, "z_" + kind).at[b]
            self.p = getattr(R, "p_" + kind).at[b]
            self.h = getattr(R, "h_" + kind).at[b]
            self.f = getattr(R, "f_" + kind).at[l]
            self.chunk = {128: 64, 320: 80}[self.rows]
            n = 4 if self.spread else 1
            self.at_pair = slots.take(n)
            self.at_x = slots.take(4 if self.spread else 2)
            self.at_y = slots.take(4)
            self.at_z = slots.take(4)
            self.at_out = slots.take(4)
            self.at_far = slots.take()
            self.at_last = slots.take()
            self.own = pltpu.make_async_copy(self.p, self.piece(self.f, z), R.local.at[local_slots.take()])
            if self.spread:
                self.yb = getattr(R, "y_" + kind).at[b]

        def piece(self, ref, where):
            size = self.rows // 4
            return ref.at[:, pl.ds(pl.multiple_of(where * size, 16), size)]

        def add(self, dst, others, chunk=None):
            for i in range(self.planes):
                accumulate(dst.at[i], [o.at[i] for o in others], chunk or self.chunk)

        def pair(self, q):
            if self.spread:
                return remote(self.g.at[q, 1 - core], self.s.at[q], sems, self.at_pair + q, sibling)
            return remote(self.g.at[1 - core], self.s, sems, self.at_pair, sibling)

        def over_x(self, q):
            if self.spread:
                return remote(self.s.at[q], self.x.at[q], sems, self.at_x + q, near[q // 2])
            half = slice(q * (self.rows // 2), (q + 1) * (self.rows // 2))
            return remote(self.s.at[:, half], self.x.at[:, half], sems, self.at_x + q, near[q])

        def came_x(self, q):
            return remote(self.s.at[q], self.x.at[q], sems, self.at_x + q, near[0])

        def over_y(self, k):
            return remote(self.s.at[(y + k) % 4], self.yb.at[k - 1], sems, self.at_y + k, along_y(k))

        def mine(self):
            return self.s.at[y] if self.spread else self.s

        def over_z(self, k):
            return remote(
                self.piece(self.mine(), (z + k) % 4), self.zb.at[k - 1], sems, self.at_z + k, along_z(k)
            )

        def over_far(self):
            return remote(self.p, self.h, sems, self.at_far, far)

        def out_z(self, k):
            return remote(self.p, self.piece(self.f, z), sems, self.at_out + k, along_z(k))

        def last(self):
            return remote(self.f, self.f, sems, self.at_last, sibling)

        def begin(self):
            if self.takes and self.kind == "m":
                take(self.kind, 0, 1)
            for q in (0, 2, 1, 3) if self.spread else (0,):
                self.pair(q).start()

        def step_x(self):
            if self.takes:
                self.when_guest(lambda: take(self.kind, 1, 2))
            for q in (0, 2, 1, 3) if self.spread else (0,):
                self.pair(q).wait()
                if self.spread:
                    self.add(self.s.at[q], [self.g.at[q, core]])
                    self.when_guest(lambda: self.over_x(q).start())
                else:
                    self.add(self.s, [self.g.at[core]])
                    self.when_guest(lambda: [self.over_x(i).start() for i in range(2)])

        def step_y(self):
            @pl.when(home)
            def _():
                if self.spread:
                    if self.takes:
                        take(self.kind, 0, 3)
                    for k in ORDER_Y + (0,):
                        q = (y + k) % 4
                        self.came_x(q).wait_recv()
                        self.add(self.s.at[q], [self.x.at[q]])
                        if k:
                            self.over_y(k).start()
                else:
                    for q in range(2):
                        self.over_x(q).wait_recv()
                    self.add(self.s, [self.x])
                    self.start_z()
                if self.gives:
                    give(self.kind, 1, near)

        def start_z(self):
            if self.takes:
                take(self.kind, 2, 3)
            for k in ORDER_Y:
                self.over_z(k).start()

        def step_z(self):
            if self.spread:

                @pl.when(home)
                def _():
                    for k in ORDER_Y:
                        self.over_y(k).wait_recv()
                    self.add(self.mine(), [self.yb.at[j] for j in range(3)])
                    if self.gives:
                        give(self.kind, 0, [along_y(k) for k in (1, 2, 3)])
                    self.start_z()

        def step_far(self):
            @pl.when(home)
            def _():
                for k in ORDER_Y:
                    self.over_z(k).wait_recv()
                for i in range(self.planes):
                    total = self.piece(self.mine(), z)[i].astype(F32)
                    for j in range(3):
                        total = total + self.zb[j, i].astype(F32)
                    self.p[i] = total.astype(BF)
                if self.takes:
                    take(self.kind, 3, 1)
                self.over_far().start()
                for k in (1, 2, 3):
                    self.over_z(k).wait_send()
                    if self.spread:
                        self.over_y(k).wait_send()
                if self.gives:
                    give(self.kind, 2, [along_z(k) for k in (1, 2, 3)])

            @pl.when(guest)
            def _():
                for q in range(4 if self.spread else 2):
                    self.over_x(q).wait_send()

            if self.gives and self.kind == "m":
                give(self.kind, 0, [sibling])

        def step_out(self):
            @pl.when(home)
            def _():
                self.over_far().wait()
                self.add(self.p, [self.h], self.rows // 4)
                self.own.start()
                for k in ORDER_Y:
                    self.out_z(k).start()
                if self.gives:
                    give(self.kind, 3, [far])

        def step_last(self):
            @pl.when(home)
            def _():
                self.own.wait()
                for k in ORDER_Y:
                    self.out_z(k).wait()
                self.last().start()

        def finish(self):
            @pl.when(home)
            def _():
                self.last().wait_send()

            @pl.when(guest)
            def _():
                self.last().wait_recv()

        def when_guest(self, body):
            @pl.when(guest)
            def _():
                body()

    first_slots = slots
    for l in (1, 0):
        if l == 0:
            slots = Slots()
            slots.take(kept_slots)
        for kind in KINDS:
            reds[kind, l] = Reduction(kind, l)

    assert max(slots.used, first_slots.used) <= SEMS and local_slots.used <= LOCAL_SEMS

    column = lax.broadcasted_iota(jnp.int32, (ROWS, PAD), 1)
    first_half = column % HEAD < HEAD // 2

    def turn(block, sign):
        ahead = pltpu.roll(block, PAD - HEAD // 2, 1)
        behind = pltpu.roll(block, HEAD // 2, 1)
        return jnp.where(first_half, -sign * ahead, sign * behind)

    def rotated(block):
        return block * R.cosine[...] + turn(block, 1.0) * R.sine[...]

    def rotated_back(block):
        return block * R.cosine[...] + turn(block * R.sine[...], -1.0)

    def inverse_rms(x):
        return lax.rsqrt(jnp.mean(x * x, axis=-1, keepdims=True) + norm_eps)

    def head_lanes(h):
        return slice(h * HEAD, (h + 1) * HEAD)

    def tables():
        one, two = R.lengths[0, 0], R.lengths[0, 1]
        row = lax.broadcasted_iota(jnp.int32, (ROWS, PAD), 0)

        def doc(t):
            return (t >= one).astype(jnp.int32) + (t >= one + two).astype(jnp.int32)

        own = doc(row)
        begins = jnp.where(own == 0, 0, jnp.where(own == 1, one, one + two))
        allowed = jnp.logical_and(own == doc(column), column <= row)
        R.bias[...] = jnp.where(allowed, 0.0, masked_value)
        slow = jnp.exp((column % (HEAD // 2)).astype(F32) * (-2.0 * log_base / HEAD))
        angles = (row - begins).astype(F32) * slow
        R.cosine[...] = jnp.cos(angles)
        R.sine[...] = jnp.sin(angles)
        wide_column = lax.broadcasted_iota(jnp.int32, (D, 8 * PAD), 1)
        wide_row = lax.broadcasted_iota(jnp.int32, (D, 8 * PAD), 0)
        lane = wide_column % PAD
        R.place[...] = jnp.where(
            jnp.logical_and(lane < SHARD, (wide_column // PAD) * SHARD + lane == wide_row), 1.0, 0.0
        ).astype(BF)
        R.wide[...] = jnp.zeros_like(R.wide)
        R.narrow[...] = jnp.zeros_like(R.narrow)
        R.gain_rows[...] = jnp.zeros_like(R.gain_rows)
        R.stream[0] = R.tokens[...].astype(F32).T

    def soft_weights(l, kv):
        rows = jnp.concatenate([R.qrot[l, :, head_lanes(kv * SHARE + i)] for i in range(SHARE)], axis=0)
        keys = R.krot[l, :, head_lanes(kv)]
        scores = dot_t(rows, keys) * score_scale
        scores = scores + jnp.concatenate([R.bias[...]] * SHARE, axis=0)
        weights = jnp.exp(scores - jnp.max(scores, axis=-1, keepdims=True))
        return rows, keys, weights / jnp.sum(weights, axis=-1, keepdims=True)

    def attention_forward(l, ready_qkv, ready_out):
        x = R.stream[l]
        normed = (x * inverse_rms(x) * R.gain_full[l : l + 1, :]).astype(BF)
        R.npad[l] = dot(normed, R.place[...]).astype(BF)

        def project(weights, width, product):
            total = jnp.zeros((ROWS, width), F32)
            for g in range(8):
                total = total + product(
                    R.npad[l, :, g * PAD : g * PAD + SHARD], weights[g // 2, g % 2]
                )
            return total

        ready_qkv()
        R.wide[:, :D] = project(R.aq, D, dot)
        R.narrow[:, :KV] = project(R.ak, KV, dot_t)
        R.vals[l, :, :KV] = project(R.av, KV, dot_t).astype(BF)
        for j in range(8):
            at = slice(j * PAD, (j + 1) * PAD)
            R.qrot[l, :, at] = rotated(R.wide[:, at]).astype(BF)
        for j in range(3):
            at = slice(j * PAD, (j + 1) * PAD)
            R.krot[l, :, at] = rotated(R.narrow[:, at]).astype(BF)
        for kv in range(KV_HEADS):
            rows, keys, soft = soft_weights(l, kv)
            out = dot(soft.astype(BF), R.vals[l, :, head_lanes(kv)]).astype(BF)
            for i in range(SHARE):
                R.gproj_q[:, head_lanes(kv * SHARE + i)] = out[i * ROWS : (i + 1) * ROWS]
        R.mpad[l] = dot(R.gproj_q[:, :D], R.place[...]).astype(BF)
        ready_out()
        total = x
        for g in range(8):
            total = total + dot(R.mpad[l, :, g * PAD : g * PAD + SHARD], R.ao[g // 2, g % 2])
        R.hidden[l] = total
        R.acts_in[l, y] = (total * inverse_rms(total) * R.gain_full[2 + l : 3 + l, :]).astype(BF)

    def blocks(n, buffer, body, between=None):
        def block(i, carry):
            k = order(i)
            b = (y - k + 4) % 4
            if between is not None:
                pl.when(i == 1)(between)

            @pl.when(i > 0)
            def _():
                arrived(n, buffer, k)

            total = body(b)
            if total is None:
                return carry

            @pl.when(i == 0)
            def _():
                R.own_part[...] = total

            @pl.when(i > 0)
            def _():
                R.parts[int(n == 1), k - 1] = total.astype(BF)
                back_copy(n, k).start()

            return carry

        lax.fori_loop(0, 4, block, 0)

    def mlp_forward(l, n, down=True, between=None):
        def body(b):
            rows = R.acts_in[l, b]
            total = jnp.zeros((ROWS, D), F32) if down else None
            for p in range(2):
                gate = dot_t(rows, R.mw[p, 0])
                up = dot_t(rows, R.mw[p, 1])
                act = (gate * jax.nn.sigmoid(gate) * up).astype(BF)
                R.s_gate[l, p, b] = gate.astype(BF)
                R.s_up[l, p, b] = up.astype(BF)
                R.s_act[l, p, b] = act
                if down:
                    total = total + dot(act, R.mw[p, 2])
            return total

        blocks(n, R.acts_in.at[l], body, between)

    def mlp_down(l, n):
        def block(i, carry):
            k = order(i)
            b = (y - k + 4) % 4
            total = dot(R.s_act[l, 0, b], R.mw[0, 2]) + dot(R.s_act[l, 1, b], R.mw[1, 2])

            @pl.when(i == 0)
            def _():
                R.out_grad[...] = (total + R.hidden[l]).T

            @pl.when(i > 0)
            def _():
                R.parts[int(n == 1), k - 1] = total.astype(BF)

            return carry

        lax.fori_loop(0, 4, block, 0)

    def result_out(n):
        R.out_act[...] = (R.out_grad[...] + collect(n, jnp.zeros((ROWS, D), F32)).T).astype(BF)

    def mlp_backward(l, n):
        def body(b):
            rows = R.grads_in[1 - l, b]
            total = jnp.zeros((ROWS, D), F32)
            for p in range(2):
                grad_active = dot_t(rows, R.mw[p, 2])
                gate = R.s_gate[l, p, b].astype(F32)
                up = R.s_up[l, p, b].astype(F32)
                sig = jax.nn.sigmoid(gate)
                grad_gate = (grad_active * up * sig * (1.0 + gate * (1.0 - sig))).astype(BF)
                grad_up = (grad_active * gate * sig).astype(BF)
                R.s_gate[l, p, b] = grad_gate
                R.s_up[l, p, b] = grad_up
                total = total + dot(grad_gate, R.mw[p, 0]) + dot(grad_up, R.mw[p, 1])
            return total

        blocks(n, R.grads_in.at[1 - l], body)

    def mlp_grads(l):
        def grads(p, carry):
            ins = R.acts_in[l].reshape(4 * ROWS, D)
            R.g_m[p, 0] = t_dot(R.s_gate[l, p].reshape(4 * ROWS, FFS), ins).astype(BF)
            R.g_m[p, 1] = t_dot(R.s_up[l, p].reshape(4 * ROWS, FFS), ins).astype(BF)
            R.g_m[p, 2] = t_dot(
                R.s_act[l, p].reshape(4 * ROWS, FFS), R.grads_in[1 - l].reshape(4 * ROWS, D)
            ).astype(BF)
            return carry

        lax.fori_loop(0, 2, grads, 0)

    def slab_loop(body):
        def run(g, carry):
            body(g, g // 2, g % 2)
            return carry

        lax.fori_loop(0, 8, run, 0)

    def norm_back(x, grad_normed, gain_row):
        r = inverse_rms(x)
        u = grad_normed * gain_row
        back = r * u - x * (r * r * r) * jnp.mean(u * x, axis=-1, keepdims=True)
        return back, jnp.sum(grad_normed * x * r, axis=0, keepdims=True)

    def back_hidden(l, n):
        grad_input = collect(n, R.own_part[...])
        back, grad_gain = norm_back(R.hidden[l], grad_input, R.gain_full[2 + l : 3 + l, :])
        grad_hidden = R.grad[...] + back
        R.grad[...] = grad_hidden
        R.glow[...] = grad_hidden.astype(BF)
        R.gain_rows[1:2, :] = grad_gain

        def back_out(g, h, i):
            R.wide[:, lanes(g, SHARD)] = dot_t(R.glow[...], R.ao[h, i])

        slab_loop(back_out)
        R.gmix[...] = dot_t(R.wide[...].astype(BF), R.place[...]).astype(BF)

    def grads_out(l):
        def body(g, h, i):
            R.g_q[h, i, 0] = t_dot(R.mpad[l, :, lanes(g, PAD)], R.glow[...]).astype(BF)

        slab_loop(body)

    def back_heads(l):
        for kv in range(KV_HEADS):
            rows, keys, soft = soft_weights(l, kv)
            heads = [kv * SHARE + i for i in range(SHARE)]
            gm = jnp.concatenate([R.gmix[:, head_lanes(h)] for h in heads], axis=0)
            grad_probs = dot_t(gm, R.vals[l, :, head_lanes(kv)])
            inner = jnp.sum(soft * grad_probs, axis=-1, keepdims=True)
            grad_scores = (soft * (grad_probs - inner)).astype(BF)
            grad_rows = dot(grad_scores, keys) * score_scale
            for i, h in enumerate(heads):
                R.wide[:, head_lanes(h)] = grad_rows[i * ROWS : (i + 1) * ROWS]
            R.narrow[:, head_lanes(kv)] = t_dot(grad_scores, rows) * score_scale
            R.gproj_v[:, head_lanes(kv)] = t_dot(soft.astype(BF), gm).astype(BF)
        for j in range(8):
            at = slice(j * PAD, (j + 1) * PAD)
            R.gproj_q[:, at] = rotated_back(R.wide[:, at]).astype(BF)
        for j in range(3):
            at = slice(j * PAD, (j + 1) * PAD)
            R.gproj_k[:, at] = rotated_back(R.narrow[:, at]).astype(BF)

    def back_stream(l):
        def back_in(g, h, i):
            R.wide[:, lanes(g, SHARD)] = (
                dot_t(R.gproj_q[:, :D], R.aq[h, i])
                + dot(R.gproj_k[:, :KV], R.ak[h, i])
                + dot(R.gproj_v[:, :KV], R.av[h, i])
            )

        slab_loop(back_in)
        high, low = halves(R.wide[...])
        grad_normed = dot_t(high, R.place[...]) + dot_t(low, R.place[...])
        back, grad_gain = norm_back(R.stream[l], grad_normed, R.gain_full[l : l + 1, :])
        R.grad[...] = R.grad[...] + back
        R.gain_rows[0:1, :] = grad_gain

    def grads_kv(l):
        def body(g, h, i):
            right = R.npad[l, :, lanes(g, PAD)]
            R.g_kv[h, i, 0] = t_dot(R.gproj_k[:, :KV], right).astype(BF)
            R.g_kv[h, i, 1] = t_dot(R.gproj_v[:, :KV], right).astype(BF)

        slab_loop(body)

    def grads_q(l):
        high, low = halves(R.gain_rows[...])
        R.gain_grad[...] = dot(high, R.place[...]) + dot(low, R.place[...])

        def body(g, h, i):
            total = t_dot(R.npad[l, :, lanes(g, PAD)], R.gproj_q[:, :D])
            rows = lax.broadcasted_iota(jnp.int32, (PAD, PAD), 0)
            corner = (
                total[:, :PAD]
                + jnp.where(rows == SHARD, R.gain_grad[0:1, lanes(g, PAD)], 0.0)
                + jnp.where(rows == SHARD + 1, R.gain_grad[1:2, lanes(g, PAD)], 0.0)
            )
            R.g_q[h, i, 0] = total.astype(BF)
            R.g_q[h, i, 0, :, :PAD] = corner.astype(BF)

        slab_loop(body)

    gather_begin(0, QKV)
    R.own_gains[...] = jnp.zeros_like(R.own_gains)
    R.own_gains[0:2, :SHARD] = R.gain_one[...]
    R.own_gains[2:4, :SHARD] = R.gain_two[...]
    gain_keep.start()
    gain_x.start()
    start_all(gain_y)
    pairs_begin(0)
    gather_home(0, QKV)
    gather_begin(0, OUT)
    planes_begin()
    tables()
    gain_x.wait()
    start_all(gain_pass)
    gather_guest(0, QKV)
    pairs_z(0)
    gather_home(0, OUT)
    gain_keep.wait()
    wait_all(gain_y)
    wait_all(gain_pass)
    for g in range(8):
        R.gain_pad[:, g * PAD : (g + 1) * PAD] = R.all_gains[g // 2, g % 2]
    R.gain_full[...] = dot_t(R.gain_pad[...], R.place[...])
    gather_guest(0, OUT)
    pairs_begin(1)

    def ready_out():
        gather_end(0, OUT)
        pairs_pass(0)
        planes_z()
        start_all(saves)

    attention_forward(0, lambda: gather_end(0, QKV), ready_out)
    spread(0, R.acts_in.at[0])
    pairs_end(0)
    save_m.start()

    def between():
        planes_pass()
        pairs_z(1)

    mlp_forward(0, 0, between=between)
    gather_guest(1, QKV)
    gather_sent(0, ALL)
    wait_all(saves)
    pairs_pass(1)
    cot = R.cotangent[...].astype(F32).T
    R.grads_in[0, y] = cot.astype(BF)
    R.grad[...] = cot
    gather_end(1, QKV)
    load_begin(QKV)
    R.stream[1] = collect(0, R.own_part[...] + R.hidden[0])
    spread(2, R.grads_in.at[0], (1, 3))
    pairs_sent(0)
    save_m.wait()
    gather_guest(1, OUT)

    def ready_out_1():
        gather_end(1, OUT)
        load_begin(OUT)
        pairs_end(1)
        start_all(load_m[1])
        load_end(OUT)

    attention_forward(1, lambda: load_end(QKV), ready_out_1)
    spread(1, R.acts_in.at[1])
    spread(2, R.grads_in.at[0], (2,))
    sent(0, R.acts_in.at[0])
    sent_back(0)
    wait_all(load_m[1])
    mlp_forward(1, 1, down=False)

    m1, o1, q1, kv1 = (reds[kind, 1] for kind in ("m", "o", "q", "kv"))
    m0, o0, q0, kv0 = (reds[kind, 0] for kind in ("m", "o", "q", "kv"))
    mlp_backward(1, 2)
    mlp_grads(1)
    gather_sent(1, ALL)
    planes_sent()
    pairs_sent(1)
    m1.begin()
    mlp_down(1, 1)
    start_all(load_m[0])
    back_hidden(1, 2)
    back(1)
    m1.step_x()
    back_heads(1)
    back_stream(1)
    R.grads_in[1, y] = R.grad[...].astype(BF)
    spread(3, R.grads_in.at[1])
    start_all(load_back)
    grads_out(1)
    o1.begin()
    grads_kv(1)
    kv1.begin()
    result_out(1)
    o1.step_x()
    grads_q(1)
    q1.begin()
    m1.step_y()
    sent(1, R.acts_in.at[1])
    sent_back(2)
    wait_all(load_m[0])
    mlp_backward(0, 3)
    kv1.step_x()
    q1.step_x()
    m1.step_far()
    mlp_grads(0)
    m0.begin()
    o1.step_y()
    wait_all(load_back)
    back_hidden(0, 3)
    m0.step_x()
    grads_out(0)
    o0.begin()
    kv1.step_y()
    q1.step_y()
    o1.step_z()
    m1.step_out()
    back_heads(0)
    o0.step_x()
    m0.step_y()
    kv1.step_z()
    q1.step_z()
    o1.step_far()
    grads_kv(0)
    kv0.begin()
    m1.step_last()
    back_stream(0)
    kv0.step_x()
    o0.step_y()
    m0.step_far()
    grads_q(0)
    q0.begin()
    R.out_grad[...] = R.grad[...].T
    o1.step_out()
    kv1.step_far()
    q1.step_far()
    q0.step_x()
    m0.step_out()
    kv0.step_y()
    o0.step_z()
    kv1.step_out()
    q1.step_out()
    o1.step_last()
    q0.step_y()
    kv0.step_z()
    o0.step_far()
    q0.step_z()
    kv0.step_far()
    o0.step_out()
    q0.step_far()
    kv0.step_out()
    m0.step_last()
    q0.step_out()
    kv1.step_last()
    q1.step_last()
    o0.step_last()
    kv0.step_last()
    q0.step_last()
    for red in (m1, o1, kv1, q1, m0, kv0, o0, q0):
        red.finish()
    sent(2, R.grads_in.at[0])
    sent(3, R.grads_in.at[1])
    sent_back(1)
    sent_back(3)


def step(*args):
    L = LAYERS

    def out(*shape, dtype=BF):
        return jax.ShapeDtypeStruct(shape, dtype)

    return pl.pallas_call(
        step_kernel,
        out_shape=(
            out(D, ROWS),
            out(D, ROWS, dtype=F32),
            out(L, 3, FFS, D),
            out(L, 1, ROWS, D),
            out(L, 1, ROWS, D),
            out(L, 2, KV, PAD),
            out(L, 4, 2, SHARD, D),
            out(L, 4, 2, KV, SHARD),
            out(L, 4, 2, KV, SHARD),
            out(L, 4, 2, SHARD, D),
            out(L, 3, FFS, D),
        ),
        in_specs=[VMEM] * 2 + [SMEM] + [VMEM] * 2 + [ANY] * 7,
        out_specs=[VMEM] * 2 + [ANY] * 9,
        scratch_shapes=list(scratch_shapes().values()),
        compiler_params=pltpu.CompilerParams(
            collective_id=1, has_side_effects=True, vmem_limit_bytes=63 * 2**20
        ),
    )(*args)


def widen_kernel(fm, fo, fq, fkv, gate, up, down, out, query, key, value, gain_one, gain_two):
    l = pl.program_id(0)
    gate[0] = fm[0, 0].astype(F32)
    up[0] = fm[0, 1].astype(F32)
    down[0] = fm[0, 2].astype(F32)

    @pl.when(pl.program_id(1) == 0)
    def _():
        out[0] = fo[0, 0, :SHARD].astype(F32)
        wide = fq[0, 0].astype(F32)
        query[0] = wide[:SHARD]
        gain_one[pl.ds(l, 1), :] = wide[SHARD : SHARD + 1, :SHARD]
        gain_two[pl.ds(l, 1), :] = wide[SHARD + 1 : SHARD + 2, :SHARD]
        key[0] = fkv[0, 0, :, :SHARD].astype(F32)
        value[0] = fkv[0, 1, :, :SHARD].astype(F32)


def widen(fm, fo, fq, fkv):
    L, parts = LAYERS, 4

    def whole(*shape):
        return pl.BlockSpec((1,) + shape, lambda l, j: (l,) + (0,) * len(shape))

    def out(*shape):
        return jax.ShapeDtypeStruct(shape, F32)

    rows = pl.BlockSpec((1, FFS // parts, D), lambda l, j: (l, j, 0))
    gain = pl.BlockSpec((L, SHARD), lambda l, j: (0, 0))
    return pl.pallas_call(
        widen_kernel,
        grid=(L, parts),
        out_shape=(
            out(L, FFS, D), out(L, FFS, D), out(L, FFS, D), out(L, SHARD, D), out(L, SHARD, D),
            out(L, KV, SHARD), out(L, KV, SHARD), out(L, SHARD), out(L, SHARD),
        ),
        in_specs=[
            pl.BlockSpec((1, 3, FFS // parts, D), lambda l, j: (l, 0, j, 0)),
            whole(1, ROWS, D),
            whole(1, ROWS, D),
            whole(2, KV, PAD),
        ],
        out_specs=[rows, rows, rows, whole(SHARD, D), whole(SHARD, D), whole(KV, SHARD), whole(KV, SHARD), gain, gain],
    )(fm, fo, fq, fkv)


def shards(
    tokens, cotangent, lengths, gain_attn, w_query, w_key, w_value, w_out, gain_mlp, w_gate, w_up, w_down
):
    def turned(a):
        return jnp.swapaxes(a, -1, -2)

    act, grad, fm, fo, fq, fkv, *_ = step(
        turned(tokens), turned(cotangent), lengths, gain_attn, gain_mlp,
        w_query, turned(w_key), turned(w_value), w_out, turned(w_gate), turned(w_up), w_down,
    )
    gate, up, down, out, query, key, value, gain_one, gain_two = widen(fm, fo, fq, fkv)
    return (
        turned(act),
        turned(grad),
        gain_one,
        query,
        turned(key),
        turned(value),
        out,
        gain_two,
        turned(gate),
        turned(up),
        down,
    )


def solution(mesh):
    in_specs = (
        P(("replica", "group"), None),
        P(("replica", "group"), None),
        P(("replica", "group"), None),
        P(None, "group"),
        P(None, "group", None),
        P(None, "group", None),
        P(None, "group", None),
        P(None, "group", None),
        P(None, "group"),
        P(None, None, "group"),
        P(None, None, "group"),
        P(None, "group", None),
    )
    out_specs = (
        P(("replica", "group"), None),
        P(("replica", "group"), None),
        P(None, "group"),
        P(None, "group", None),
        P(None, "group", None),
        P(None, "group", None),
        P(None, "group", None),
        P(None, "group"),
        P(None, None, "group"),
        P(None, None, "group"),
        P(None, "group", None),
    )
    return jax.shard_map(shards, mesh=mesh, in_specs=in_specs, out_specs=out_specs, check_vma=False)
```

```python
import jax
import jax.numpy as jnp
from jax import lax
from jax.experimental import pallas as pl
from jax.experimental.pallas import tpu as pltpu
from jax.sharding import PartitionSpec as P

Q_HEADS = 15
KV_HEADS = 5
HEAD = 64
LAYERS = 2
D = 960
SHARD = 120
PAD = 128
FFS = 320
ROWS = 128
KV = KV_HEADS * HEAD
SHARE = Q_HEADS // KV_HEADS

norm_eps = 1e-05
rope_base = 100000.0
log_base = 11.512925464970229
score_scale = 0.125
masked_value = -1e30
MESH = pl.DeviceIdType.MESH
BF = jnp.bfloat16
F32 = jnp.float32
ANY = pl.BlockSpec(memory_space=pl.ANY)
VMEM = pl.BlockSpec(memory_space=pltpu.VMEM)
SMEM = pl.BlockSpec(memory_space=pltpu.SMEM)


def coords():
    r = lax.axis_index("replica")
    g = lax.axis_index("group")
    return r // 8, (r // 2) % 4, r % 2, g // 2, g % 2


def device(x_hi, z, core, y, x_lo):
    return ((x_hi * 4 + z) * 2 + core, y * 2 + x_lo)


def remote(src, dst, sems, index, target):
    return pltpu.make_async_remote_copy(
        src_ref=src,
        dst_ref=dst,
        send_sem=sems[0].at[index],
        recv_sem=sems[1].at[index],
        device_id=target,
        device_id_type=MESH,
    )


def dot(a, b):
    return lax.dot_general(a, b, (((1,), (0,)), ((), ())), preferred_element_type=F32)


def dot_t(a, b):
    return lax.dot_general(a, b, (((1,), (1,)), ((), ())), preferred_element_type=F32)


def t_dot(a, b):
    return lax.dot_general(a, b, (((0,), (0,)), ((), ())), preferred_element_type=F32)


def lanes(g, width):
    return pl.ds(pl.multiple_of(g * PAD, PAD), width)


def halves(a):
    high = a.astype(BF)
    return high, (a - high.astype(F32)).astype(BF)


def accumulate(dst, others, chunk):
    def body(i, carry):
        at = pl.ds(pl.multiple_of(i * chunk, chunk), chunk)
        total = dst[at, :].astype(F32)
        for other in others:
            total = total + other[at, :].astype(F32)
        dst[at, :] = total.astype(dst.dtype)
        return carry

    lax.fori_loop(0, dst.shape[0] // chunk, body, 0)


class Slots:
    def __init__(self):
        self.used = 0

    def take(self, count=1):
        self.used += count
        return self.used - count


def order(k):
    return k + (k // 2) * (5 - 2 * k)


KINDS = {
    "m": ((3, FFS, D), False),
    "o": ((1, ROWS, D), True),
    "q": ((1, ROWS, D), True),
    "kv": ((2, KV, PAD), True),
}
TWICE = ("q", "kv")
SUMS_TWICE = ("o", "q", "kv")
ORDER_Y = (1, 3, 2)


def quarter(shape):
    return (shape[0], shape[1] // 4, shape[2])


def scratch_shapes():
    L = LAYERS
    named = {}

    def buf(name, *shape, dtype=BF):
        named[name] = pltpu.VMEM(shape, dtype)

    buf("aq", 4, 2, SHARD, D)
    buf("ao", 4, 2, SHARD, D)
    buf("ak", 4, 2, KV, SHARD)
    buf("av", 4, 2, KV, SHARD)
    buf("mw", 2, 3, FFS, D)
    buf("all_gains", 4, 2, 16, PAD)
    buf("own_gains", 16, PAD)
    buf("place", D, 8 * PAD)
    buf("cosine", ROWS, PAD, dtype=F32)
    buf("sine", ROWS, PAD, dtype=F32)
    buf("bias", ROWS, ROWS, dtype=F32)
    buf("gain_full", 16, D, dtype=F32)
    buf("gain_pad", 16, 8 * PAD)
    buf("gain_grad", 16, 8 * PAD, dtype=F32)
    buf("gain_rows", 16, D, dtype=F32)
    buf("stream", L, ROWS, D, dtype=F32)
    buf("hidden", L, ROWS, D, dtype=F32)
    buf("grad", ROWS, D, dtype=F32)
    buf("wide", ROWS, 8 * PAD, dtype=F32)
    buf("narrow", ROWS, 3 * PAD, dtype=F32)
    buf("own_part", ROWS, D, dtype=F32)
    buf("npad", L, ROWS, 8 * PAD)
    buf("mpad", L, ROWS, 8 * PAD)
    buf("qrot", L, ROWS, 8 * PAD)
    buf("krot", L, ROWS, 3 * PAD)
    buf("vals", L, ROWS, 3 * PAD)
    buf("gproj_q", ROWS, 8 * PAD)
    buf("gproj_k", ROWS, 3 * PAD)
    buf("gproj_v", ROWS, 3 * PAD)
    buf("gmix", ROWS, D)
    buf("glow", ROWS, D)
    buf("acts_in", L, 4, ROWS, D)
    buf("grads_in", 2, 4, ROWS, D)
    buf("parts", 2, 3, ROWS, D)
    buf("came", 2, 3, ROWS, D)
    buf("s_gate", L, 2, 4, ROWS, FFS)
    buf("s_up", L, 2, 4, ROWS, FFS)
    buf("s_act", L, 2, 4, ROWS, FFS)
    for kind, (shape, spread) in KINDS.items():
        four = (4,) if spread else ()
        copies = L if kind in TWICE else 1
        if kind != "o":
            buf("g_" + kind, *four, 2, *shape)
        buf("s_" + kind, L if kind in SUMS_TWICE else 1, *four, *shape)
        buf("x_" + kind, copies, *four, *shape)
        if spread:
            buf("y_" + kind, copies, 3, *shape)
        buf("z_" + kind, copies, 3, *quarter(shape))
        buf("p_" + kind, copies, *quarter(shape))
        buf("h_" + kind, copies, *quarter(shape))
    named["send"] = pltpu.SemaphoreType.DMA((SEMS,))
    named["recv"] = pltpu.SemaphoreType.DMA((SEMS,))
    named["local"] = pltpu.SemaphoreType.DMA((LOCAL_SEMS,))
    named["credit"] = pltpu.SemaphoreType.REGULAR((8,))
    return named


SEMS = 266
LOCAL_SEMS = 53
INPUTS = ("tokens", "cotangent", "lengths", "gain_one", "gain_two", "wq", "wk", "wv", "wo", "wg", "wu", "wd")
OUTPUTS = ("out_act", "out_grad", "f_m", "f_o", "f_q", "f_kv", "hq", "hk", "hv", "ho", "hm")


class Refs:
    pass


def step_kernel(*refs):
    R = Refs()
    names = INPUTS + OUTPUTS + tuple(scratch_shapes())
    for name, ref in zip(names, refs, strict=True):
        setattr(R, name, ref)
    x_hi, z, core, y, x_lo = coords()
    sems = (R.send, R.recv)
    slots = Slots()
    local_slots = Slots()
    spread_at = [slots.take(4) for _ in range(4)]
    back_at = [slots.take(4) for _ in range(4)]
    kept_slots = slots.used
    sibling = device(x_hi, z, 1 - core, y, x_lo)
    near = [device(x_hi, z, core, y, 1 - x_lo), device(1 - x_hi, z, core, y, 1 - x_lo)]
    far = device(1 - x_hi, z, core, y, x_lo)

    def along_y(k):
        return device(x_hi, z, core, (y + k) % 4, x_lo)

    def along_z(k):
        return device(x_hi, (z + k) % 4, core, y, x_lo)

    barrier = pltpu.get_barrier_semaphore()
    everyone = [along_y(k) for k in (1, 2, 3)] + [along_z(k) for k in (1, 2, 3)]
    everyone += near + [far, sibling]
    for target in everyone:
        pl.semaphore_signal(barrier, inc=1, device_id=target, device_id_type=MESH)
    pl.semaphore_wait(barrier, len(everyone))
    home = core == x_lo
    guest = jnp.logical_not(home)

    def keep(src, dst):
        return pltpu.make_async_copy(src, dst, R.local.at[local_slots.take()])

    def start_all(copies):
        for copy in copies:
            copy.start()

    def wait_all(copies):
        for copy in copies:
            copy.wait()

    slab_weights = [
        (R.wq, (R.aq, R.hq), 0),
        (R.wk, (R.ak, R.hk), 1),
        (R.wv, (R.av, R.hv), 1),
        (R.wo, (R.ao, R.ho), None),
    ]
    own_copy, ring, cross, swap, first_swap = {}, {}, {}, {}, {}
    for l in range(LAYERS):
        for a, (src, (here, there), side) in enumerate(slab_weights):
            dst = here if l == 0 else there.at[1]
            if l == 0:
                own_copy[a] = keep(src.at[l], dst.at[y, core])
            for k in (1, 2, 3):
                ring[l, a, k] = remote(src.at[l], dst.at[y, core], sems, slots.take(), along_y(k))
            for k in range(4):
                at = dst.at[(y - k + 4) % 4, core]
                to = near[(0, 0, 1, 1)[k] if side is None else 1 if side == 0 and k == 2 else side]
                cross[l, a, k] = remote(src.at[l] if k == 0 else at, at, sems, slots.take(), to)
                slot = slots.take()
                swap[l, a, k] = remote(at, at, sems, slot, sibling)
                if k == 0:
                    first_swap[l, a] = remote(src.at[l], at, sems, slot, sibling)
    QKV, OUT, ALL = (0, 1, 2), (3,), (0, 1, 2, 3)
    PLANES = (((0, 1), (3, 1)), ((0, 2), (3, 2)), ((0, 3), (3, 3)), tuple((a, k) for a in (1, 2) for k in (1, 2, 3)))
    ring_z = {}
    for units in PLANES:
        for a, k in units:
            at = slab_weights[a][1][1].at[1, (y - k + 4) % 4, core]
            for m in (1, 2, 3):
                ring_z[a, k, m] = remote(at, at, sems, slots.take(), along_z(m))

    def by_plane(body):
        for plane in range(4):

            @pl.when(jnp.logical_and(home, z == plane))
            def _():
                body(plane)

    def planes_begin():
        @pl.when(home)
        def _():
            for a in ALL:
                cross[1, a, 0].start()
                first_swap[1, a].start()

        def body(plane):
            for a, k in PLANES[plane]:
                ring[1, a, k].start()

        by_plane(body)

    def planes_z():
        def body(plane):
            for a, k in PLANES[plane]:
                ring[1, a, k].wait_recv()
                for m in (1, 3, 2):
                    ring_z[a, k, m].start()
                cross[1, a, k].start()
                swap[1, a, k].start()

        by_plane(body)

    def planes_pass():
        def body(plane):
            for other in (3, 0, 1, 2):
                if other != plane:
                    for a, k in PLANES[other]:
                        ring_z[a, k, (plane - other) % 4].wait_recv()
                        cross[1, a, k].start()
                        swap[1, a, k].start()

        by_plane(body)

    def planes_sent():
        def body(plane):
            for a, k in PLANES[plane]:
                ring[1, a, k].wait_send()
                for m in (1, 2, 3):
                    ring_z[a, k, m].wait_send()

        by_plane(body)

    def gather_begin(l, arrays):
        @pl.when(home)
        def _():
            for a in arrays:
                for k in ORDER_Y:
                    ring[l, a, k].start()
                cross[l, a, 0].start()
                first_swap[l, a].start()
                if l == 0:
                    own_copy[a].start()

    def gather_home(l, arrays):
        @pl.when(home)
        def _():
            for k in ORDER_Y:
                for a in arrays:
                    ring[l, a, k].wait_recv()
                    cross[l, a, k].start()
                    swap[l, a, k].start()

    def gather_guest(l, arrays):
        @pl.when(guest)
        def _():
            for k in (0,) + ORDER_Y:
                for a in arrays:
                    cross[l, a, k].wait_recv()
                    swap[l, a, k].start()

    def gather_end(l, arrays):
        for a in arrays:
            for k in range(4):
                swap[l, a, k].wait_recv()
        if l == 0:

            @pl.when(home)
            def _():
                for a in arrays:
                    own_copy[a].wait()

    def gather_sent(l, arrays):
        for a in arrays:

            @pl.when(home)
            def _():
                if l == 0:
                    for k in (1, 2, 3):
                        ring[l, a, k].wait_send()
                for k in range(4):
                    cross[l, a, k].wait_send()

            for k in range(4):
                swap[l, a, k].wait_send()

    saves = [keep(here, there.at[0]) for _, (here, there), _ in slab_weights]
    load_back = [keep(there.at[0], here) for _, (here, there), _ in slab_weights]
    load_own, load_core, load_rest = [], [], []
    for src, (here, there), _ in slab_weights:
        slot = local_slots.take()
        at = here.at[y, core]
        load_own.append(pltpu.make_async_copy(src.at[1], at, R.local.at[slot]))
        load_core.append(pltpu.make_async_copy(there.at[1, y, core], at, R.local.at[slot]))
        rest = [keep(there.at[1, y, 1 - core], here.at[y, 1 - core])]
        for k in (1, 2, 3):
            rest.append(keep(there.at[1, (y + k) % 4], here.at[(y + k) % 4]))
        load_rest.append(rest)

    def load_begin(arrays):
        for a in arrays:
            start_all(load_rest[a])

        @pl.when(home)
        def _():
            start_all([load_own[a] for a in arrays])

        @pl.when(guest)
        def _():
            start_all([load_core[a] for a in arrays])

    def load_end(arrays):
        for a in arrays:
            wait_all(load_rest[a])
            load_own[a].wait()

    mlp_in = [R.wg, R.wu, R.wd]
    save_m = keep(R.mw.at[1 - x_lo], R.hm.at[0])
    load_m = [
        [keep(R.hm.at[l], R.mw.at[1 - x_lo])]
        + [keep(mlp_in[a].at[l], R.mw.at[x_lo, a]) for a in range(3)]
        for l in range(LAYERS)
    ]

    own_gain, other_gain = R.all_gains.at[y, x_lo], R.all_gains.at[y, 1 - x_lo]
    gain_keep = keep(R.own_gains, own_gain)
    gain_x = remote(R.own_gains, own_gain, sems, slots.take(), near[0])
    gain_y = [remote(R.own_gains, own_gain, sems, slots.take(), along_y(k)) for k in (1, 2, 3)]
    gain_pass = [remote(other_gain, other_gain, sems, slots.take(), along_y(k)) for k in (1, 2, 3)]

    SIZES = ((0, 48), (48, 32))
    cross_m, ring_m, pass_m, keep_m = {}, {}, {}, {}
    slot_cross = {(l, a): slots.take() for l in range(LAYERS) for a in range(3)}
    slot_ring = {(l, k): slots.take() for l in range(LAYERS) for k in (1, 2, 3)}
    slot_pass = {(l, k): slots.take() for l in range(LAYERS) for k in range(4)}
    for l in range(LAYERS):
        there_m = R.mw.at[x_lo] if l == 0 else R.hm.at[1]
        here_m = R.mw.at[1 - x_lo] if l == 0 else R.hm.at[1]
        if l == 0:
            for a in range(3):
                keep_m[a] = keep(mlp_in[a].at[l], R.mw.at[x_lo, a])
        for c, (first, size) in enumerate(SIZES):

            def rows(where):
                return pl.ds(pl.multiple_of(where * (FFS // 4) + first, 16), size)

            for a in range(3):
                cross_m[l, c, a] = remote(
                    mlp_in[a].at[l, rows(z)], there_m.at[a, rows(z)], sems, slot_cross[l, a], near[c]
                )
            for k in range(4):
                at = here_m.at[:, rows((z - k + 4) % 4)]
                pass_m[l, c, k] = remote(at, at, sems, slot_pass[l, k], sibling)
            for k in (1, 2, 3):
                at = here_m.at[:, rows(z)]
                ring_m[l, c, k] = remote(at, at, sems, slot_ring[l, k], along_z(k))

    def by_core(body):
        for c in range(2):

            @pl.when(core == c)
            def _():
                body(c)

    def pairs_begin(l):
        def body(c):
            for a in range(3):
                cross_m[l, c, a].start()

        by_core(body)
        if l == 0:
            start_all(keep_m.values())

    def pairs_z(l):
        def body(c):
            for a in range(3):
                cross_m[l, c, a].wait_recv()
            for k in ORDER_Y:
                ring_m[l, c, k].start()
            pass_m[l, c, 0].start()

        by_core(body)

    def pairs_pass(l):
        def body(c):
            for k in ORDER_Y:
                ring_m[l, c, k].wait_recv()
                pass_m[l, c, k].start()

        by_core(body)

    def pairs_end(l):
        def body(c):
            for k in range(4):
                pass_m[l, 1 - c, k].wait_recv()

        by_core(body)
        if l == 0:
            wait_all(keep_m.values())

    def pairs_sent(l):
        def body(c):
            for a in range(3):
                cross_m[l, c, a].wait_send()
            for k in (1, 2, 3):
                ring_m[l, c, k].wait_send()
            for k in range(4):
                pass_m[l, c, k].wait_send()

        by_core(body)


    def spread_copy(n, buffer, k):
        return remote(buffer.at[y], buffer.at[y], sems, spread_at[n] + k, along_y(k))

    def spread(n, buffer, targets=ORDER_Y):
        for k in targets:
            spread_copy(n, buffer, k).start()

    def arrived(n, buffer, k):
        there = buffer.at[(y - k + 4) % 4]
        remote(there, there, sems, spread_at[n] + k, along_y(k)).wait_recv()

    def back_copy(n, k):
        return remote(
            R.parts.at[int(n == 1), k - 1], R.came.at[int(n == 1), k - 1], sems, back_at[n] + k, along_y(4 - k)
        )

    def collect(n, total):
        for k in ORDER_Y:
            back_copy(n, k).wait_recv()
            total = total + R.came[int(n == 1), k - 1].astype(F32)
        return total

    def back(n):
        for k in ORDER_Y:
            back_copy(n, k).start()

    def sent(n, buffer):
        for k in (1, 2, 3):
            spread_copy(n, buffer, k).wait_send()

    def sent_back(n):
        for k in (1, 2, 3):
            back_copy(n, k).wait_send()

    reds = {}
    credit_at = {"m": 0, "o": 4}

    def give(kind, which, targets):
        for target in targets:
            pl.semaphore_signal(
                R.credit.at[credit_at[kind] + which], inc=1, device_id=target, device_id_type=MESH
            )

    def take(kind, which, count):
        pl.semaphore_wait(R.credit.at[credit_at[kind] + which], count)

    class Reduction:
        def __init__(self, kind, l):
            self.kind, self.l = kind, l
            shape, self.spread = KINDS[kind]
            self.planes, self.rows = shape[0], shape[1]
            self.b = b = l if kind in TWICE else 0
            self.gives = kind in credit_at and l == 1
            self.takes = kind in credit_at and l == 0
            self.g = R.g_q if kind == "o" else getattr(R, "g_" + kind)
            self.s = getattr(R, "s_" + kind).at[l if kind in SUMS_TWICE else 0]
            self.x = getattr(R, "x_" + kind).at[b]
            self.zb = getattr(R, "z_" + kind).at[b]
            self.p = getattr(R, "p_" + kind).at[b]
            self.h = getattr(R, "h_" + kind).at[b]
            self.f = getattr(R, "f_" + kind).at[l]
            self.chunk = {128: 64, 320: 80}[self.rows]
            n = 4 if self.spread else 1
            self.at_pair = slots.take(n)
            self.at_x = slots.take(4 if self.spread else 2)
            self.at_y = slots.take(4)
            self.at_z = slots.take(4)
            self.at_out = slots.take(4)
            self.at_far = slots.take()
            self.at_last = slots.take()
            self.own = pltpu.make_async_copy(self.p, self.piece(self.f, z), R.local.at[local_slots.take()])
            if self.spread:
                self.yb = getattr(R, "y_" + kind).at[b]

        def piece(self, ref, where):
            size = self.rows // 4
            return ref.at[:, pl.ds(pl.multiple_of(where * size, 16), size)]

        def add(self, dst, others, chunk=None):
            for i in range(self.planes):
                accumulate(dst.at[i], [o.at[i] for o in others], chunk or self.chunk)

        def pair(self, q):
            if self.spread:
                return remote(self.g.at[q, 1 - core], self.s.at[q], sems, self.at_pair + q, sibling)
            return remote(self.g.at[1 - core], self.s, sems, self.at_pair, sibling)

        def over_x(self, q):
            if self.spread:
                return remote(self.s.at[q], self.x.at[q], sems, self.at_x + q, near[q // 2])
            half = slice(q * (self.rows // 2), (q + 1) * (self.rows // 2))
            return remote(self.s.at[:, half], self.x.at[:, half], sems, self.at_x + q, near[q])

        def came_x(self, q):
            return remote(self.s.at[q], self.x.at[q], sems, self.at_x + q, near[0])

        def over_y(self, k):
            return remote(self.s.at[(y + k) % 4], self.yb.at[k - 1], sems, self.at_y + k, along_y(k))

        def mine(self):
            return self.s.at[y] if self.spread else self.s

        def over_z(self, k):
            return remote(
                self.piece(self.mine(), (z + k) % 4), self.zb.at[k - 1], sems, self.at_z + k, along_z(k)
            )

        def over_far(self):
            return remote(self.p, self.h, sems, self.at_far, far)

        def out_z(self, k):
            return remote(self.p, self.piece(self.f, z), sems, self.at_out + k, along_z(k))

        def last(self):
            return remote(self.f, self.f, sems, self.at_last, sibling)

        def begin(self):
            if self.takes and self.kind == "m":
                take(self.kind, 0, 1)
            for q in (0, 2, 1, 3) if self.spread else (0,):
                self.pair(q).start()

        def step_x(self):
            if self.takes:
                self.when_guest(lambda: take(self.kind, 1, 2))
            for q in (0, 2, 1, 3) if self.spread else (0,):
                self.pair(q).wait()
                if self.spread:
                    self.add(self.s.at[q], [self.g.at[q, core]])
                    self.when_guest(lambda: self.over_x(q).start())
                else:
                    self.add(self.s, [self.g.at[core]])
                    self.when_guest(lambda: [self.over_x(i).start() for i in range(2)])

        def step_y(self):
            @pl.when(home)
            def _():
                if self.spread:
                    if self.takes:
                        take(self.kind, 0, 3)
                    for k in ORDER_Y + (0,):
                        q = (y + k) % 4
                        self.came_x(q).wait_recv()
                        self.add(self.s.at[q], [self.x.at[q]])
                        if k:
                            self.over_y(k).start()
                else:
                    for q in range(2):
                        self.over_x(q).wait_recv()
                    self.add(self.s, [self.x])
                    self.start_z()
                if self.gives:
                    give(self.kind, 1, near)

        def start_z(self):
            if self.takes:
                take(self.kind, 2, 3)
            for k in ORDER_Y:
                self.over_z(k).start()

        def step_z(self):
            if self.spread:

                @pl.when(home)
                def _():
                    for k in ORDER_Y:
                        self.over_y(k).wait_recv()
                    self.add(self.mine(), [self.yb.at[j] for j in range(3)])
                    if self.gives:
                        give(self.kind, 0, [along_y(k) for k in (1, 2, 3)])
                    self.start_z()

        def step_far(self):
            @pl.when(home)
            def _():
                for k in ORDER_Y:
                    self.over_z(k).wait_recv()
                for i in range(self.planes):
                    total = self.piece(self.mine(), z)[i].astype(F32)
                    for j in range(3):
                        total = total + self.zb[j, i].astype(F32)
                    self.p[i] = total.astype(BF)
                if self.takes:
                    take(self.kind, 3, 1)
                self.over_far().start()
                for k in (1, 2, 3):
                    self.over_z(k).wait_send()
                    if self.spread:
                        self.over_y(k).wait_send()
                if self.gives:
                    give(self.kind, 2, [along_z(k) for k in (1, 2, 3)])

            @pl.when(guest)
            def _():
                for q in range(4 if self.spread else 2):
                    self.over_x(q).wait_send()

            if self.gives and self.kind == "m":
                give(self.kind, 0, [sibling])

        def step_out(self):
            @pl.when(home)
            def _():
                self.over_far().wait()
                self.add(self.p, [self.h], self.rows // 4)
                self.own.start()
                for k in ORDER_Y:
                    self.out_z(k).start()
                if self.gives:
                    give(self.kind, 3, [far])

        def step_last(self):
            @pl.when(home)
            def _():
                self.own.wait()
                for k in ORDER_Y:
                    self.out_z(k).wait()
                self.last().start()

        def finish(self):
            @pl.when(home)
            def _():
                self.last().wait_send()

            @pl.when(guest)
            def _():
                self.last().wait_recv()

        def when_guest(self, body):
            @pl.when(guest)
            def _():
                body()

    first_slots = slots
    for l in (1, 0):
        if l == 0:
            slots = Slots()
            slots.take(kept_slots)
        for kind in KINDS:
            reds[kind, l] = Reduction(kind, l)

    assert max(slots.used, first_slots.used) <= SEMS and local_slots.used <= LOCAL_SEMS

    column = lax.broadcasted_iota(jnp.int32, (ROWS, PAD), 1)
    first_half = column % HEAD < HEAD // 2

    def turn(block, sign):
        ahead = pltpu.roll(block, PAD - HEAD // 2, 1)
        behind = pltpu.roll(block, HEAD // 2, 1)
        return jnp.where(first_half, -sign * ahead, sign * behind)

    def rotated(block):
        return block * R.cosine[...] + turn(block, 1.0) * R.sine[...]

    def rotated_back(block):
        return block * R.cosine[...] + turn(block * R.sine[...], -1.0)

    def inverse_rms(x):
        return lax.rsqrt(jnp.mean(x * x, axis=-1, keepdims=True) + norm_eps)

    def head_lanes(h):
        return slice(h * HEAD, (h + 1) * HEAD)

    def tables():
        one, two = R.lengths[0, 0], R.lengths[0, 1]
        row = lax.broadcasted_iota(jnp.int32, (ROWS, PAD), 0)

        def doc(t):
            return (t >= one).astype(jnp.int32) + (t >= one + two).astype(jnp.int32)

        own = doc(row)
        begins = jnp.where(own == 0, 0, jnp.where(own == 1, one, one + two))
        allowed = jnp.logical_and(own == doc(column), column <= row)
        R.bias[...] = jnp.where(allowed, 0.0, masked_value)
        slow = jnp.exp((column % (HEAD // 2)).astype(F32) * (-2.0 * log_base / HEAD))
        angles = (row - begins).astype(F32) * slow
        R.cosine[...] = jnp.cos(angles)
        R.sine[...] = jnp.sin(angles)
        wide_column = lax.broadcasted_iota(jnp.int32, (D, 8 * PAD), 1)
        wide_row = lax.broadcasted_iota(jnp.int32, (D, 8 * PAD), 0)
        lane = wide_column % PAD
        R.place[...] = jnp.where(
            jnp.logical_and(lane < SHARD, (wide_column // PAD) * SHARD + lane == wide_row), 1.0, 0.0
        ).astype(BF)
        R.wide[...] = jnp.zeros_like(R.wide)
        R.narrow[...] = jnp.zeros_like(R.narrow)
        R.gain_rows[...] = jnp.zeros_like(R.gain_rows)
        R.stream[0] = R.tokens[...].astype(F32).T

    def soft_weights(l, kv):
        rows = jnp.concatenate([R.qrot[l, :, head_lanes(kv * SHARE + i)] for i in range(SHARE)], axis=0)
        keys = R.krot[l, :, head_lanes(kv)]
        scores = dot_t(rows, keys) * score_scale
        scores = scores + jnp.concatenate([R.bias[...]] * SHARE, axis=0)
        weights = jnp.exp(scores - jnp.max(scores, axis=-1, keepdims=True))
        return rows, keys, weights / jnp.sum(weights, axis=-1, keepdims=True)

    def attention_forward(l, ready_qkv, ready_out):
        x = R.stream[l]
        normed = (x * inverse_rms(x) * R.gain_full[l : l + 1, :]).astype(BF)
        R.npad[l] = dot(normed, R.place[...]).astype(BF)

        def project(weights, width, product):
            total = jnp.zeros((ROWS, width), F32)
            for g in range(8):
                total = total + product(
                    R.npad[l, :, g * PAD : g * PAD + SHARD], weights[g // 2, g % 2]
                )
            return total

        ready_qkv()
        R.wide[:, :D] = project(R.aq, D, dot)
        R.narrow[:, :KV] = project(R.ak, KV, dot_t)
        R.vals[l, :, :KV] = project(R.av, KV, dot_t).astype(BF)
        for j in range(8):
            at = slice(j * PAD, (j + 1) * PAD)
            R.qrot[l, :, at] = rotated(R.wide[:, at]).astype(BF)
        for j in range(3):
            at = slice(j * PAD, (j + 1) * PAD)
            R.krot[l, :, at] = rotated(R.narrow[:, at]).astype(BF)
        for kv in range(KV_HEADS):
            rows, keys, soft = soft_weights(l, kv)
            out = dot(soft.astype(BF), R.vals[l, :, head_lanes(kv)]).astype(BF)
            for i in range(SHARE):
                R.gproj_q[:, head_lanes(kv * SHARE + i)] = out[i * ROWS : (i + 1) * ROWS]
        R.mpad[l] = dot(R.gproj_q[:, :D], R.place[...]).astype(BF)
        ready_out()
        total = x
        for g in range(8):
            total = total + dot(R.mpad[l, :, g * PAD : g * PAD + SHARD], R.ao[g // 2, g % 2])
        R.hidden[l] = total
        R.acts_in[l, y] = (total * inverse_rms(total) * R.gain_full[2 + l : 3 + l, :]).astype(BF)

    def blocks(n, buffer, body, between=None):
        def block(i, carry):
            k = order(i)
            b = (y - k + 4) % 4
            if between is not None:
                pl.when(i == 1)(between)

            @pl.when(i > 0)
            def _():
                arrived(n, buffer, k)

            total = body(b)
            if total is None:
                return carry

            @pl.when(i == 0)
            def _():
                R.own_part[...] = total

            @pl.when(i > 0)
            def _():
                R.parts[int(n == 1), k - 1] = total.astype(BF)
                back_copy(n, k).start()

            return carry

        lax.fori_loop(0, 4, block, 0)

    def mlp_forward(l, n, down=True, between=None):
        def body(b):
            rows = R.acts_in[l, b]
            total = jnp.zeros((ROWS, D), F32) if down else None
            for p in range(2):
                gate = dot_t(rows, R.mw[p, 0])
                up = dot_t(rows, R.mw[p, 1])
                act = (gate * jax.nn.sigmoid(gate) * up).astype(BF)
                R.s_gate[l, p, b] = gate.astype(BF)
                R.s_up[l, p, b] = up.astype(BF)
                R.s_act[l, p, b] = act
                if down:
                    total = total + dot(act, R.mw[p, 2])
            return total

        blocks(n, R.acts_in.at[l], body, between)

    def mlp_down(l, n):
        def block(i, carry):
            k = order(i)
            b = (y - k + 4) % 4
            total = dot(R.s_act[l, 0, b], R.mw[0, 2]) + dot(R.s_act[l, 1, b], R.mw[1, 2])

            @pl.when(i == 0)
            def _():
                R.out_grad[...] = (total + R.hidden[l]).T

            @pl.when(i > 0)
            def _():
                R.parts[int(n == 1), k - 1] = total.astype(BF)

            return carry

        lax.fori_loop(0, 4, block, 0)

    def result_out(n):
        R.out_act[...] = (R.out_grad[...] + collect(n, jnp.zeros((ROWS, D), F32)).T).astype(BF)

    def mlp_backward(l, n):
        def body(b):
            rows = R.grads_in[1 - l, b]
            total = jnp.zeros((ROWS, D), F32)
            for p in range(2):
                grad_active = dot_t(rows, R.mw[p, 2])
                gate = R.s_gate[l, p, b].astype(F32)
                up = R.s_up[l, p, b].astype(F32)
                sig = jax.nn.sigmoid(gate)
                grad_gate = (grad_active * up * sig * (1.0 + gate * (1.0 - sig))).astype(BF)
                grad_up = (grad_active * gate * sig).astype(BF)
                R.s_gate[l, p, b] = grad_gate
                R.s_up[l, p, b] = grad_up
                total = total + dot(grad_gate, R.mw[p, 0]) + dot(grad_up, R.mw[p, 1])
            return total

        blocks(n, R.grads_in.at[1 - l], body)

    def mlp_grads(l):
        def grads(p, carry):
            ins = R.acts_in[l].reshape(4 * ROWS, D)
            R.g_m[p, 0] = t_dot(R.s_gate[l, p].reshape(4 * ROWS, FFS), ins).astype(BF)
            R.g_m[p, 1] = t_dot(R.s_up[l, p].reshape(4 * ROWS, FFS), ins).astype(BF)
            R.g_m[p, 2] = t_dot(
                R.s_act[l, p].reshape(4 * ROWS, FFS), R.grads_in[1 - l].reshape(4 * ROWS, D)
            ).astype(BF)
            return carry

        lax.fori_loop(0, 2, grads, 0)

    def slab_loop(body):
        def run(g, carry):
            body(g, g // 2, g % 2)
            return carry

        lax.fori_loop(0, 8, run, 0)

    def norm_back(x, grad_normed, gain_row):
        r = inverse_rms(x)
        u = grad_normed * gain_row
        back = r * u - x * (r * r * r) * jnp.mean(u * x, axis=-1, keepdims=True)
        return back, jnp.sum(grad_normed * x * r, axis=0, keepdims=True)

    def back_hidden(l, n):
        grad_input = collect(n, R.own_part[...])
        back, grad_gain = norm_back(R.hidden[l], grad_input, R.gain_full[2 + l : 3 + l, :])
        grad_hidden = R.grad[...] + back
        R.grad[...] = grad_hidden
        R.glow[...] = grad_hidden.astype(BF)
        R.gain_rows[1:2, :] = grad_gain

        def back_out(g, h, i):
            R.wide[:, lanes(g, SHARD)] = dot_t(R.glow[...], R.ao[h, i])

        slab_loop(back_out)
        R.gmix[...] = dot_t(R.wide[...].astype(BF), R.place[...]).astype(BF)

    def grads_out(l):
        def body(g, h, i):
            R.g_q[h, i, 0] = t_dot(R.mpad[l, :, lanes(g, PAD)], R.glow[...]).astype(BF)

        slab_loop(body)

    def back_heads(l):
        for kv in range(KV_HEADS):
            rows, keys, soft = soft_weights(l, kv)
            heads = [kv * SHARE + i for i in range(SHARE)]
            gm = jnp.concatenate([R.gmix[:, head_lanes(h)] for h in heads], axis=0)
            grad_probs = dot_t(gm, R.vals[l, :, head_lanes(kv)])
            inner = jnp.sum(soft * grad_probs, axis=-1, keepdims=True)
            grad_scores = (soft * (grad_probs - inner)).astype(BF)
            grad_rows = dot(grad_scores, keys) * score_scale
            for i, h in enumerate(heads):
                R.wide[:, head_lanes(h)] = grad_rows[i * ROWS : (i + 1) * ROWS]
            R.narrow[:, head_lanes(kv)] = t_dot(grad_scores, rows) * score_scale
            R.gproj_v[:, head_lanes(kv)] = t_dot(soft.astype(BF), gm).astype(BF)
        for j in range(8):
            at = slice(j * PAD, (j + 1) * PAD)
            R.gproj_q[:, at] = rotated_back(R.wide[:, at]).astype(BF)
        for j in range(3):
            at = slice(j * PAD, (j + 1) * PAD)
            R.gproj_k[:, at] = rotated_back(R.narrow[:, at]).astype(BF)

    def back_stream(l):
        def back_in(g, h, i):
            R.wide[:, lanes(g, SHARD)] = (
                dot_t(R.gproj_q[:, :D], R.aq[h, i])
                + dot(R.gproj_k[:, :KV], R.ak[h, i])
                + dot(R.gproj_v[:, :KV], R.av[h, i])
            )

        slab_loop(back_in)
        high, low = halves(R.wide[...])
        grad_normed = dot_t(high, R.place[...]) + dot_t(low, R.place[...])
        back, grad_gain = norm_back(R.stream[l], grad_normed, R.gain_full[l : l + 1, :])
        R.grad[...] = R.grad[...] + back
        R.gain_rows[0:1, :] = grad_gain

    def grads_kv(l):
        def body(g, h, i):
            right = R.npad[l, :, lanes(g, PAD)]
            R.g_kv[h, i, 0] = t_dot(R.gproj_k[:, :KV], right).astype(BF)
            R.g_kv[h, i, 1] = t_dot(R.gproj_v[:, :KV], right).astype(BF)

        slab_loop(body)

    def grads_q(l):
        high, low = halves(R.gain_rows[...])
        R.gain_grad[...] = dot(high, R.place[...]) + dot(low, R.place[...])

        def body(g, h, i):
            total = t_dot(R.npad[l, :, lanes(g, PAD)], R.gproj_q[:, :D])
            rows = lax.broadcasted_iota(jnp.int32, (PAD, PAD), 0)
            corner = (
                total[:, :PAD]
                + jnp.where(rows == SHARD, R.gain_grad[0:1, lanes(g, PAD)], 0.0)
                + jnp.where(rows == SHARD + 1, R.gain_grad[1:2, lanes(g, PAD)], 0.0)
            )
            R.g_q[h, i, 0] = total.astype(BF)
            R.g_q[h, i, 0, :, :PAD] = corner.astype(BF)

        slab_loop(body)

    gather_begin(0, QKV)
    R.own_gains[...] = jnp.zeros_like(R.own_gains)
    R.own_gains[0:2, :SHARD] = R.gain_one[...]
    R.own_gains[2:4, :SHARD] = R.gain_two[...]
    gain_keep.start()
    gain_x.start()
    start_all(gain_y)
    pairs_begin(0)
    gather_home(0, QKV)
    gather_begin(0, OUT)
    planes_begin()
    tables()
    gain_x.wait()
    start_all(gain_pass)
    gather_guest(0, QKV)
    pairs_z(0)
    gather_home(0, OUT)
    gain_keep.wait()
    wait_all(gain_y)
    wait_all(gain_pass)
    for g in range(8):
        R.gain_pad[:, g * PAD : (g + 1) * PAD] = R.all_gains[g // 2, g % 2]
    R.gain_full[...] = dot_t(R.gain_pad[...], R.place[...])
    gather_guest(0, OUT)
    pairs_begin(1)

    def ready_out():
        gather_end(0, OUT)
        pairs_pass(0)
        planes_z()
        start_all(saves)

    attention_forward(0, lambda: gather_end(0, QKV), ready_out)
    spread(0, R.acts_in.at[0])
    pairs_end(0)
    save_m.start()

    def between():
        planes_pass()
        pairs_z(1)

    mlp_forward(0, 0, between=between)
    gather_guest(1, QKV)
    gather_sent(0, ALL)
    wait_all(saves)
    pairs_pass(1)
    cot = R.cotangent[...].astype(F32).T
    R.grads_in[0, y] = cot.astype(BF)
    R.grad[...] = cot
    gather_end(1, QKV)
    load_begin(QKV)
    R.stream[1] = collect(0, R.own_part[...] + R.hidden[0])
    spread(2, R.grads_in.at[0], (1, 3))
    pairs_sent(0)
    save_m.wait()
    gather_guest(1, OUT)

    def ready_out_1():
        gather_end(1, OUT)
        load_begin(OUT)
        pairs_end(1)
        start_all(load_m[1])
        load_end(OUT)

    attention_forward(1, lambda: load_end(QKV), ready_out_1)
    spread(1, R.acts_in.at[1])
    spread(2, R.grads_in.at[0], (2,))
    sent(0, R.acts_in.at[0])
    sent_back(0)
    wait_all(load_m[1])
    mlp_forward(1, 1, down=False)

    m1, o1, q1, kv1 = (reds[kind, 1] for kind in ("m", "o", "q", "kv"))
    m0, o0, q0, kv0 = (reds[kind, 0] for kind in ("m", "o", "q", "kv"))
    mlp_backward(1, 2)
    mlp_grads(1)
    gather_sent(1, ALL)
    planes_sent()
    pairs_sent(1)
    m1.begin()
    mlp_down(1, 1)
    start_all(load_m[0])
    back_hidden(1, 2)
    back(1)
    m1.step_x()
    back_heads(1)
    back_stream(1)
    R.grads_in[1, y] = R.grad[...].astype(BF)
    spread(3, R.grads_in.at[1])
    start_all(load_back)
    grads_out(1)
    o1.begin()
    grads_kv(1)
    kv1.begin()
    result_out(1)
    o1.step_x()
    m1.step_y()
    grads_q(1)
    q1.begin()
    sent(1, R.acts_in.at[1])
    sent_back(2)
    wait_all(load_m[0])
    mlp_backward(0, 3)
    kv1.step_x()
    q1.step_x()
    mlp_grads(0)
    m1.step_far()
    m0.begin()
    o1.step_y()
    wait_all(load_back)
    back_hidden(0, 3)
    m0.step_x()
    grads_out(0)
    o0.begin()
    kv1.step_y()
    q1.step_y()
    o1.step_z()
    m1.step_out()
    back_heads(0)
    o0.step_x()
    grads_kv(0)
    kv0.begin()
    kv1.step_z()
    q1.step_z()
    m0.step_y()
    back_stream(0)
    kv0.step_x()
    grads_q(0)
    q0.begin()
    o1.step_far()
    R.out_grad[...] = R.grad[...].T
    o0.step_y()
    q0.step_x()
    m1.step_last()
    m0.step_far()
    kv0.step_y()
    kv1.step_far()
    q1.step_far()
    o1.step_out()
    o0.step_z()
    kv0.step_z()
    q0.step_y()
    kv1.step_out()
    q1.step_out()
    o1.step_last()
    o0.step_far()
    kv0.step_far()
    q0.step_z()
    m0.step_out()
    o0.step_out()
    kv0.step_out()
    q0.step_far()
    kv1.step_last()
    q1.step_last()
    q0.step_out()
    o0.step_last()
    kv0.step_last()
    m0.step_last()
    q0.step_last()
    for red in (m1, o1, kv1, q1, m0, kv0, o0, q0):
        red.finish()
    sent(2, R.grads_in.at[0])
    sent(3, R.grads_in.at[1])
    sent_back(1)
    sent_back(3)


def step(*args):
    L = LAYERS

    def out(*shape, dtype=BF):
        return jax.ShapeDtypeStruct(shape, dtype)

    return pl.pallas_call(
        step_kernel,
        out_shape=(
            out(D, ROWS),
            out(D, ROWS, dtype=F32),
            out(L, 3, FFS, D),
            out(L, 1, ROWS, D),
            out(L, 1, ROWS, D),
            out(L, 2, KV, PAD),
            out(L, 4, 2, SHARD, D),
            out(L, 4, 2, KV, SHARD),
            out(L, 4, 2, KV, SHARD),
            out(L, 4, 2, SHARD, D),
            out(L, 3, FFS, D),
        ),
        in_specs=[VMEM] * 2 + [SMEM] + [VMEM] * 2 + [ANY] * 7,
        out_specs=[VMEM] * 2 + [ANY] * 9,
        scratch_shapes=list(scratch_shapes().values()),
        compiler_params=pltpu.CompilerParams(
            collective_id=1, has_side_effects=True, vmem_limit_bytes=63 * 2**20
        ),
    )(*args)


def widen_kernel(
    act, grad, fm, fo, fq, fkv,
    act_out, grad_out, gate, up, down, out, query, key, value, gain_one, gain_two,
    act_v, grad_v, fm_v, fo_v, fq_v, fkv_v, m_w, o_w, q_w, k_w, v_w, came, went,
):
    ins = [pltpu.make_async_copy(fm.at[l], fm_v.at[l], came.at[l]) for l in range(LAYERS)]
    rest = ((fq, fq_v), (fo, fo_v), (fkv, fkv_v), (act, act_v), (grad, grad_v))
    ins += [pltpu.make_async_copy(src, dst, came.at[2 + i]) for i, (src, dst) in enumerate(rest)]
    for copy in ins:
        copy.start()
    outs = []

    def put(src, dst):
        outs.append(pltpu.make_async_copy(src, dst, went.at[len(outs)]))
        outs[-1].start()

    for l in range(LAYERS):
        ins[l].wait()
        for a, dst in enumerate((gate, up, down)):
            m_w[l, a] = fm_v[l, a].astype(F32)
            put(m_w.at[l, a], dst.at[l])
    for copy in ins[2:]:
        copy.wait()
    put(act_v, act_out)
    put(grad_v, grad_out)
    for l in range(LAYERS):
        wide = fq_v[l, 0].astype(F32)
        q_w[l] = wide[:SHARD]
        gain_one[l : l + 1, :] = wide[SHARD : SHARD + 1, :SHARD]
        gain_two[l : l + 1, :] = wide[SHARD + 1 : SHARD + 2, :SHARD]
    put(q_w, query)
    o_w[...] = fo_v[:, 0, :SHARD].astype(F32)
    put(o_w, out)
    k_w[...] = fkv_v[:, 0, :, :SHARD].astype(F32)
    put(k_w, key)
    v_w[...] = fkv_v[:, 1, :, :SHARD].astype(F32)
    put(v_w, value)
    for copy in outs:
        copy.wait()


def widen(act, grad, fm, fo, fq, fkv):
    L = LAYERS

    def out(*shape):
        return jax.ShapeDtypeStruct(shape, F32)

    ins = (act, grad, fm, fo, fq, fkv)
    wide = ((L, 3, FFS, D), (L, SHARD, D), (L, SHARD, D), (L, KV, SHARD), (L, KV, SHARD))
    return pl.pallas_call(
        widen_kernel,
        out_shape=(
            jax.ShapeDtypeStruct(act.shape, act.dtype), out(*grad.shape),
            out(L, FFS, D), out(L, FFS, D), out(L, FFS, D), out(L, SHARD, D), out(L, SHARD, D),
            out(L, KV, SHARD), out(L, KV, SHARD), out(L, SHARD), out(L, SHARD),
        ),
        in_specs=[ANY] * 6,
        out_specs=[ANY] * 9 + [VMEM] * 2,
        scratch_shapes=[pltpu.VMEM(a.shape, a.dtype) for a in ins]
        + [pltpu.VMEM(shape, F32) for shape in wide]
        + [pltpu.SemaphoreType.DMA((7,)), pltpu.SemaphoreType.DMA((12,))],
        compiler_params=pltpu.CompilerParams(vmem_limit_bytes=63 * 2**20),
    )(*ins)


def shards(
    tokens, cotangent, lengths, gain_attn, w_query, w_key, w_value, w_out, gain_mlp, w_gate, w_up, w_down
):
    def turned(a):
        return jnp.swapaxes(a, -1, -2)

    act, grad, fm, fo, fq, fkv, *_ = step(
        turned(tokens), turned(cotangent), lengths, gain_attn, gain_mlp,
        w_query, turned(w_key), turned(w_value), w_out, turned(w_gate), turned(w_up), w_down,
    )
    act, grad, gate, up, down, out, query, key, value, gain_one, gain_two = widen(
        act, grad, fm, fo, fq, fkv
    )
    return (
        turned(act),
        turned(grad),
        gain_one,
        query,
        turned(key),
        turned(value),
        out,
        gain_two,
        turned(gate),
        turned(up),
        down,
    )


def solution(mesh):
    in_specs = (
        P(("replica", "group"), None),
        P(("replica", "group"), None),
        P(("replica", "group"), None),
        P(None, "group"),
        P(None, "group", None),
        P(None, "group", None),
        P(None, "group", None),
        P(None, "group", None),
        P(None, "group"),
        P(None, None, "group"),
        P(None, None, "group"),
        P(None, "group", None),
    )
    out_specs = (
        P(("replica", "group"), None),
        P(("replica", "group"), None),
        P(None, "group"),
        P(None, "group", None),
        P(None, "group", None),
        P(None, "group", None),
        P(None, "group", None),
        P(None, "group"),
        P(None, None, "group"),
        P(None, None, "group"),
        P(None, "group", None),
    )
    return jax.shard_map(shards, mesh=mesh, in_specs=in_specs, out_specs=out_specs, check_vma=False)
```

```python
import jax
import jax.numpy as jnp
from jax import lax
from jax.experimental import pallas as pl
from jax.experimental.pallas import tpu as pltpu
from jax.sharding import PartitionSpec as P

Q_HEADS = 15
KV_HEADS = 5
HEAD = 64
LAYERS = 2
D = 960
SHARD = 120
PAD = 128
FFS = 320
ROWS = 128
KV = KV_HEADS * HEAD
SHARE = Q_HEADS // KV_HEADS

norm_eps = 1e-05
rope_base = 100000.0
log_base = 11.512925464970229
score_scale = 0.125
masked_value = -1e30
MESH = pl.DeviceIdType.MESH
BF = jnp.bfloat16
F32 = jnp.float32
ANY = pl.BlockSpec(memory_space=pl.ANY)
VMEM = pl.BlockSpec(memory_space=pltpu.VMEM)
SMEM = pl.BlockSpec(memory_space=pltpu.SMEM)


def coords():
    r = lax.axis_index("replica")
    g = lax.axis_index("group")
    return r // 8, (r // 2) % 4, r % 2, g // 2, g % 2


def device(x_hi, z, core, y, x_lo):
    return ((x_hi * 4 + z) * 2 + core, y * 2 + x_lo)


def remote(src, dst, sems, index, target):
    return pltpu.make_async_remote_copy(
        src_ref=src,
        dst_ref=dst,
        send_sem=sems[0].at[index],
        recv_sem=sems[1].at[index],
        device_id=target,
        device_id_type=MESH,
    )


def dot(a, b):
    return lax.dot_general(a, b, (((1,), (0,)), ((), ())), preferred_element_type=F32)


def dot_t(a, b):
    return lax.dot_general(a, b, (((1,), (1,)), ((), ())), preferred_element_type=F32)


def t_dot(a, b):
    return lax.dot_general(a, b, (((0,), (0,)), ((), ())), preferred_element_type=F32)


def lanes(g, width):
    return pl.ds(pl.multiple_of(g * PAD, PAD), width)


def halves(a):
    high = a.astype(BF)
    return high, (a - high.astype(F32)).astype(BF)


def accumulate(dst, others, chunk):
    def body(i, carry):
        at = pl.ds(pl.multiple_of(i * chunk, chunk), chunk)
        total = dst[at, :].astype(F32)
        for other in others:
            total = total + other[at, :].astype(F32)
        dst[at, :] = total.astype(dst.dtype)
        return carry

    lax.fori_loop(0, dst.shape[0] // chunk, body, 0)


class Slots:
    def __init__(self):
        self.used = 0

    def take(self, count=1):
        self.used += count
        return self.used - count


def order(k):
    return k + (k // 2) * (5 - 2 * k)


KINDS = {
    "m": ((3, FFS, D), False),
    "o": ((1, ROWS, D), True),
    "q": ((1, ROWS, D), True),
    "kv": ((2, KV, PAD), True),
}
TWICE = ("q", "kv")
SUMS_TWICE = ("o", "q", "kv")
ORDER_Y = (1, 3, 2)


def quarter(shape):
    return (shape[0], shape[1] // 4, shape[2])


def scratch_shapes():
    L = LAYERS
    named = {}

    def buf(name, *shape, dtype=BF):
        named[name] = pltpu.VMEM(shape, dtype)

    buf("aq", 4, 2, SHARD, D)
    buf("ao", 4, 2, SHARD, D)
    buf("ak", 4, 2, KV, SHARD)
    buf("av", 4, 2, KV, SHARD)
    buf("mw", 2, 3, FFS, D)
    buf("all_gains", 4, 2, 16, PAD)
    buf("own_gains", 16, PAD)
    buf("place", D, 8 * PAD)
    buf("cosine", ROWS, PAD, dtype=F32)
    buf("sine", ROWS, PAD, dtype=F32)
    buf("bias", ROWS, ROWS, dtype=F32)
    buf("gain_full", 16, D, dtype=F32)
    buf("gain_pad", 16, 8 * PAD)
    buf("gain_grad", 16, 8 * PAD, dtype=F32)
    buf("gain_rows", 16, D, dtype=F32)
    buf("stream", L, ROWS, D, dtype=F32)
    buf("hidden", L, ROWS, D, dtype=F32)
    buf("grad", ROWS, D, dtype=F32)
    buf("wide", ROWS, 8 * PAD, dtype=F32)
    buf("narrow", ROWS, 3 * PAD, dtype=F32)
    buf("own_part", ROWS, D, dtype=F32)
    buf("npad", L, ROWS, 8 * PAD)
    buf("mpad", L, ROWS, 8 * PAD)
    buf("qrot", L, ROWS, 8 * PAD)
    buf("krot", L, ROWS, 3 * PAD)
    buf("vals", L, ROWS, 3 * PAD)
    buf("gproj_q", ROWS, 8 * PAD)
    buf("gproj_k", ROWS, 3 * PAD)
    buf("gproj_v", ROWS, 3 * PAD)
    buf("gmix", ROWS, D)
    buf("glow", ROWS, D)
    buf("acts_in", L, 4, ROWS, D)
    buf("grads_in", 2, 4, ROWS, D)
    buf("parts", 2, 3, ROWS, D)
    buf("came", 2, 3, ROWS, D)
    buf("s_gate", L, 2, 4, ROWS, FFS)
    buf("s_up", L, 2, 4, ROWS, FFS)
    buf("s_act", L, 2, 4, ROWS, FFS)
    for kind, (shape, spread) in KINDS.items():
        four = (4,) if spread else ()
        copies = L if kind in TWICE else 1
        if kind != "o":
            buf("g_" + kind, *four, 2, *shape)
        buf("s_" + kind, L if kind in SUMS_TWICE else 1, *four, *shape)
        buf("x_" + kind, copies, *four, *shape)
        if spread:
            buf("y_" + kind, copies, 3, *shape)
        buf("z_" + kind, copies, 3, *quarter(shape))
        buf("p_" + kind, copies, *quarter(shape))
        buf("h_" + kind, copies, *quarter(shape))
    named["send"] = pltpu.SemaphoreType.DMA((SEMS,))
    named["recv"] = pltpu.SemaphoreType.DMA((SEMS,))
    named["local"] = pltpu.SemaphoreType.DMA((LOCAL_SEMS,))
    named["credit"] = pltpu.SemaphoreType.REGULAR((8,))
    return named


SEMS = 274
LOCAL_SEMS = 53
INPUTS = ("tokens", "cotangent", "lengths", "gain_one", "gain_two", "wq", "wk", "wv", "wo", "wg", "wu", "wd")
OUTPUTS = ("out_act", "out_grad", "f_m", "f_o", "f_q", "f_kv", "hq", "hk", "hv", "ho", "hm")


class Refs:
    pass


def step_kernel(*refs):
    R = Refs()
    names = INPUTS + OUTPUTS + tuple(scratch_shapes())
    for name, ref in zip(names, refs, strict=True):
        setattr(R, name, ref)
    x_hi, z, core, y, x_lo = coords()
    sems = (R.send, R.recv)
    slots = Slots()
    local_slots = Slots()
    spread_at = [slots.take(4) for _ in range(4)]
    back_at = [slots.take(4) for _ in range(4)]
    kept_slots = slots.used
    sibling = device(x_hi, z, 1 - core, y, x_lo)
    near = [device(x_hi, z, core, y, 1 - x_lo), device(1 - x_hi, z, core, y, 1 - x_lo)]
    far = device(1 - x_hi, z, core, y, x_lo)

    def along_y(k):
        return device(x_hi, z, core, (y + k) % 4, x_lo)

    def along_z(k):
        return device(x_hi, (z + k) % 4, core, y, x_lo)

    barrier = pltpu.get_barrier_semaphore()
    everyone = [along_y(k) for k in (1, 2, 3)] + [along_z(k) for k in (1, 2, 3)]
    everyone += near + [far, sibling]
    for target in everyone:
        pl.semaphore_signal(barrier, inc=1, device_id=target, device_id_type=MESH)
    pl.semaphore_wait(barrier, len(everyone))
    home = core == x_lo
    guest = jnp.logical_not(home)

    def keep(src, dst):
        return pltpu.make_async_copy(src, dst, R.local.at[local_slots.take()])

    def start_all(copies):
        for copy in copies:
            copy.start()

    def wait_all(copies):
        for copy in copies:
            copy.wait()

    slab_weights = [
        (R.wq, (R.aq, R.hq), 0),
        (R.wk, (R.ak, R.hk), 1),
        (R.wv, (R.av, R.hv), 1),
        (R.wo, (R.ao, R.ho), None),
    ]
    own_copy, ring, cross, swap, first_swap = {}, {}, {}, {}, {}
    for l in range(LAYERS):
        for a, (src, (here, there), side) in enumerate(slab_weights):
            dst = here if l == 0 else there.at[1]
            if l == 0:
                own_copy[a] = keep(src.at[l], dst.at[y, core])
            for k in (1, 2, 3):
                ring[l, a, k] = remote(src.at[l], dst.at[y, core], sems, slots.take(), along_y(k))
            for k in range(4):
                at = dst.at[(y - k + 4) % 4, core]
                to = near[(0, 0, 1, 1)[k] if side is None else 1 if side == 0 and k == 2 else side]
                cross[l, a, k] = remote(src.at[l] if k == 0 else at, at, sems, slots.take(), to)
                slot = slots.take()
                swap[l, a, k] = remote(at, at, sems, slot, sibling)
                if k == 0:
                    first_swap[l, a] = remote(src.at[l], at, sems, slot, sibling)
    QKV, OUT, ALL = (0, 1, 2), (3,), (0, 1, 2, 3)
    PLANES = (((0, 1), (3, 1)), ((0, 2), (3, 2)), ((0, 3), (3, 3)), tuple((a, k) for a in (1, 2) for k in (1, 2, 3)))
    ring_z = {}
    for units in PLANES:
        for a, k in units:
            at = slab_weights[a][1][1].at[1, (y - k + 4) % 4, core]
            for m in (1, 2, 3):
                ring_z[a, k, m] = remote(at, at, sems, slots.take(), along_z(m))

    def by_plane(body):
        for plane in range(4):

            @pl.when(jnp.logical_and(home, z == plane))
            def _():
                body(plane)

    def planes_begin():
        @pl.when(home)
        def _():
            for a in ALL:
                cross[1, a, 0].start()
                first_swap[1, a].start()

        def body(plane):
            for a, k in PLANES[plane]:
                ring[1, a, k].start()

        by_plane(body)

    def planes_z():
        def body(plane):
            for a, k in PLANES[plane]:
                ring[1, a, k].wait_recv()
                for m in (1, 3, 2):
                    ring_z[a, k, m].start()
                cross[1, a, k].start()
                swap[1, a, k].start()

        by_plane(body)

    def planes_pass():
        def body(plane):
            for other in (3, 0, 1, 2):
                if other != plane:
                    for a, k in PLANES[other]:
                        ring_z[a, k, (plane - other) % 4].wait_recv()
                        cross[1, a, k].start()
                        swap[1, a, k].start()

        by_plane(body)

    def planes_sent():
        def body(plane):
            for a, k in PLANES[plane]:
                ring[1, a, k].wait_send()
                for m in (1, 2, 3):
                    ring_z[a, k, m].wait_send()

        by_plane(body)

    def gather_begin(l, arrays):
        @pl.when(home)
        def _():
            for a in arrays:
                for k in ORDER_Y:
                    ring[l, a, k].start()
                cross[l, a, 0].start()
                first_swap[l, a].start()
                if l == 0:
                    own_copy[a].start()

    def gather_home(l, arrays):
        @pl.when(home)
        def _():
            for k in ORDER_Y:
                for a in arrays:
                    ring[l, a, k].wait_recv()
                    cross[l, a, k].start()
                    swap[l, a, k].start()

    def gather_guest(l, arrays):
        @pl.when(guest)
        def _():
            for k in (0,) + ORDER_Y:
                for a in arrays:
                    cross[l, a, k].wait_recv()
                    swap[l, a, k].start()

    def gather_end(l, arrays):
        for a in arrays:
            for k in range(4):
                swap[l, a, k].wait_recv()
        if l == 0:

            @pl.when(home)
            def _():
                for a in arrays:
                    own_copy[a].wait()

    def gather_sent(l, arrays):
        for a in arrays:

            @pl.when(home)
            def _():
                if l == 0:
                    for k in (1, 2, 3):
                        ring[l, a, k].wait_send()
                for k in range(4):
                    cross[l, a, k].wait_send()

            for k in range(4):
                swap[l, a, k].wait_send()

    saves = [keep(here, there.at[0]) for _, (here, there), _ in slab_weights]
    load_back = [keep(there.at[0], here) for _, (here, there), _ in slab_weights]
    load_own, load_core, load_rest = [], [], []
    for src, (here, there), _ in slab_weights:
        slot = local_slots.take()
        at = here.at[y, core]
        load_own.append(pltpu.make_async_copy(src.at[1], at, R.local.at[slot]))
        load_core.append(pltpu.make_async_copy(there.at[1, y, core], at, R.local.at[slot]))
        rest = [keep(there.at[1, y, 1 - core], here.at[y, 1 - core])]
        for k in (1, 2, 3):
            rest.append(keep(there.at[1, (y + k) % 4], here.at[(y + k) % 4]))
        load_rest.append(rest)

    def load_begin(arrays):
        for a in arrays:
            start_all(load_rest[a])

        @pl.when(home)
        def _():
            start_all([load_own[a] for a in arrays])

        @pl.when(guest)
        def _():
            start_all([load_core[a] for a in arrays])

    def load_end(arrays):
        for a in arrays:
            wait_all(load_rest[a])
            load_own[a].wait()

    mlp_in = [R.wg, R.wu, R.wd]
    save_m = keep(R.mw.at[1 - x_lo], R.hm.at[0])
    load_m = [
        [keep(R.hm.at[l], R.mw.at[1 - x_lo])]
        + [keep(mlp_in[a].at[l], R.mw.at[x_lo, a]) for a in range(3)]
        for l in range(LAYERS)
    ]

    own_gain, other_gain = R.all_gains.at[y, x_lo], R.all_gains.at[y, 1 - x_lo]
    gain_keep = keep(R.own_gains, own_gain)
    gain_x = remote(R.own_gains, own_gain, sems, slots.take(), near[0])
    gain_y = [remote(R.own_gains, own_gain, sems, slots.take(), along_y(k)) for k in (1, 2, 3)]
    gain_pass = [remote(other_gain, other_gain, sems, slots.take(), along_y(k)) for k in (1, 2, 3)]

    SIZES = ((0, 48), (48, 32))
    cross_m, ring_m, pass_m, keep_m = {}, {}, {}, {}
    slot_cross = {(l, a): slots.take() for l in range(LAYERS) for a in range(3)}
    slot_ring = {(l, k): slots.take() for l in range(LAYERS) for k in (1, 2, 3)}
    slot_pass = {(l, k): slots.take() for l in range(LAYERS) for k in range(4)}
    for l in range(LAYERS):
        there_m = R.mw.at[x_lo] if l == 0 else R.hm.at[1]
        here_m = R.mw.at[1 - x_lo] if l == 0 else R.hm.at[1]
        if l == 0:
            for a in range(3):
                keep_m[a] = keep(mlp_in[a].at[l], R.mw.at[x_lo, a])
        for c, (first, size) in enumerate(SIZES):

            def rows(where):
                return pl.ds(pl.multiple_of(where * (FFS // 4) + first, 16), size)

            for a in range(3):
                cross_m[l, c, a] = remote(
                    mlp_in[a].at[l, rows(z)], there_m.at[a, rows(z)], sems, slot_cross[l, a], near[c]
                )
            for k in range(4):
                at = here_m.at[:, rows((z - k + 4) % 4)]
                pass_m[l, c, k] = remote(at, at, sems, slot_pass[l, k], sibling)
            for k in (1, 2, 3):
                at = here_m.at[:, rows(z)]
                ring_m[l, c, k] = remote(at, at, sems, slot_ring[l, k], along_z(k))

    def by_core(body):
        for c in range(2):

            @pl.when(core == c)
            def _():
                body(c)

    def pairs_begin(l):
        def body(c):
            for a in range(3):
                cross_m[l, c, a].start()

        by_core(body)
        if l == 0:
            start_all(keep_m.values())

    def pairs_z(l):
        def body(c):
            for a in range(3):
                cross_m[l, c, a].wait_recv()
            for k in ORDER_Y:
                ring_m[l, c, k].start()
            pass_m[l, c, 0].start()

        by_core(body)

    def pairs_pass(l):
        def body(c):
            for k in ORDER_Y:
                ring_m[l, c, k].wait_recv()
                pass_m[l, c, k].start()

        by_core(body)

    def pairs_end(l):
        def body(c):
            for k in range(4):
                pass_m[l, 1 - c, k].wait_recv()

        by_core(body)
        if l == 0:
            wait_all(keep_m.values())

    def pairs_sent(l):
        def body(c):
            for a in range(3):
                cross_m[l, c, a].wait_send()
            for k in (1, 2, 3):
                ring_m[l, c, k].wait_send()
            for k in range(4):
                pass_m[l, c, k].wait_send()

        by_core(body)


    def spread_copy(n, buffer, k):
        return remote(buffer.at[y], buffer.at[y], sems, spread_at[n] + k, along_y(k))

    def spread(n, buffer, targets=ORDER_Y):
        for k in targets:
            spread_copy(n, buffer, k).start()

    def arrived(n, buffer, k):
        there = buffer.at[(y - k + 4) % 4]
        remote(there, there, sems, spread_at[n] + k, along_y(k)).wait_recv()

    def back_copy(n, k):
        return remote(
            R.parts.at[int(n == 1), k - 1], R.came.at[int(n == 1), k - 1], sems, back_at[n] + k, along_y(4 - k)
        )

    def collect(n, total):
        for k in ORDER_Y:
            back_copy(n, k).wait_recv()
            total = total + R.came[int(n == 1), k - 1].astype(F32)
        return total

    def back(n):
        for k in ORDER_Y:
            back_copy(n, k).start()

    def sent(n, buffer):
        for k in (1, 2, 3):
            spread_copy(n, buffer, k).wait_send()

    def sent_back(n):
        for k in (1, 2, 3):
            back_copy(n, k).wait_send()

    reds = {}
    credit_at = {"m": 0, "o": 4}

    def give(kind, which, targets):
        for target in targets:
            pl.semaphore_signal(
                R.credit.at[credit_at[kind] + which], inc=1, device_id=target, device_id_type=MESH
            )

    def take(kind, which, count):
        pl.semaphore_wait(R.credit.at[credit_at[kind] + which], count)

    class Reduction:
        def __init__(self, kind, l):
            self.kind, self.l = kind, l
            shape, self.spread = KINDS[kind]
            self.planes, self.rows = shape[0], shape[1]
            self.b = b = l if kind in TWICE else 0
            self.gives = kind in credit_at and l == 1
            self.takes = kind in credit_at and l == 0
            self.g = R.g_q if kind == "o" else getattr(R, "g_" + kind)
            self.s = getattr(R, "s_" + kind).at[l if kind in SUMS_TWICE else 0]
            self.x = getattr(R, "x_" + kind).at[b]
            self.zb = getattr(R, "z_" + kind).at[b]
            self.p = getattr(R, "p_" + kind).at[b]
            self.h = getattr(R, "h_" + kind).at[b]
            self.f = getattr(R, "f_" + kind).at[l]
            self.chunk = {128: 64, 320: 80}[self.rows]
            n = 4 if self.spread else 1
            self.at_pair = slots.take(n)
            self.at_x = slots.take(4 if self.spread else 2)
            self.at_y = slots.take(4)
            self.at_z = slots.take(4)
            self.at_out = slots.take(4 * self.planes if kind == "m" else 4)
            self.at_far = slots.take()
            self.at_last = slots.take()
            self.own = pltpu.make_async_copy(self.p, self.piece(self.f, z), R.local.at[local_slots.take()])
            if self.spread:
                self.yb = getattr(R, "y_" + kind).at[b]

        def piece(self, ref, where):
            size = self.rows // 4
            return ref.at[:, pl.ds(pl.multiple_of(where * size, 16), size)]

        def add(self, dst, others, chunk=None):
            for i in range(self.planes):
                accumulate(dst.at[i], [o.at[i] for o in others], chunk or self.chunk)

        def pair(self, q):
            if self.spread:
                return remote(self.g.at[q, 1 - core], self.s.at[q], sems, self.at_pair + q, sibling)
            return remote(self.g.at[1 - core], self.s, sems, self.at_pair, sibling)

        def over_x(self, q):
            if self.spread:
                return remote(self.s.at[q], self.x.at[q], sems, self.at_x + q, near[q // 2])
            half = slice(q * (self.rows // 2), (q + 1) * (self.rows // 2))
            return remote(self.s.at[:, half], self.x.at[:, half], sems, self.at_x + q, near[q])

        def came_x(self, q):
            return remote(self.s.at[q], self.x.at[q], sems, self.at_x + q, near[0])

        def over_y(self, k):
            return remote(self.s.at[(y + k) % 4], self.yb.at[k - 1], sems, self.at_y + k, along_y(k))

        def mine(self):
            return self.s.at[y] if self.spread else self.s

        def over_z(self, k):
            return remote(
                self.piece(self.mine(), (z + k) % 4), self.zb.at[k - 1], sems, self.at_z + k, along_z(k)
            )

        def over_far(self):
            return remote(self.p, self.h, sems, self.at_far, far)

        def out_z(self, k):
            return remote(self.p, self.piece(self.f, z), sems, self.at_out + k, along_z(k))

        def out_z_plane(self, k, i):
            src, dst = self.p.at[i], self.piece(self.f, z).at[i]
            return remote(src, dst, sems, self.at_out + 4 * i + k, along_z(k))

        def outs(self, planes=None):
            if self.spread:
                return [self.out_z(k) for k in ORDER_Y]
            return [self.out_z_plane(k, i) for i in planes or range(self.planes) for k in ORDER_Y]

        def last(self):
            return remote(self.f, self.f, sems, self.at_last, sibling)

        def begin(self):
            if self.takes and self.kind == "m":
                take(self.kind, 0, 1)
            for q in (0, 2, 1, 3) if self.spread else (0,):
                self.pair(q).start()

        def step_x(self):
            if self.takes:
                self.when_guest(lambda: take(self.kind, 1, 2))
            for q in (0, 2, 1, 3) if self.spread else (0,):
                self.pair(q).wait()
                if self.spread:
                    self.add(self.s.at[q], [self.g.at[q, core]])
                    self.when_guest(lambda: self.over_x(q).start())
                else:
                    self.add(self.s, [self.g.at[core]])
                    self.when_guest(lambda: [self.over_x(i).start() for i in range(2)])

        def step_y(self):
            @pl.when(home)
            def _():
                if self.spread:
                    if self.takes:
                        take(self.kind, 0, 3)
                    for k in ORDER_Y + (0,):
                        q = (y + k) % 4
                        self.came_x(q).wait_recv()
                        self.add(self.s.at[q], [self.x.at[q]])
                        if k:
                            self.over_y(k).start()
                else:
                    for q in range(2):
                        self.over_x(q).wait_recv()
                    self.add(self.s, [self.x])
                    self.start_z()
                if self.gives:
                    give(self.kind, 1, near)

        def start_z(self):
            if self.takes:
                take(self.kind, 2, 3)
            for k in ORDER_Y:
                self.over_z(k).start()

        def step_z(self):
            if self.spread:

                @pl.when(home)
                def _():
                    for k in ORDER_Y:
                        self.over_y(k).wait_recv()
                    self.add(self.mine(), [self.yb.at[j] for j in range(3)])
                    if self.gives:
                        give(self.kind, 0, [along_y(k) for k in (1, 2, 3)])
                    self.start_z()

        def step_far(self):
            @pl.when(home)
            def _():
                for k in ORDER_Y:
                    self.over_z(k).wait_recv()
                for i in range(self.planes):
                    total = self.piece(self.mine(), z)[i].astype(F32)
                    for j in range(3):
                        total = total + self.zb[j, i].astype(F32)
                    self.p[i] = total.astype(BF)
                if self.takes:
                    take(self.kind, 3, 1)
                self.over_far().start()
                for k in (1, 2, 3):
                    self.over_z(k).wait_send()
                    if self.spread:
                        self.over_y(k).wait_send()
                if self.gives:
                    give(self.kind, 2, [along_z(k) for k in (1, 2, 3)])

            @pl.when(guest)
            def _():
                for q in range(4 if self.spread else 2):
                    self.over_x(q).wait_send()

            if self.gives and self.kind == "m":
                give(self.kind, 0, [sibling])

        def step_out(self, planes=None):
            @pl.when(home)
            def _():
                self.over_far().wait()
                self.add(self.p, [self.h], self.rows // 4)
                self.own.start()
                start_all(self.outs(planes))
                if self.gives:
                    give(self.kind, 3, [far])

        def step_last(self):
            @pl.when(home)
            def _():
                self.own.wait()
                wait_all(self.outs())
                self.last().start()

        def step_out_rest(self, planes):
            @pl.when(home)
            def _():
                start_all(self.outs(planes))

        def finish(self):
            @pl.when(home)
            def _():
                self.last().wait_send()

            @pl.when(guest)
            def _():
                self.last().wait_recv()

        def when_guest(self, body):
            @pl.when(guest)
            def _():
                body()

    first_slots = slots
    for l in (1, 0):
        if l == 0:
            slots = Slots()
            slots.take(kept_slots)
        for kind in KINDS:
            reds[kind, l] = Reduction(kind, l)

    assert max(slots.used, first_slots.used) <= SEMS and local_slots.used <= LOCAL_SEMS

    column = lax.broadcasted_iota(jnp.int32, (ROWS, PAD), 1)
    first_half = column % HEAD < HEAD // 2

    def turn(block, sign):
        ahead = pltpu.roll(block, PAD - HEAD // 2, 1)
        behind = pltpu.roll(block, HEAD // 2, 1)
        return jnp.where(first_half, -sign * ahead, sign * behind)

    def rotated(block):
        return block * R.cosine[...] + turn(block, 1.0) * R.sine[...]

    def rotated_back(block):
        return block * R.cosine[...] + turn(block * R.sine[...], -1.0)

    def inverse_rms(x):
        return lax.rsqrt(jnp.mean(x * x, axis=-1, keepdims=True) + norm_eps)

    def head_lanes(h):
        return slice(h * HEAD, (h + 1) * HEAD)

    def tables():
        one, two = R.lengths[0, 0], R.lengths[0, 1]
        row = lax.broadcasted_iota(jnp.int32, (ROWS, PAD), 0)

        def doc(t):
            return (t >= one).astype(jnp.int32) + (t >= one + two).astype(jnp.int32)

        own = doc(row)
        begins = jnp.where(own == 0, 0, jnp.where(own == 1, one, one + two))
        allowed = jnp.logical_and(own == doc(column), column <= row)
        R.bias[...] = jnp.where(allowed, 0.0, masked_value)
        slow = jnp.exp((column % (HEAD // 2)).astype(F32) * (-2.0 * log_base / HEAD))
        angles = (row - begins).astype(F32) * slow
        R.cosine[...] = jnp.cos(angles)
        R.sine[...] = jnp.sin(angles)
        wide_column = lax.broadcasted_iota(jnp.int32, (D, 8 * PAD), 1)
        wide_row = lax.broadcasted_iota(jnp.int32, (D, 8 * PAD), 0)
        lane = wide_column % PAD
        R.place[...] = jnp.where(
            jnp.logical_and(lane < SHARD, (wide_column // PAD) * SHARD + lane == wide_row), 1.0, 0.0
        ).astype(BF)
        R.wide[...] = jnp.zeros_like(R.wide)
        R.narrow[...] = jnp.zeros_like(R.narrow)
        R.gain_rows[...] = jnp.zeros_like(R.gain_rows)
        R.stream[0] = R.tokens[...].astype(F32).T

    def soft_weights(l, kv):
        rows = jnp.concatenate([R.qrot[l, :, head_lanes(kv * SHARE + i)] for i in range(SHARE)], axis=0)
        keys = R.krot[l, :, head_lanes(kv)]
        scores = dot_t(rows, keys) * score_scale
        scores = scores + jnp.concatenate([R.bias[...]] * SHARE, axis=0)
        weights = jnp.exp(scores - jnp.max(scores, axis=-1, keepdims=True))
        return rows, keys, weights / jnp.sum(weights, axis=-1, keepdims=True)

    def attention_forward(l, ready_qkv, ready_out):
        x = R.stream[l]
        normed = (x * inverse_rms(x) * R.gain_full[l : l + 1, :]).astype(BF)
        R.npad[l] = dot(normed, R.place[...]).astype(BF)

        def project(weights, width, product):
            total = jnp.zeros((ROWS, width), F32)
            for g in range(8):
                total = total + product(
                    R.npad[l, :, g * PAD : g * PAD + SHARD], weights[g // 2, g % 2]
                )
            return total

        ready_qkv()
        R.wide[:, :D] = project(R.aq, D, dot)
        R.narrow[:, :KV] = project(R.ak, KV, dot_t)
        R.vals[l, :, :KV] = project(R.av, KV, dot_t).astype(BF)
        for j in range(8):
            at = slice(j * PAD, (j + 1) * PAD)
            R.qrot[l, :, at] = rotated(R.wide[:, at]).astype(BF)
        for j in range(3):
            at = slice(j * PAD, (j + 1) * PAD)
            R.krot[l, :, at] = rotated(R.narrow[:, at]).astype(BF)
        for kv in range(KV_HEADS):
            rows, keys, soft = soft_weights(l, kv)
            out = dot(soft.astype(BF), R.vals[l, :, head_lanes(kv)]).astype(BF)
            for i in range(SHARE):
                R.gproj_q[:, head_lanes(kv * SHARE + i)] = out[i * ROWS : (i + 1) * ROWS]
        R.mpad[l] = dot(R.gproj_q[:, :D], R.place[...]).astype(BF)
        ready_out()
        total = x
        for g in range(8):
            total = total + dot(R.mpad[l, :, g * PAD : g * PAD + SHARD], R.ao[g // 2, g % 2])
        R.hidden[l] = total
        R.acts_in[l, y] = (total * inverse_rms(total) * R.gain_full[2 + l : 3 + l, :]).astype(BF)

    def blocks(n, buffer, body, between=None):
        def block(i, carry):
            k = order(i)
            b = (y - k + 4) % 4
            if between is not None:
                pl.when(i == 3)(between)

            @pl.when(i > 0)
            def _():
                arrived(n, buffer, k)

            total = body(b)
            if total is None:
                return carry

            @pl.when(i == 0)
            def _():
                R.own_part[...] = total

            @pl.when(i > 0)
            def _():
                R.parts[int(n == 1), k - 1] = total.astype(BF)
                back_copy(n, k).start()

            return carry

        lax.fori_loop(0, 4, block, 0)

    def mlp_forward(l, n, down=True, between=None):
        def body(b):
            rows = R.acts_in[l, b]
            total = jnp.zeros((ROWS, D), F32) if down else None
            for p in range(2):
                gate = dot_t(rows, R.mw[p, 0])
                up = dot_t(rows, R.mw[p, 1])
                act = (gate * jax.nn.sigmoid(gate) * up).astype(BF)
                R.s_gate[l, p, b] = gate.astype(BF)
                R.s_up[l, p, b] = up.astype(BF)
                R.s_act[l, p, b] = act
                if down:
                    total = total + dot(act, R.mw[p, 2])
            return total

        blocks(n, R.acts_in.at[l], body, between)

    def mlp_down(l, n):
        def block(i, carry):
            k = order(i)
            b = (y - k + 4) % 4
            total = dot(R.s_act[l, 0, b], R.mw[0, 2]) + dot(R.s_act[l, 1, b], R.mw[1, 2])

            @pl.when(i == 0)
            def _():
                R.out_grad[...] = (total + R.hidden[l]).T

            @pl.when(i > 0)
            def _():
                R.parts[int(n == 1), k - 1] = total.astype(BF)

            return carry

        lax.fori_loop(0, 4, block, 0)

    def result_out(n):
        R.out_act[...] = (R.out_grad[...] + collect(n, jnp.zeros((ROWS, D), F32)).T).astype(BF)

    def mlp_backward(l, n):
        def body(b):
            rows = R.grads_in[1 - l, b]
            total = jnp.zeros((ROWS, D), F32)
            for p in range(2):
                grad_active = dot_t(rows, R.mw[p, 2])
                gate = R.s_gate[l, p, b].astype(F32)
                up = R.s_up[l, p, b].astype(F32)
                sig = jax.nn.sigmoid(gate)
                grad_gate = (grad_active * up * sig * (1.0 + gate * (1.0 - sig))).astype(BF)
                grad_up = (grad_active * gate * sig).astype(BF)
                R.s_gate[l, p, b] = grad_gate
                R.s_up[l, p, b] = grad_up
                total = total + dot(grad_gate, R.mw[p, 0]) + dot(grad_up, R.mw[p, 1])
            return total

        blocks(n, R.grads_in.at[1 - l], body)

    def mlp_grads(l):
        def grads(p, carry):
            ins = R.acts_in[l].reshape(4 * ROWS, D)
            R.g_m[p, 0] = t_dot(R.s_gate[l, p].reshape(4 * ROWS, FFS), ins).astype(BF)
            R.g_m[p, 1] = t_dot(R.s_up[l, p].reshape(4 * ROWS, FFS), ins).astype(BF)
            R.g_m[p, 2] = t_dot(
                R.s_act[l, p].reshape(4 * ROWS, FFS), R.grads_in[1 - l].reshape(4 * ROWS, D)
            ).astype(BF)
            return carry

        lax.fori_loop(0, 2, grads, 0)

    def slab_loop(body):
        def run(g, carry):
            body(g, g // 2, g % 2)
            return carry

        lax.fori_loop(0, 8, run, 0)

    def norm_back(x, grad_normed, gain_row):
        r = inverse_rms(x)
        u = grad_normed * gain_row
        back = r * u - x * (r * r * r) * jnp.mean(u * x, axis=-1, keepdims=True)
        return back, jnp.sum(grad_normed * x * r, axis=0, keepdims=True)

    def back_hidden(l, n):
        grad_input = collect(n, R.own_part[...])
        back, grad_gain = norm_back(R.hidden[l], grad_input, R.gain_full[2 + l : 3 + l, :])
        grad_hidden = R.grad[...] + back
        R.grad[...] = grad_hidden
        R.glow[...] = grad_hidden.astype(BF)
        R.gain_rows[1:2, :] = grad_gain

        def back_out(g, h, i):
            R.wide[:, lanes(g, SHARD)] = dot_t(R.glow[...], R.ao[h, i])

        slab_loop(back_out)
        R.gmix[...] = dot_t(R.wide[...].astype(BF), R.place[...]).astype(BF)

    def grads_out(l):
        def body(g, h, i):
            R.g_q[h, i, 0] = t_dot(R.mpad[l, :, lanes(g, PAD)], R.glow[...]).astype(BF)

        slab_loop(body)

    def back_heads(l):
        for kv in range(KV_HEADS):
            rows, keys, soft = soft_weights(l, kv)
            heads = [kv * SHARE + i for i in range(SHARE)]
            gm = jnp.concatenate([R.gmix[:, head_lanes(h)] for h in heads], axis=0)
            grad_probs = dot_t(gm, R.vals[l, :, head_lanes(kv)])
            inner = jnp.sum(soft * grad_probs, axis=-1, keepdims=True)
            grad_scores = (soft * (grad_probs - inner)).astype(BF)
            grad_rows = dot(grad_scores, keys) * score_scale
            for i, h in enumerate(heads):
                R.wide[:, head_lanes(h)] = grad_rows[i * ROWS : (i + 1) * ROWS]
            R.narrow[:, head_lanes(kv)] = t_dot(grad_scores, rows) * score_scale
            R.gproj_v[:, head_lanes(kv)] = t_dot(soft.astype(BF), gm).astype(BF)
        for j in range(8):
            at = slice(j * PAD, (j + 1) * PAD)
            R.gproj_q[:, at] = rotated_back(R.wide[:, at]).astype(BF)
        for j in range(3):
            at = slice(j * PAD, (j + 1) * PAD)
            R.gproj_k[:, at] = rotated_back(R.narrow[:, at]).astype(BF)

    def back_stream(l):
        def back_in(g, h, i):
            R.wide[:, lanes(g, SHARD)] = (
                dot_t(R.gproj_q[:, :D], R.aq[h, i])
                + dot(R.gproj_k[:, :KV], R.ak[h, i])
                + dot(R.gproj_v[:, :KV], R.av[h, i])
            )

        slab_loop(back_in)
        high, low = halves(R.wide[...])
        grad_normed = dot_t(high, R.place[...]) + dot_t(low, R.place[...])
        back, grad_gain = norm_back(R.stream[l], grad_normed, R.gain_full[l : l + 1, :])
        R.grad[...] = R.grad[...] + back
        R.gain_rows[0:1, :] = grad_gain

    def grads_kv(l):
        def body(g, h, i):
            right = R.npad[l, :, lanes(g, PAD)]
            R.g_kv[h, i, 0] = t_dot(R.gproj_k[:, :KV], right).astype(BF)
            R.g_kv[h, i, 1] = t_dot(R.gproj_v[:, :KV], right).astype(BF)

        slab_loop(body)

    def grads_q(l):
        high, low = halves(R.gain_rows[...])
        R.gain_grad[...] = dot(high, R.place[...]) + dot(low, R.place[...])

        def body(g, h, i):
            total = t_dot(R.npad[l, :, lanes(g, PAD)], R.gproj_q[:, :D])
            rows = lax.broadcasted_iota(jnp.int32, (PAD, PAD), 0)
            corner = (
                total[:, :PAD]
                + jnp.where(rows == SHARD, R.gain_grad[0:1, lanes(g, PAD)], 0.0)
                + jnp.where(rows == SHARD + 1, R.gain_grad[1:2, lanes(g, PAD)], 0.0)
            )
            R.g_q[h, i, 0] = total.astype(BF)
            R.g_q[h, i, 0, :, :PAD] = corner.astype(BF)

        slab_loop(body)

    gather_begin(0, QKV)
    R.own_gains[...] = jnp.zeros_like(R.own_gains)
    R.own_gains[0:2, :SHARD] = R.gain_one[...]
    R.own_gains[2:4, :SHARD] = R.gain_two[...]
    gain_keep.start()
    gain_x.start()
    start_all(gain_y)
    pairs_begin(0)
    gather_home(0, QKV)
    gather_begin(0, OUT)
    planes_begin()
    cot = R.cotangent[...].astype(F32).T
    R.grads_in[0, y] = cot.astype(BF)
    R.grad[...] = cot
    tables()
    gain_x.wait()
    start_all(gain_pass)
    gather_guest(0, QKV)
    pairs_z(0)
    gather_home(0, OUT)
    gain_keep.wait()
    wait_all(gain_y)
    wait_all(gain_pass)
    for g in range(8):
        R.gain_pad[:, g * PAD : (g + 1) * PAD] = R.all_gains[g // 2, g % 2]
    R.gain_full[...] = dot_t(R.gain_pad[...], R.place[...])
    gather_guest(0, OUT)
    pairs_begin(1)

    def ready_out():
        gather_end(0, OUT)
        pairs_pass(0)
        planes_z()
        start_all(saves)

    attention_forward(0, lambda: gather_end(0, QKV), ready_out)
    spread(0, R.acts_in.at[0])
    pairs_end(0)
    save_m.start()

    def between():
        planes_pass()
        pairs_z(1)

    mlp_forward(0, 0, between=between)
    gather_guest(1, QKV)
    gather_sent(0, ALL)
    wait_all(saves)
    gather_end(1, QKV)
    load_begin(QKV)
    R.stream[1] = collect(0, R.own_part[...] + R.hidden[0])
    spread(2, R.grads_in.at[0], (1, 3))
    pairs_pass(1)
    pairs_sent(0)
    save_m.wait()
    gather_guest(1, OUT)

    def ready_out_1():
        gather_end(1, OUT)
        load_begin(OUT)
        pairs_end(1)
        start_all(load_m[1])
        load_end(OUT)

    attention_forward(1, lambda: load_end(QKV), ready_out_1)
    spread(1, R.acts_in.at[1])
    spread(2, R.grads_in.at[0], (2,))
    sent(0, R.acts_in.at[0])
    sent_back(0)
    wait_all(load_m[1])
    mlp_forward(1, 1, down=False)

    m1, o1, q1, kv1 = (reds[kind, 1] for kind in ("m", "o", "q", "kv"))
    m0, o0, q0, kv0 = (reds[kind, 0] for kind in ("m", "o", "q", "kv"))
    mlp_backward(1, 2)
    mlp_grads(1)
    gather_sent(1, ALL)
    planes_sent()
    pairs_sent(1)
    m1.begin()
    mlp_down(1, 1)
    start_all(load_m[0])
    back_hidden(1, 2)
    back(1)
    m1.step_x()
    back_heads(1)
    back_stream(1)
    R.grads_in[1, y] = R.grad[...].astype(BF)
    spread(3, R.grads_in.at[1])
    start_all(load_back)
    grads_out(1)
    o1.begin()
    grads_kv(1)
    kv1.begin()
    result_out(1)
    o1.step_x()
    m1.step_y()
    grads_q(1)
    q1.begin()
    sent(1, R.acts_in.at[1])
    sent_back(2)
    wait_all(load_m[0])
    mlp_backward(0, 3)
    kv1.step_x()
    q1.step_x()
    mlp_grads(0)
    m1.step_far()
    m0.begin()
    o1.step_y()
    wait_all(load_back)
    back_hidden(0, 3)
    m0.step_x()
    grads_out(0)
    o0.begin()
    kv1.step_y()
    q1.step_y()
    o1.step_z()
    m1.step_out()
    back_heads(0)
    o0.step_x()
    grads_kv(0)
    kv0.begin()
    kv1.step_z()
    q1.step_z()
    m0.step_y()
    back_stream(0)
    kv0.step_x()
    grads_q(0)
    q0.begin()
    o1.step_far()
    R.out_grad[...] = R.grad[...].T
    o0.step_y()
    q0.step_x()
    m1.step_last()
    m0.step_far()
    kv0.step_y()
    kv1.step_far()
    q1.step_far()
    o1.step_out()
    o0.step_z()
    kv0.step_z()
    q0.step_y()
    kv1.step_out()
    q1.step_out()
    o1.step_last()
    o0.step_far()
    m0.step_out((0,))
    kv0.step_far()
    q0.step_z()
    m0.step_out_rest((1, 2))
    o0.step_out()
    kv0.step_out()
    q0.step_far()
    kv1.step_last()
    q1.step_last()
    q0.step_out()
    o0.step_last()
    kv0.step_last()
    m0.step_last()
    q0.step_last()
    for red in (m1, o1, kv1, q1, m0, kv0, o0, q0):
        red.finish()
    sent(2, R.grads_in.at[0])
    sent(3, R.grads_in.at[1])
    sent_back(1)
    sent_back(3)


def step(*args):
    L = LAYERS

    def out(*shape, dtype=BF):
        return jax.ShapeDtypeStruct(shape, dtype)

    return pl.pallas_call(
        step_kernel,
        out_shape=(
            out(D, ROWS),
            out(D, ROWS, dtype=F32),
            out(L, 3, FFS, D),
            out(L, 1, ROWS, D),
            out(L, 1, ROWS, D),
            out(L, 2, KV, PAD),
            out(L, 4, 2, SHARD, D),
            out(L, 4, 2, KV, SHARD),
            out(L, 4, 2, KV, SHARD),
            out(L, 4, 2, SHARD, D),
            out(L, 3, FFS, D),
        ),
        in_specs=[VMEM] * 2 + [SMEM] + [VMEM] * 2 + [ANY] * 7,
        out_specs=[VMEM] * 2 + [ANY] * 9,
        scratch_shapes=list(scratch_shapes().values()),
        compiler_params=pltpu.CompilerParams(
            collective_id=1, has_side_effects=True, vmem_limit_bytes=63 * 2**20
        ),
    )(*args)


def widen_kernel(
    act, grad, fm, fo, fq, fkv,
    act_out, grad_out, gate, up, down, out, query, key, value, gain_one, gain_two,
    act_v, grad_v, fm_v, fo_v, fq_v, fkv_v, m_w, o_w, q_w, k_w, v_w, came, went,
):
    ins = [pltpu.make_async_copy(fm.at[l], fm_v.at[l], came.at[l]) for l in range(LAYERS)]
    rest = ((fq, fq_v), (fo, fo_v), (fkv, fkv_v), (act, act_v), (grad, grad_v))
    ins += [pltpu.make_async_copy(src, dst, came.at[2 + i]) for i, (src, dst) in enumerate(rest)]
    for copy in ins:
        copy.start()
    outs = []

    def put(src, dst):
        outs.append(pltpu.make_async_copy(src, dst, went.at[len(outs)]))
        outs[-1].start()

    for l in range(LAYERS):
        ins[l].wait()
        for a, dst in enumerate((gate, up, down)):
            m_w[l, a] = fm_v[l, a].astype(F32)
            put(m_w.at[l, a], dst.at[l])
    for copy in ins[2:]:
        copy.wait()
    put(act_v, act_out)
    put(grad_v, grad_out)
    for l in range(LAYERS):
        wide = fq_v[l, 0].astype(F32)
        q_w[l] = wide[:SHARD]
        gain_one[l : l + 1, :] = wide[SHARD : SHARD + 1, :SHARD]
        gain_two[l : l + 1, :] = wide[SHARD + 1 : SHARD + 2, :SHARD]
    put(q_w, query)
    o_w[...] = fo_v[:, 0, :SHARD].astype(F32)
    put(o_w, out)
    k_w[...] = fkv_v[:, 0, :, :SHARD].astype(F32)
    put(k_w, key)
    v_w[...] = fkv_v[:, 1, :, :SHARD].astype(F32)
    put(v_w, value)
    for copy in outs:
        copy.wait()


def widen(act, grad, fm, fo, fq, fkv):
    L = LAYERS

    def out(*shape):
        return jax.ShapeDtypeStruct(shape, F32)

    ins = (act, grad, fm, fo, fq, fkv)
    wide = ((L, 3, FFS, D), (L, SHARD, D), (L, SHARD, D), (L, KV, SHARD), (L, KV, SHARD))
    return pl.pallas_call(
        widen_kernel,
        out_shape=(
            jax.ShapeDtypeStruct(act.shape, act.dtype), out(*grad.shape),
            out(L, FFS, D), out(L, FFS, D), out(L, FFS, D), out(L, SHARD, D), out(L, SHARD, D),
            out(L, KV, SHARD), out(L, KV, SHARD), out(L, SHARD), out(L, SHARD),
        ),
        in_specs=[ANY] * 6,
        out_specs=[ANY] * 9 + [VMEM] * 2,
        scratch_shapes=[pltpu.VMEM(a.shape, a.dtype) for a in ins]
        + [pltpu.VMEM(shape, F32) for shape in wide]
        + [pltpu.SemaphoreType.DMA((7,)), pltpu.SemaphoreType.DMA((12,))],
        compiler_params=pltpu.CompilerParams(vmem_limit_bytes=63 * 2**20),
    )(*ins)


def shards(
    tokens, cotangent, lengths, gain_attn, w_query, w_key, w_value, w_out, gain_mlp, w_gate, w_up, w_down
):
    def turned(a):
        return jnp.swapaxes(a, -1, -2)

    act, grad, fm, fo, fq, fkv, *_ = step(
        turned(tokens), turned(cotangent), lengths, gain_attn, gain_mlp,
        w_query, turned(w_key), turned(w_value), w_out, turned(w_gate), turned(w_up), w_down,
    )
    act, grad, gate, up, down, out, query, key, value, gain_one, gain_two = widen(
        act, grad, fm, fo, fq, fkv
    )
    return (
        turned(act),
        turned(grad),
        gain_one,
        query,
        turned(key),
        turned(value),
        out,
        gain_two,
        turned(gate),
        turned(up),
        down,
    )


def solution(mesh):
    in_specs = (
        P(("replica", "group"), None),
        P(("replica", "group"), None),
        P(("replica", "group"), None),
        P(None, "group"),
        P(None, "group", None),
        P(None, "group", None),
        P(None, "group", None),
        P(None, "group", None),
        P(None, "group"),
        P(None, None, "group"),
        P(None, None, "group"),
        P(None, "group", None),
    )
    out_specs = (
        P(("replica", "group"), None),
        P(("replica", "group"), None),
        P(None, "group"),
        P(None, "group", None),
        P(None, "group", None),
        P(None, "group", None),
        P(None, "group", None),
        P(None, "group"),
        P(None, None, "group"),
        P(None, None, "group"),
        P(None, "group", None),
    )
    return jax.shard_map(shards, mesh=mesh, in_specs=in_specs, out_specs=out_specs, check_vma=False)
```

```python
import jax
import jax.numpy as jnp
from jax import lax
from jax.experimental import pallas as pl
from jax.experimental.pallas import tpu as pltpu
from jax.sharding import PartitionSpec as P

Q_HEADS = 15
KV_HEADS = 5
HEAD = 64
LAYERS = 2
D = 960
SHARD = 120
PAD = 128
FFS = 320
ROWS = 128
KV = KV_HEADS * HEAD
SHARE = Q_HEADS // KV_HEADS

norm_eps = 1e-05
rope_base = 100000.0
log_base = 11.512925464970229
score_scale = 0.125
masked_value = -1e30
MESH = pl.DeviceIdType.MESH
BF = jnp.bfloat16
F32 = jnp.float32
ANY = pl.BlockSpec(memory_space=pl.ANY)
VMEM = pl.BlockSpec(memory_space=pltpu.VMEM)
SMEM = pl.BlockSpec(memory_space=pltpu.SMEM)


def coords():
    r = lax.axis_index("replica")
    g = lax.axis_index("group")
    return r // 8, (r // 2) % 4, r % 2, g // 2, g % 2


def device(x_hi, z, core, y, x_lo):
    return ((x_hi * 4 + z) * 2 + core, y * 2 + x_lo)


def remote(src, dst, sems, index, target):
    return pltpu.make_async_remote_copy(
        src_ref=src,
        dst_ref=dst,
        send_sem=sems[0].at[index],
        recv_sem=sems[1].at[index],
        device_id=target,
        device_id_type=MESH,
    )


def dot(a, b):
    return lax.dot_general(a, b, (((1,), (0,)), ((), ())), preferred_element_type=F32)


def dot_t(a, b):
    return lax.dot_general(a, b, (((1,), (1,)), ((), ())), preferred_element_type=F32)


def t_dot(a, b):
    return lax.dot_general(a, b, (((0,), (0,)), ((), ())), preferred_element_type=F32)


def lanes(g, width):
    return pl.ds(pl.multiple_of(g * PAD, PAD), width)


def halves(a):
    high = a.astype(BF)
    return high, (a - high.astype(F32)).astype(BF)


def accumulate(dst, others, chunk):
    def body(i, carry):
        at = pl.ds(pl.multiple_of(i * chunk, chunk), chunk)
        total = dst[at, :].astype(F32)
        for other in others:
            total = total + other[at, :].astype(F32)
        dst[at, :] = total.astype(dst.dtype)
        return carry

    lax.fori_loop(0, dst.shape[0] // chunk, body, 0)


class Slots:
    def __init__(self):
        self.used = 0

    def take(self, count=1):
        self.used += count
        return self.used - count


def order(k):
    return k + (k // 2) * (5 - 2 * k)


KINDS = {
    "m": ((3, FFS, D), False),
    "o": ((1, ROWS, D), True),
    "q": ((1, ROWS, D), True),
    "kv": ((2, KV, PAD), True),
}
TWICE = ("q", "kv")
SUMS_TWICE = ("o", "q", "kv")
ORDER_Y = (1, 3, 2)


def quarter(shape):
    return (shape[0], shape[1] // 4, shape[2])


def scratch_shapes():
    L = LAYERS
    named = {}

    def buf(name, *shape, dtype=BF):
        named[name] = pltpu.VMEM(shape, dtype)

    buf("aq", 4, 2, SHARD, D)
    buf("ao", 4, 2, SHARD, D)
    buf("ak", 4, 2, KV, SHARD)
    buf("av", 4, 2, KV, SHARD)
    buf("mw", 2, 3, FFS, D)
    buf("all_gains", 4, 2, 16, PAD)
    buf("own_gains", 16, PAD)
    buf("place", D, 8 * PAD)
    buf("cosine", ROWS, PAD, dtype=F32)
    buf("sine", ROWS, PAD, dtype=F32)
    buf("bias", ROWS, ROWS, dtype=F32)
    buf("gain_full", 16, D, dtype=F32)
    buf("gain_pad", 16, 8 * PAD)
    buf("gain_grad", 16, 8 * PAD, dtype=F32)
    buf("gain_rows", 16, D, dtype=F32)
    buf("stream", L, ROWS, D, dtype=F32)
    buf("hidden", L, ROWS, D, dtype=F32)
    buf("grad", ROWS, D, dtype=F32)
    buf("wide", ROWS, 8 * PAD, dtype=F32)
    buf("narrow", ROWS, 3 * PAD, dtype=F32)
    buf("own_part", ROWS, D, dtype=F32)
    buf("npad", L, ROWS, 8 * PAD)
    buf("mpad", L, ROWS, 8 * PAD)
    buf("qrot", L, ROWS, 8 * PAD)
    buf("krot", L, ROWS, 3 * PAD)
    buf("vals", L, ROWS, 3 * PAD)
    buf("gproj_q", ROWS, 8 * PAD)
    buf("gproj_k", ROWS, 3 * PAD)
    buf("gproj_v", ROWS, 3 * PAD)
    buf("gmix", ROWS, D)
    buf("glow", ROWS, D)
    buf("acts_in", L, 4, ROWS, D)
    buf("grads_in", 2, 4, ROWS, D)
    buf("parts", 2, 3, ROWS, D)
    buf("came", 2, 3, ROWS, D)
    buf("s_gate", L, 2, 4, ROWS, FFS)
    buf("s_up", L, 2, 4, ROWS, FFS)
    buf("s_act", L, 2, 4, ROWS, FFS)
    for kind, (shape, spread) in KINDS.items():
        four = (4,) if spread else ()
        copies = L if kind in TWICE else 1
        if kind != "o":
            buf("g_" + kind, *four, 2, *shape)
        buf("s_" + kind, L if kind in SUMS_TWICE else 1, *four, *shape)
        buf("x_" + kind, copies, *four, *shape)
        if spread:
            buf("y_" + kind, copies, 3, *shape)
        buf("z_" + kind, copies, 3, *quarter(shape))
        buf("p_" + kind, copies, *quarter(shape))
        buf("h_" + kind, copies, *quarter(shape))
    named["send"] = pltpu.SemaphoreType.DMA((SEMS,))
    named["recv"] = pltpu.SemaphoreType.DMA((SEMS,))
    named["local"] = pltpu.SemaphoreType.DMA((LOCAL_SEMS,))
    named["credit"] = pltpu.SemaphoreType.REGULAR((8,))
    return named


SEMS = 274
LOCAL_SEMS = 53
INPUTS = ("tokens", "cotangent", "lengths", "gain_one", "gain_two", "wq", "wk", "wv", "wo", "wg", "wu", "wd")
OUTPUTS = ("out_act", "out_grad", "f_m", "f_o", "f_q", "f_kv", "hq", "hk", "hv", "ho", "hm")


class Refs:
    pass


def step_kernel(*refs):
    R = Refs()
    names = INPUTS + OUTPUTS + tuple(scratch_shapes())
    for name, ref in zip(names, refs, strict=True):
        setattr(R, name, ref)
    x_hi, z, core, y, x_lo = coords()
    sems = (R.send, R.recv)
    slots = Slots()
    local_slots = Slots()
    spread_at = [slots.take(4) for _ in range(4)]
    back_at = [slots.take(4) for _ in range(4)]
    kept_slots = slots.used
    sibling = device(x_hi, z, 1 - core, y, x_lo)
    near = [device(x_hi, z, core, y, 1 - x_lo), device(1 - x_hi, z, core, y, 1 - x_lo)]
    far = device(1 - x_hi, z, core, y, x_lo)

    def along_y(k):
        return device(x_hi, z, core, (y + k) % 4, x_lo)

    def along_z(k):
        return device(x_hi, (z + k) % 4, core, y, x_lo)

    barrier = pltpu.get_barrier_semaphore()
    everyone = [along_y(k) for k in (1, 2, 3)] + [along_z(k) for k in (1, 2, 3)]
    everyone += near + [far, sibling]
    for target in everyone:
        pl.semaphore_signal(barrier, inc=1, device_id=target, device_id_type=MESH)
    pl.semaphore_wait(barrier, len(everyone))
    home = core == x_lo
    guest = jnp.logical_not(home)

    def keep(src, dst):
        return pltpu.make_async_copy(src, dst, R.local.at[local_slots.take()])

    def start_all(copies):
        for copy in copies:
            copy.start()

    def wait_all(copies):
        for copy in copies:
            copy.wait()

    slab_weights = [
        (R.wq, (R.aq, R.hq), 0),
        (R.wk, (R.ak, R.hk), 1),
        (R.wv, (R.av, R.hv), 1),
        (R.wo, (R.ao, R.ho), None),
    ]
    own_copy, ring, cross, swap, first_swap = {}, {}, {}, {}, {}
    for l in range(LAYERS):
        for a, (src, (here, there), side) in enumerate(slab_weights):
            dst = here if l == 0 else there.at[1]
            if l == 0:
                own_copy[a] = keep(src.at[l], dst.at[y, core])
            for k in (1, 2, 3):
                ring[l, a, k] = remote(src.at[l], dst.at[y, core], sems, slots.take(), along_y(k))
            for k in range(4):
                at = dst.at[(y - k + 4) % 4, core]
                to = near[(0, 0, 1, 1)[k] if side is None else 1 if side == 0 and k == 2 else side]
                cross[l, a, k] = remote(src.at[l] if k == 0 else at, at, sems, slots.take(), to)
                slot = slots.take()
                swap[l, a, k] = remote(at, at, sems, slot, sibling)
                if k == 0:
                    first_swap[l, a] = remote(src.at[l], at, sems, slot, sibling)
    QKV, OUT, ALL = (0, 1, 2), (3,), (0, 1, 2, 3)
    PLANES = (((0, 1), (3, 1)), ((0, 2), (3, 2)), ((0, 3), (3, 3)), tuple((a, k) for a in (1, 2) for k in (1, 2, 3)))
    ring_z = {}
    for units in PLANES:
        for a, k in units:
            at = slab_weights[a][1][1].at[1, (y - k + 4) % 4, core]
            for m in (1, 2, 3):
                ring_z[a, k, m] = remote(at, at, sems, slots.take(), along_z(m))

    def by_plane(body):
        for plane in range(4):

            @pl.when(jnp.logical_and(home, z == plane))
            def _():
                body(plane)

    def planes_begin():
        @pl.when(home)
        def _():
            for a in ALL:
                cross[1, a, 0].start()
                first_swap[1, a].start()

        def body(plane):
            for a, k in PLANES[plane]:
                ring[1, a, k].start()

        by_plane(body)

    def planes_z():
        def body(plane):
            for a, k in PLANES[plane]:
                ring[1, a, k].wait_recv()
                for m in (1, 3, 2):
                    ring_z[a, k, m].start()
                cross[1, a, k].start()
                swap[1, a, k].start()

        by_plane(body)

    def planes_pass():
        def body(plane):
            for other in (3, 0, 1, 2):
                if other != plane:
                    for a, k in PLANES[other]:
                        ring_z[a, k, (plane - other) % 4].wait_recv()
                        cross[1, a, k].start()
                        swap[1, a, k].start()

        by_plane(body)

    def planes_sent():
        def body(plane):
            for a, k in PLANES[plane]:
                ring[1, a, k].wait_send()
                for m in (1, 2, 3):
                    ring_z[a, k, m].wait_send()

        by_plane(body)

    def gather_begin(l, arrays):
        @pl.when(home)
        def _():
            for a in arrays:
                for k in ORDER_Y:
                    ring[l, a, k].start()
                cross[l, a, 0].start()
                first_swap[l, a].start()
                if l == 0:
                    own_copy[a].start()

    def gather_home(l, arrays):
        @pl.when(home)
        def _():
            for k in ORDER_Y:
                for a in arrays:
                    ring[l, a, k].wait_recv()
                    cross[l, a, k].start()
                    swap[l, a, k].start()

    def gather_guest(l, arrays):
        @pl.when(guest)
        def _():
            for k in (0,) + ORDER_Y:
                for a in arrays:
                    cross[l, a, k].wait_recv()
                    swap[l, a, k].start()

    def gather_end(l, arrays):
        for a in arrays:
            for k in range(4):
                swap[l, a, k].wait_recv()
        if l == 0:

            @pl.when(home)
            def _():
                for a in arrays:
                    own_copy[a].wait()

    def gather_sent(l, arrays):
        for a in arrays:

            @pl.when(home)
            def _():
                if l == 0:
                    for k in (1, 2, 3):
                        ring[l, a, k].wait_send()
                for k in range(4):
                    cross[l, a, k].wait_send()

            for k in range(4):
                swap[l, a, k].wait_send()

    saves = [keep(here, there.at[0]) for _, (here, there), _ in slab_weights]
    load_back = [keep(there.at[0], here) for _, (here, there), _ in slab_weights]
    load_own, load_core, load_rest = [], [], []
    for src, (here, there), _ in slab_weights:
        slot = local_slots.take()
        at = here.at[y, core]
        load_own.append(pltpu.make_async_copy(src.at[1], at, R.local.at[slot]))
        load_core.append(pltpu.make_async_copy(there.at[1, y, core], at, R.local.at[slot]))
        rest = [keep(there.at[1, y, 1 - core], here.at[y, 1 - core])]
        for k in (1, 2, 3):
            rest.append(keep(there.at[1, (y + k) % 4], here.at[(y + k) % 4]))
        load_rest.append(rest)

    def load_begin(arrays):
        for a in arrays:
            start_all(load_rest[a])

        @pl.when(home)
        def _():
            start_all([load_own[a] for a in arrays])

        @pl.when(guest)
        def _():
            start_all([load_core[a] for a in arrays])

    def load_end(arrays):
        for a in arrays:
            wait_all(load_rest[a])
            load_own[a].wait()

    mlp_in = [R.wg, R.wu, R.wd]
    save_m = keep(R.mw.at[1 - x_lo], R.hm.at[0])
    load_m = [
        [keep(R.hm.at[l], R.mw.at[1 - x_lo])]
        + [keep(mlp_in[a].at[l], R.mw.at[x_lo, a]) for a in range(3)]
        for l in range(LAYERS)
    ]

    own_gain, other_gain = R.all_gains.at[y, x_lo], R.all_gains.at[y, 1 - x_lo]
    gain_keep = keep(R.own_gains, own_gain)
    gain_x = remote(R.own_gains, own_gain, sems, slots.take(), near[0])
    gain_y = [remote(R.own_gains, own_gain, sems, slots.take(), along_y(k)) for k in (1, 2, 3)]
    gain_pass = [remote(other_gain, other_gain, sems, slots.take(), along_y(k)) for k in (1, 2, 3)]

    SIZES = ((0, 48), (48, 32))
    cross_m, ring_m, pass_m, keep_m = {}, {}, {}, {}
    slot_cross = {(l, a): slots.take() for l in range(LAYERS) for a in range(3)}
    slot_ring = {(l, k): slots.take() for l in range(LAYERS) for k in (1, 2, 3)}
    slot_pass = {(l, k): slots.take() for l in range(LAYERS) for k in range(4)}
    for l in range(LAYERS):
        there_m = R.mw.at[x_lo] if l == 0 else R.hm.at[1]
        here_m = R.mw.at[1 - x_lo] if l == 0 else R.hm.at[1]
        if l == 0:
            for a in range(3):
                keep_m[a] = keep(mlp_in[a].at[l], R.mw.at[x_lo, a])
        for c, (first, size) in enumerate(SIZES):

            def rows(where):
                return pl.ds(pl.multiple_of(where * (FFS // 4) + first, 16), size)

            for a in range(3):
                cross_m[l, c, a] = remote(
                    mlp_in[a].at[l, rows(z)], there_m.at[a, rows(z)], sems, slot_cross[l, a], near[c]
                )
            for k in range(4):
                at = here_m.at[:, rows((z - k + 4) % 4)]
                pass_m[l, c, k] = remote(at, at, sems, slot_pass[l, k], sibling)
            for k in (1, 2, 3):
                at = here_m.at[:, rows(z)]
                ring_m[l, c, k] = remote(at, at, sems, slot_ring[l, k], along_z(k))

    def by_core(body):
        for c in range(2):

            @pl.when(core == c)
            def _():
                body(c)

    def pairs_begin(l):
        def body(c):
            for a in range(3):
                cross_m[l, c, a].start()

        by_core(body)
        if l == 0:
            start_all(keep_m.values())

    def pairs_z(l):
        def body(c):
            for a in range(3):
                cross_m[l, c, a].wait_recv()
            for k in ORDER_Y:
                ring_m[l, c, k].start()
            pass_m[l, c, 0].start()

        by_core(body)

    def pairs_pass(l):
        def body(c):
            for k in ORDER_Y:
                ring_m[l, c, k].wait_recv()
                pass_m[l, c, k].start()

        by_core(body)

    def pairs_end(l):
        def body(c):
            for k in range(4):
                pass_m[l, 1 - c, k].wait_recv()

        by_core(body)
        if l == 0:
            wait_all(keep_m.values())

    def pairs_sent(l):
        def body(c):
            for a in range(3):
                cross_m[l, c, a].wait_send()
            for k in (1, 2, 3):
                ring_m[l, c, k].wait_send()
            for k in range(4):
                pass_m[l, c, k].wait_send()

        by_core(body)


    def spread_copy(n, buffer, k):
        return remote(buffer.at[y], buffer.at[y], sems, spread_at[n] + k, along_y(k))

    def spread(n, buffer, targets=ORDER_Y):
        for k in targets:
            spread_copy(n, buffer, k).start()

    def arrived(n, buffer, k):
        there = buffer.at[(y - k + 4) % 4]
        remote(there, there, sems, spread_at[n] + k, along_y(k)).wait_recv()

    def back_copy(n, k):
        return remote(
            R.parts.at[int(n == 1), k - 1], R.came.at[int(n == 1), k - 1], sems, back_at[n] + k, along_y(4 - k)
        )

    def collect(n, total):
        for k in ORDER_Y:
            back_copy(n, k).wait_recv()
            total = total + R.came[int(n == 1), k - 1].astype(F32)
        return total

    def back(n):
        for k in ORDER_Y:
            back_copy(n, k).start()

    def sent(n, buffer):
        for k in (1, 2, 3):
            spread_copy(n, buffer, k).wait_send()

    def sent_back(n):
        for k in (1, 2, 3):
            back_copy(n, k).wait_send()

    reds = {}
    credit_at = {"m": 0, "o": 4}

    def give(kind, which, targets):
        for target in targets:
            pl.semaphore_signal(
                R.credit.at[credit_at[kind] + which], inc=1, device_id=target, device_id_type=MESH
            )

    def take(kind, which, count):
        pl.semaphore_wait(R.credit.at[credit_at[kind] + which], count)

    class Reduction:
        def __init__(self, kind, l):
            self.kind, self.l = kind, l
            shape, self.spread = KINDS[kind]
            self.planes, self.rows = shape[0], shape[1]
            self.b = b = l if kind in TWICE else 0
            self.gives = kind in credit_at and l == 1
            self.takes = kind in credit_at and l == 0
            self.g = R.g_q if kind == "o" else getattr(R, "g_" + kind)
            self.s = getattr(R, "s_" + kind).at[l if kind in SUMS_TWICE else 0]
            self.x = getattr(R, "x_" + kind).at[b]
            self.zb = getattr(R, "z_" + kind).at[b]
            self.p = getattr(R, "p_" + kind).at[b]
            self.h = getattr(R, "h_" + kind).at[b]
            self.f = getattr(R, "f_" + kind).at[l]
            self.chunk = {128: 64, 320: 80}[self.rows]
            n = 4 if self.spread else 1
            self.at_pair = slots.take(n)
            self.at_x = slots.take(4 if self.spread else 2)
            self.at_y = slots.take(4)
            self.at_z = slots.take(4)
            self.at_out = slots.take(4 * self.planes if kind == "m" else 4)
            self.at_far = slots.take()
            self.at_last = slots.take()
            self.own = pltpu.make_async_copy(self.p, self.piece(self.f, z), R.local.at[local_slots.take()])
            if self.spread:
                self.yb = getattr(R, "y_" + kind).at[b]

        def piece(self, ref, where):
            size = self.rows // 4
            return ref.at[:, pl.ds(pl.multiple_of(where * size, 16), size)]

        def add(self, dst, others, chunk=None):
            for i in range(self.planes):
                accumulate(dst.at[i], [o.at[i] for o in others], chunk or self.chunk)

        def pair(self, q):
            if self.spread:
                return remote(self.g.at[q, 1 - core], self.s.at[q], sems, self.at_pair + q, sibling)
            return remote(self.g.at[1 - core], self.s, sems, self.at_pair, sibling)

        def over_x(self, q):
            if self.spread:
                return remote(self.s.at[q], self.x.at[q], sems, self.at_x + q, near[q // 2])
            half = slice(q * (self.rows // 2), (q + 1) * (self.rows // 2))
            return remote(self.s.at[:, half], self.x.at[:, half], sems, self.at_x + q, near[q])

        def came_x(self, q):
            return remote(self.s.at[q], self.x.at[q], sems, self.at_x + q, near[0])

        def over_y(self, k):
            return remote(self.s.at[(y + k) % 4], self.yb.at[k - 1], sems, self.at_y + k, along_y(k))

        def mine(self):
            return self.s.at[y] if self.spread else self.s

        def over_z(self, k):
            return remote(
                self.piece(self.mine(), (z + k) % 4), self.zb.at[k - 1], sems, self.at_z + k, along_z(k)
            )

        def over_far(self):
            return remote(self.p, self.h, sems, self.at_far, far)

        def out_z(self, k):
            return remote(self.p, self.piece(self.f, z), sems, self.at_out + k, along_z(k))

        def out_z_plane(self, k, i):
            src, dst = self.p.at[i], self.piece(self.f, z).at[i]
            return remote(src, dst, sems, self.at_out + 4 * i + k, along_z(k))

        def outs(self, planes=None):
            if self.spread:
                return [self.out_z(k) for k in ORDER_Y]
            return [self.out_z_plane(k, i) for i in planes or range(self.planes) for k in ORDER_Y]

        def last(self):
            return remote(self.f, self.f, sems, self.at_last, sibling)

        def begin(self):
            if self.takes and self.kind == "m":
                take(self.kind, 0, 1)
            for q in (0, 2, 1, 3) if self.spread else (0,):
                self.pair(q).start()

        def step_x(self):
            if self.takes:
                self.when_guest(lambda: take(self.kind, 1, 2))
            for q in (0, 2, 1, 3) if self.spread else (0,):
                self.pair(q).wait()
                if self.spread:
                    self.add(self.s.at[q], [self.g.at[q, core]])
                    self.when_guest(lambda: self.over_x(q).start())
                else:
                    self.add(self.s, [self.g.at[core]])
                    self.when_guest(lambda: [self.over_x(i).start() for i in range(2)])

        def step_y(self):
            @pl.when(home)
            def _():
                if self.spread:
                    if self.takes:
                        take(self.kind, 0, 3)
                    for k in ORDER_Y + (0,):
                        q = (y + k) % 4
                        self.came_x(q).wait_recv()
                        self.add(self.s.at[q], [self.x.at[q]])
                        if k:
                            self.over_y(k).start()
                else:
                    for q in range(2):
                        self.over_x(q).wait_recv()
                    self.add(self.s, [self.x])
                    self.start_z()
                if self.gives:
                    give(self.kind, 1, near)

        def start_z(self):
            if self.takes:
                take(self.kind, 2, 3)
            for k in ORDER_Y:
                self.over_z(k).start()

        def step_z(self):
            if self.spread:

                @pl.when(home)
                def _():
                    for k in ORDER_Y:
                        self.over_y(k).wait_recv()
                    self.add(self.mine(), [self.yb.at[j] for j in range(3)])
                    if self.gives:
                        give(self.kind, 0, [along_y(k) for k in (1, 2, 3)])
                    self.start_z()

        def step_far(self):
            @pl.when(home)
            def _():
                for k in ORDER_Y:
                    self.over_z(k).wait_recv()
                for i in range(self.planes):
                    total = self.piece(self.mine(), z)[i].astype(F32)
                    for j in range(3):
                        total = total + self.zb[j, i].astype(F32)
                    self.p[i] = total.astype(BF)
                if self.takes:
                    take(self.kind, 3, 1)
                self.over_far().start()
                for k in (1, 2, 3):
                    self.over_z(k).wait_send()
                    if self.spread:
                        self.over_y(k).wait_send()
                if self.gives:
                    give(self.kind, 2, [along_z(k) for k in (1, 2, 3)])

            @pl.when(guest)
            def _():
                for q in range(4 if self.spread else 2):
                    self.over_x(q).wait_send()

            if self.gives and self.kind == "m":
                give(self.kind, 0, [sibling])

        def step_out(self, planes=None):
            @pl.when(home)
            def _():
                self.over_far().wait()
                self.add(self.p, [self.h], self.rows // 4)
                self.own.start()
                start_all(self.outs(planes))
                if self.gives:
                    give(self.kind, 3, [far])

        def step_last(self):
            @pl.when(home)
            def _():
                self.own.wait()
                wait_all(self.outs())
                self.last().start()

        def step_out_rest(self, planes):
            @pl.when(home)
            def _():
                start_all(self.outs(planes))

        def finish(self):
            @pl.when(home)
            def _():
                self.last().wait_send()

            @pl.when(guest)
            def _():
                self.last().wait_recv()

        def when_guest(self, body):
            @pl.when(guest)
            def _():
                body()

    first_slots = slots
    for l in (1, 0):
        if l == 0:
            slots = Slots()
            slots.take(kept_slots)
        for kind in KINDS:
            reds[kind, l] = Reduction(kind, l)

    assert max(slots.used, first_slots.used) <= SEMS and local_slots.used <= LOCAL_SEMS

    column = lax.broadcasted_iota(jnp.int32, (ROWS, PAD), 1)
    first_half = column % HEAD < HEAD // 2

    def turn(block, sign):
        ahead = pltpu.roll(block, PAD - HEAD // 2, 1)
        behind = pltpu.roll(block, HEAD // 2, 1)
        return jnp.where(first_half, -sign * ahead, sign * behind)

    def rotated(block):
        return block * R.cosine[...] + turn(block, 1.0) * R.sine[...]

    def rotated_back(block):
        return block * R.cosine[...] + turn(block * R.sine[...], -1.0)

    def inverse_rms(x):
        return lax.rsqrt(jnp.mean(x * x, axis=-1, keepdims=True) + norm_eps)

    def head_lanes(h):
        return slice(h * HEAD, (h + 1) * HEAD)

    def tables():
        one, two = R.lengths[0, 0], R.lengths[0, 1]
        row = lax.broadcasted_iota(jnp.int32, (ROWS, PAD), 0)

        def doc(t):
            return (t >= one).astype(jnp.int32) + (t >= one + two).astype(jnp.int32)

        own = doc(row)
        begins = jnp.where(own == 0, 0, jnp.where(own == 1, one, one + two))
        allowed = jnp.logical_and(own == doc(column), column <= row)
        R.bias[...] = jnp.where(allowed, 0.0, masked_value)
        slow = jnp.exp((column % (HEAD // 2)).astype(F32) * (-2.0 * log_base / HEAD))
        angles = (row - begins).astype(F32) * slow
        R.cosine[...] = jnp.cos(angles)
        R.sine[...] = jnp.sin(angles)
        wide_column = lax.broadcasted_iota(jnp.int32, (D, 8 * PAD), 1)
        wide_row = lax.broadcasted_iota(jnp.int32, (D, 8 * PAD), 0)
        lane = wide_column % PAD
        R.place[...] = jnp.where(
            jnp.logical_and(lane < SHARD, (wide_column // PAD) * SHARD + lane == wide_row), 1.0, 0.0
        ).astype(BF)
        R.wide[...] = jnp.zeros_like(R.wide)
        R.narrow[...] = jnp.zeros_like(R.narrow)
        R.gain_rows[...] = jnp.zeros_like(R.gain_rows)
        R.stream[0] = R.tokens[...].astype(F32).T

    def soft_weights(l, kv):
        rows = jnp.concatenate([R.qrot[l, :, head_lanes(kv * SHARE + i)] for i in range(SHARE)], axis=0)
        keys = R.krot[l, :, head_lanes(kv)]
        scores = dot_t(rows, keys) * score_scale
        scores = scores + jnp.concatenate([R.bias[...]] * SHARE, axis=0)
        weights = jnp.exp(scores - jnp.max(scores, axis=-1, keepdims=True))
        return rows, keys, weights / jnp.sum(weights, axis=-1, keepdims=True)

    def attention_forward(l, ready_qkv, ready_out):
        x = R.stream[l]
        normed = (x * inverse_rms(x) * R.gain_full[l : l + 1, :]).astype(BF)
        R.npad[l] = dot(normed, R.place[...]).astype(BF)

        def project(weights, width, product):
            total = jnp.zeros((ROWS, width), F32)
            for g in range(8):
                total = total + product(
                    R.npad[l, :, g * PAD : g * PAD + SHARD], weights[g // 2, g % 2]
                )
            return total

        ready_qkv()
        R.wide[:, :D] = project(R.aq, D, dot)
        R.narrow[:, :KV] = project(R.ak, KV, dot_t)
        R.vals[l, :, :KV] = project(R.av, KV, dot_t).astype(BF)
        for j in range(8):
            at = slice(j * PAD, (j + 1) * PAD)
            R.qrot[l, :, at] = rotated(R.wide[:, at]).astype(BF)
        for j in range(3):
            at = slice(j * PAD, (j + 1) * PAD)
            R.krot[l, :, at] = rotated(R.narrow[:, at]).astype(BF)
        for kv in range(KV_HEADS):
            rows, keys, soft = soft_weights(l, kv)
            out = dot(soft.astype(BF), R.vals[l, :, head_lanes(kv)]).astype(BF)
            for i in range(SHARE):
                R.gproj_q[:, head_lanes(kv * SHARE + i)] = out[i * ROWS : (i + 1) * ROWS]
        R.mpad[l] = dot(R.gproj_q[:, :D], R.place[...]).astype(BF)
        ready_out()
        total = x
        for g in range(8):
            total = total + dot(R.mpad[l, :, g * PAD : g * PAD + SHARD], R.ao[g // 2, g % 2])
        R.hidden[l] = total
        R.acts_in[l, y] = (total * inverse_rms(total) * R.gain_full[2 + l : 3 + l, :]).astype(BF)

    def blocks(n, buffer, body, between=None):
        def block(i, carry):
            k = order(i)
            b = (y - k + 4) % 4
            if between is not None:
                pl.when(i == 3)(between)

            @pl.when(i > 0)
            def _():
                arrived(n, buffer, k)

            total = body(b)
            if total is None:
                return carry

            @pl.when(i == 0)
            def _():
                R.own_part[...] = total

            @pl.when(i > 0)
            def _():
                R.parts[int(n == 1), k - 1] = total.astype(BF)
                back_copy(n, k).start()

            return carry

        lax.fori_loop(0, 4, block, 0)

    def mlp_forward(l, n, down=True, between=None):
        def body(b):
            rows = R.acts_in[l, b]
            total = jnp.zeros((ROWS, D), F32) if down else None
            for p in range(2):
                gate = dot_t(rows, R.mw[p, 0])
                up = dot_t(rows, R.mw[p, 1])
                act = (gate * jax.nn.sigmoid(gate) * up).astype(BF)
                R.s_gate[l, p, b] = gate.astype(BF)
                R.s_up[l, p, b] = up.astype(BF)
                R.s_act[l, p, b] = act
                if down:
                    total = total + dot(act, R.mw[p, 2])
            return total

        blocks(n, R.acts_in.at[l], body, between)

    def mlp_down(l, n):
        def block(i, carry):
            k = order(i)
            b = (y - k + 4) % 4
            total = dot(R.s_act[l, 0, b], R.mw[0, 2]) + dot(R.s_act[l, 1, b], R.mw[1, 2])

            @pl.when(i == 0)
            def _():
                R.out_grad[...] = (total + R.hidden[l]).T

            @pl.when(i > 0)
            def _():
                R.parts[int(n == 1), k - 1] = total.astype(BF)

            return carry

        lax.fori_loop(0, 4, block, 0)

    def result_out(n):
        R.out_act[...] = (R.out_grad[...] + collect(n, jnp.zeros((ROWS, D), F32)).T).astype(BF)

    def mlp_backward(l, n):
        def body(b):
            rows = R.grads_in[1 - l, b]
            total = jnp.zeros((ROWS, D), F32)
            for p in range(2):
                grad_active = dot_t(rows, R.mw[p, 2])
                gate = R.s_gate[l, p, b].astype(F32)
                up = R.s_up[l, p, b].astype(F32)
                sig = jax.nn.sigmoid(gate)
                grad_gate = (grad_active * up * sig * (1.0 + gate * (1.0 - sig))).astype(BF)
                grad_up = (grad_active * gate * sig).astype(BF)
                R.s_gate[l, p, b] = grad_gate
                R.s_up[l, p, b] = grad_up
                total = total + dot(grad_gate, R.mw[p, 0]) + dot(grad_up, R.mw[p, 1])
            return total

        blocks(n, R.grads_in.at[1 - l], body)

    def mlp_grads(l):
        def grads(p, carry):
            ins = R.acts_in[l].reshape(4 * ROWS, D)
            R.g_m[p, 0] = t_dot(R.s_gate[l, p].reshape(4 * ROWS, FFS), ins).astype(BF)
            R.g_m[p, 1] = t_dot(R.s_up[l, p].reshape(4 * ROWS, FFS), ins).astype(BF)
            R.g_m[p, 2] = t_dot(
                R.s_act[l, p].reshape(4 * ROWS, FFS), R.grads_in[1 - l].reshape(4 * ROWS, D)
            ).astype(BF)
            return carry

        lax.fori_loop(0, 2, grads, 0)

    def slab_loop(body):
        def run(g, carry):
            body(g, g // 2, g % 2)
            return carry

        lax.fori_loop(0, 8, run, 0)

    def norm_back(x, grad_normed, gain_row):
        r = inverse_rms(x)
        u = grad_normed * gain_row
        back = r * u - x * (r * r * r) * jnp.mean(u * x, axis=-1, keepdims=True)
        return back, jnp.sum(grad_normed * x * r, axis=0, keepdims=True)

    def back_hidden(l, n):
        grad_input = collect(n, R.own_part[...])
        back, grad_gain = norm_back(R.hidden[l], grad_input, R.gain_full[2 + l : 3 + l, :])
        grad_hidden = R.grad[...] + back
        R.grad[...] = grad_hidden
        R.glow[...] = grad_hidden.astype(BF)
        R.gain_rows[1:2, :] = grad_gain

        def back_out(g, h, i):
            R.wide[:, lanes(g, SHARD)] = dot_t(R.glow[...], R.ao[h, i])

        slab_loop(back_out)
        R.gmix[...] = dot_t(R.wide[...].astype(BF), R.place[...]).astype(BF)

    def grads_out(l):
        def body(g, h, i):
            R.g_q[h, i, 0] = t_dot(R.mpad[l, :, lanes(g, PAD)], R.glow[...]).astype(BF)

        slab_loop(body)

    def back_heads(l):
        for kv in range(KV_HEADS):
            rows, keys, soft = soft_weights(l, kv)
            heads = [kv * SHARE + i for i in range(SHARE)]
            gm = jnp.concatenate([R.gmix[:, head_lanes(h)] for h in heads], axis=0)
            grad_probs = dot_t(gm, R.vals[l, :, head_lanes(kv)])
            inner = jnp.sum(soft * grad_probs, axis=-1, keepdims=True)
            grad_scores = (soft * (grad_probs - inner)).astype(BF)
            grad_rows = dot(grad_scores, keys) * score_scale
            for i, h in enumerate(heads):
                R.wide[:, head_lanes(h)] = grad_rows[i * ROWS : (i + 1) * ROWS]
            R.narrow[:, head_lanes(kv)] = t_dot(grad_scores, rows) * score_scale
            R.gproj_v[:, head_lanes(kv)] = t_dot(soft.astype(BF), gm).astype(BF)
        for j in range(8):
            at = slice(j * PAD, (j + 1) * PAD)
            R.gproj_q[:, at] = rotated_back(R.wide[:, at]).astype(BF)
        for j in range(3):
            at = slice(j * PAD, (j + 1) * PAD)
            R.gproj_k[:, at] = rotated_back(R.narrow[:, at]).astype(BF)

    def back_stream(l):
        def back_in(g, h, i):
            R.wide[:, lanes(g, SHARD)] = (
                dot_t(R.gproj_q[:, :D], R.aq[h, i])
                + dot(R.gproj_k[:, :KV], R.ak[h, i])
                + dot(R.gproj_v[:, :KV], R.av[h, i])
            )

        slab_loop(back_in)
        high, low = halves(R.wide[...])
        grad_normed = dot_t(high, R.place[...]) + dot_t(low, R.place[...])
        back, grad_gain = norm_back(R.stream[l], grad_normed, R.gain_full[l : l + 1, :])
        R.grad[...] = R.grad[...] + back
        R.gain_rows[0:1, :] = grad_gain

    def grads_kv(l):
        def body(g, h, i):
            right = R.npad[l, :, lanes(g, PAD)]
            R.g_kv[h, i, 0] = t_dot(R.gproj_k[:, :KV], right).astype(BF)
            R.g_kv[h, i, 1] = t_dot(R.gproj_v[:, :KV], right).astype(BF)

        slab_loop(body)

    def grads_q(l):
        high, low = halves(R.gain_rows[...])
        R.gain_grad[...] = dot(high, R.place[...]) + dot(low, R.place[...])

        def body(g, h, i):
            total = t_dot(R.npad[l, :, lanes(g, PAD)], R.gproj_q[:, :D])
            rows = lax.broadcasted_iota(jnp.int32, (PAD, PAD), 0)
            corner = (
                total[:, :PAD]
                + jnp.where(rows == SHARD, R.gain_grad[0:1, lanes(g, PAD)], 0.0)
                + jnp.where(rows == SHARD + 1, R.gain_grad[1:2, lanes(g, PAD)], 0.0)
            )
            R.g_q[h, i, 0] = total.astype(BF)
            R.g_q[h, i, 0, :, :PAD] = corner.astype(BF)

        slab_loop(body)

    gather_begin(0, QKV)
    R.own_gains[...] = jnp.zeros_like(R.own_gains)
    R.own_gains[0:2, :SHARD] = R.gain_one[...]
    R.own_gains[2:4, :SHARD] = R.gain_two[...]
    gain_keep.start()
    gain_x.start()
    start_all(gain_y)
    pairs_begin(0)
    gather_home(0, QKV)
    gather_begin(0, OUT)
    planes_begin()
    cot = R.cotangent[...].astype(F32).T
    R.grads_in[0, y] = cot.astype(BF)
    R.grad[...] = cot
    tables()
    gain_x.wait()
    start_all(gain_pass)
    gather_guest(0, QKV)
    pairs_z(0)
    gather_home(0, OUT)
    gain_keep.wait()
    wait_all(gain_y)
    wait_all(gain_pass)
    for g in range(8):
        R.gain_pad[:, g * PAD : (g + 1) * PAD] = R.all_gains[g // 2, g % 2]
    R.gain_full[...] = dot_t(R.gain_pad[...], R.place[...])
    gather_guest(0, OUT)
    pairs_begin(1)

    def ready_out():
        gather_end(0, OUT)
        pairs_pass(0)
        planes_z()
        start_all(saves)

    attention_forward(0, lambda: gather_end(0, QKV), ready_out)
    spread(0, R.acts_in.at[0])
    pairs_end(0)
    save_m.start()

    def between():
        planes_pass()
        pairs_z(1)

    mlp_forward(0, 0, between=between)
    gather_guest(1, QKV)
    gather_sent(0, ALL)
    wait_all(saves)
    gather_end(1, QKV)
    load_begin(QKV)
    R.stream[1] = collect(0, R.own_part[...] + R.hidden[0])
    spread(2, R.grads_in.at[0], (1, 3))
    pairs_pass(1)
    pairs_sent(0)
    save_m.wait()
    gather_guest(1, OUT)

    def ready_out_1():
        gather_end(1, OUT)
        load_begin(OUT)
        pairs_end(1)
        start_all(load_m[1])
        load_end(OUT)

    attention_forward(1, lambda: load_end(QKV), ready_out_1)
    spread(1, R.acts_in.at[1])
    spread(2, R.grads_in.at[0], (2,))
    sent(0, R.acts_in.at[0])
    sent_back(0)
    wait_all(load_m[1])
    mlp_forward(1, 1, down=False)

    m1, o1, q1, kv1 = (reds[kind, 1] for kind in ("m", "o", "q", "kv"))
    m0, o0, q0, kv0 = (reds[kind, 0] for kind in ("m", "o", "q", "kv"))
    mlp_backward(1, 2)
    mlp_grads(1)
    gather_sent(1, ALL)
    planes_sent()
    pairs_sent(1)
    m1.begin()
    mlp_down(1, 1)
    start_all(load_m[0])
    back_hidden(1, 2)
    back(1)
    m1.step_x()
    back_heads(1)
    back_stream(1)
    R.grads_in[1, y] = R.grad[...].astype(BF)
    spread(3, R.grads_in.at[1])
    start_all(load_back)
    grads_out(1)
    o1.begin()
    grads_kv(1)
    kv1.begin()
    result_out(1)
    o1.step_x()
    m1.step_y()
    grads_q(1)
    q1.begin()
    sent(1, R.acts_in.at[1])
    sent_back(2)
    wait_all(load_m[0])
    mlp_backward(0, 3)
    kv1.step_x()
    q1.step_x()
    mlp_grads(0)
    m1.step_far()
    m0.begin()
    o1.step_y()
    wait_all(load_back)
    back_hidden(0, 3)
    m0.step_x()
    grads_out(0)
    o0.begin()
    kv1.step_y()
    q1.step_y()
    o1.step_z()
    m1.step_out()
    back_heads(0)
    o0.step_x()
    grads_kv(0)
    kv0.begin()
    m0.step_y()
    back_stream(0)
    kv0.step_x()
    grads_q(0)
    q0.begin()
    o1.step_far()
    R.out_grad[...] = R.grad[...].T
    o0.step_y()
    q0.step_x()
    kv0.step_y()
    kv1.step_z()
    q1.step_z()
    m1.step_last()
    o1.step_out()
    m0.step_far()
    o0.step_z()
    q0.step_y()
    kv0.step_z()
    kv1.step_far()
    q1.step_far()
    o1.step_last()
    o0.step_far()
    m0.step_out((0,))
    kv0.step_far()
    q0.step_z()
    m0.step_out_rest((1, 2))
    kv1.step_out()
    q1.step_out()
    o0.step_out()
    kv0.step_out()
    q0.step_far()
    q0.step_out()
    kv1.step_last()
    q1.step_last()
    o0.step_last()
    kv0.step_last()
    m0.step_last()
    q0.step_last()
    for red in (m1, o1, kv1, q1, m0, kv0, o0, q0):
        red.finish()
    sent(2, R.grads_in.at[0])
    sent(3, R.grads_in.at[1])
    sent_back(1)
    sent_back(3)


def step(*args):
    L = LAYERS

    def out(*shape, dtype=BF):
        return jax.ShapeDtypeStruct(shape, dtype)

    return pl.pallas_call(
        step_kernel,
        out_shape=(
            out(D, ROWS),
            out(D, ROWS, dtype=F32),
            out(L, 3, FFS, D),
            out(L, 1, ROWS, D),
            out(L, 1, ROWS, D),
            out(L, 2, KV, PAD),
            out(L, 4, 2, SHARD, D),
            out(L, 4, 2, KV, SHARD),
            out(L, 4, 2, KV, SHARD),
            out(L, 4, 2, SHARD, D),
            out(L, 3, FFS, D),
        ),
        in_specs=[VMEM] * 2 + [SMEM] + [VMEM] * 2 + [ANY] * 7,
        out_specs=[VMEM] * 2 + [ANY] * 9,
        scratch_shapes=list(scratch_shapes().values()),
        compiler_params=pltpu.CompilerParams(
            collective_id=1, has_side_effects=True, vmem_limit_bytes=63 * 2**20
        ),
    )(*args)


def widen_kernel(
    act, grad, fm, fo, fq, fkv,
    act_out, grad_out, gate, up, down, out, query, key, value, gain_one, gain_two,
    act_v, grad_v, fm_v, fo_v, fq_v, fkv_v, m_w, o_w, q_w, k_w, v_w, came, went,
):
    ins = [pltpu.make_async_copy(fm.at[l], fm_v.at[l], came.at[l]) for l in range(LAYERS)]
    rest = ((fq, fq_v), (fo, fo_v), (fkv, fkv_v), (act, act_v), (grad, grad_v))
    ins += [pltpu.make_async_copy(src, dst, came.at[2 + i]) for i, (src, dst) in enumerate(rest)]
    for copy in ins:
        copy.start()
    outs = []

    def put(src, dst):
        outs.append(pltpu.make_async_copy(src, dst, went.at[len(outs)]))
        outs[-1].start()

    for l in range(LAYERS):
        ins[l].wait()
        for a, dst in enumerate((gate, up, down)):
            m_w[l, a] = fm_v[l, a].astype(F32)
            put(m_w.at[l, a], dst.at[l])
    for copy in ins[2:]:
        copy.wait()
    put(act_v, act_out)
    put(grad_v, grad_out)
    for l in range(LAYERS):
        wide = fq_v[l, 0].astype(F32)
        q_w[l] = wide[:SHARD]
        gain_one[l : l + 1, :] = wide[SHARD : SHARD + 1, :SHARD]
        gain_two[l : l + 1, :] = wide[SHARD + 1 : SHARD + 2, :SHARD]
    put(q_w, query)
    o_w[...] = fo_v[:, 0, :SHARD].astype(F32)
    put(o_w, out)
    k_w[...] = fkv_v[:, 0, :, :SHARD].astype(F32)
    put(k_w, key)
    v_w[...] = fkv_v[:, 1, :, :SHARD].astype(F32)
    put(v_w, value)
    for copy in outs:
        copy.wait()


def widen(act, grad, fm, fo, fq, fkv):
    L = LAYERS

    def out(*shape):
        return jax.ShapeDtypeStruct(shape, F32)

    ins = (act, grad, fm, fo, fq, fkv)
    wide = ((L, 3, FFS, D), (L, SHARD, D), (L, SHARD, D), (L, KV, SHARD), (L, KV, SHARD))
    return pl.pallas_call(
        widen_kernel,
        out_shape=(
            jax.ShapeDtypeStruct(act.shape, act.dtype), out(*grad.shape),
            out(L, FFS, D), out(L, FFS, D), out(L, FFS, D), out(L, SHARD, D), out(L, SHARD, D),
            out(L, KV, SHARD), out(L, KV, SHARD), out(L, SHARD), out(L, SHARD),
        ),
        in_specs=[ANY] * 6,
        out_specs=[ANY] * 9 + [VMEM] * 2,
        scratch_shapes=[pltpu.VMEM(a.shape, a.dtype) for a in ins]
        + [pltpu.VMEM(shape, F32) for shape in wide]
        + [pltpu.SemaphoreType.DMA((7,)), pltpu.SemaphoreType.DMA((12,))],
        compiler_params=pltpu.CompilerParams(vmem_limit_bytes=63 * 2**20),
    )(*ins)


def shards(
    tokens, cotangent, lengths, gain_attn, w_query, w_key, w_value, w_out, gain_mlp, w_gate, w_up, w_down
):
    def turned(a):
        return jnp.swapaxes(a, -1, -2)

    act, grad, fm, fo, fq, fkv, *_ = step(
        turned(tokens), turned(cotangent), lengths, gain_attn, gain_mlp,
        w_query, turned(w_key), turned(w_value), w_out, turned(w_gate), turned(w_up), w_down,
    )
    act, grad, gate, up, down, out, query, key, value, gain_one, gain_two = widen(
        act, grad, fm, fo, fq, fkv
    )
    return (
        turned(act),
        turned(grad),
        gain_one,
        query,
        turned(key),
        turned(value),
        out,
        gain_two,
        turned(gate),
        turned(up),
        down,
    )


def solution(mesh):
    in_specs = (
        P(("replica", "group"), None),
        P(("replica", "group"), None),
        P(("replica", "group"), None),
        P(None, "group"),
        P(None, "group", None),
        P(None, "group", None),
        P(None, "group", None),
        P(None, "group", None),
        P(None, "group"),
        P(None, None, "group"),
        P(None, None, "group"),
        P(None, "group", None),
    )
    out_specs = (
        P(("replica", "group"), None),
        P(("replica", "group"), None),
        P(None, "group"),
        P(None, "group", None),
        P(None, "group", None),
        P(None, "group", None),
        P(None, "group", None),
        P(None, "group"),
        P(None, None, "group"),
        P(None, None, "group"),
        P(None, "group", None),
    )
    return jax.shard_map(shards, mesh=mesh, in_specs=in_specs, out_specs=out_specs, check_vma=False)
```
